32 devices in a mesh: wide: 8 (over z, x), narrow: 4 (over y, core).
Axes of the slice: x: 2, y: 2, z: 4, core: 2. Of those that a mesh axis runs over, the one named last changes fastest.
Arguments:
- tokens: bfloat16 [25216, 768], P(('wide', 'narrow')), may hold values from -6 to 6
- patch_mask: int32 [25216], P(('wide', 'narrow')), may hold values from 0 to 1, as said below
- cotangent: bfloat16 [25216, 768], P(('wide', 'narrow')), may hold values from -6 to 6
- mask_token: bfloat16 [768], replicated, may hold values from -6 to 6
- first_gain: bfloat16 [768], replicated, may hold values from 0.5 to 1.5
- first_bias: bfloat16 [768], replicated, may hold values from -2 to 2
- qkv_weight: bfloat16 [768, 3, 768], P(None, None, 'narrow'), may hold values from -0.3125 to 0.3125
- query_bias: bfloat16 [768], P('narrow'), may hold values from -2 to 2
- value_bias: bfloat16 [768], P('narrow'), may hold values from -2 to 2
- position_bias: bfloat16 [12, 197, 197], P('narrow'), may hold values from -3 to 3
- output_weight: bfloat16 [768, 768], P('narrow'), may hold values from -0.875 to 0.875
- output_bias: bfloat16 [768], replicated, may hold values from -2 to 2
- attention_scale: bfloat16 [768], replicated, may hold values from 0.5 to 1.5
- second_gain: bfloat16 [768], replicated, may hold values from 0.5 to 1.5
- second_bias: bfloat16 [768], replicated, may hold values from -2 to 2
- up_weight: bfloat16 [768, 3072], P(None, 'narrow'), may hold values from -0.21875 to 0.21875
- up_bias: bfloat16 [3072], P('narrow'), may hold values from -2 to 2
- down_weight: bfloat16 [3072, 768], P('narrow'), may hold values from -0.109375 to 0.109375
- down_bias: bfloat16 [768], replicated, may hold values from -2 to 2
- feedforward_scale: bfloat16 [768], replicated, may hold values from 0.5 to 1.5
Outputs:
- layer_out: bfloat16 [25216, 768], P(('wide', 'narrow'))
- input_grad: float32 [25216, 768], P(('wide', 'narrow'))
- mask_token_grad: float32 [768], replicated
- first_gain_grad: float32 [768], replicated
- first_bias_grad: float32 [768], replicated
- qkv_weight_grad: float32 [768, 3, 768], P(None, None, 'narrow')
- query_bias_grad: float32 [768], P('narrow')
- value_bias_grad: float32 [768], P('narrow')
- position_bias_grad: float32 [12, 197, 197], P('narrow')
- output_weight_grad: float32 [768, 768], P('narrow')
- output_bias_grad: float32 [768], replicated
- attention_scale_grad: float32 [768], replicated
- second_gain_grad: float32 [768], replicated
- second_bias_grad: float32 [768], replicated
- up_weight_grad: float32 [768, 3072], P(None, 'narrow')
- up_bias_grad: float32 [3072], P('narrow')
- down_weight_grad: float32 [3072, 768], P('narrow')
- down_bias_grad: float32 [768], replicated
- feedforward_scale_grad: float32 [768], replicated
The draws below stay inside these ranges and needn't reach their ends.
Inputs may be any that keep to these rules, and one draw needn't show every extreme that they name: `patch_mask`: the first row of each image (its class token) is 0; each image has 79 to 156 of its other 196 rows at 1.
All inputs are finite; a program needn't handle non-finite values.
Results may differ from the reference program's by a relative error of at most 0.019.
The reference program's roundings to bfloat16 on the way count: a program that leaves them out, or rounds other values in their place, can miss the bound.
Values may be sent and summed in bfloat16 or wider, within the bound.
No kernel may reach another device: no remote copies, remote signals or barrier semaphores. Data moves between devices by JAX's collectives and lax.ppermute only.
A program may use at most 192 MiB of HBM per device.

```python
import jax
import jax.numpy as jnp
from jax import lax

D = 768
HEADS = 12
HEAD_DIM = 64
FF = 3072
LEN = 197
IMG_GRP = 16
IMAGES = 128
ROWS = 25216


def draw_patch_mask(key, part):
    image_keys = jax.random.split(key, IMAGES)
    counts = jax.random.randint(jax.random.fold_in(key, 7), (IMAGES, 1), 79, 157)
    ranking = jax.vmap(lambda single: jax.random.permutation(single, LEN - 1))(image_keys)
    chosen = (ranking < counts).astype(jnp.int32)
    leading = jnp.zeros((IMAGES, 1), jnp.int32)
    return jnp.concatenate([leading, chosen], axis=1).reshape(IMAGES * LEN)


def level_of(stream_key, extent, pieces, smallest, high):
    factor_of = 1.0
    for axis_at, parts in pieces:
        draws = jax.random.uniform(jax.random.fold_in(jax.random.fold_in(stream_key, 6), axis_at), (parts,), jnp.float32, smallest / len(pieces), high / len(pieces))
        factor_of = factor_of * jnp.repeat(jnp.exp(draws), extent[axis_at] // parts).reshape((-1,) + (1,) * (len(extent) - 1 - axis_at))
    return factor_of


def scatter_about(own_key, dims, width, reach, cuts=(), kind=jnp.bfloat16):
    drawn = jax.random.normal(own_key, dims, jnp.float32) * width
    if len(cuts) > 0:
        drawn = level_of(own_key, dims, cuts, -0.22, 0.18) * drawn
    return jnp.clip(drawn, min=-reach, max=reach).astype(kind)


def setup_inputs(seed: int = 0) -> dict:
    keys = jax.random.split(jax.random.key(seed), 21)
    tokens = scatter_about(keys[0], (ROWS, D), 1.0, 6.0, ((0, 32),))
    patch_mask = draw_patch_mask(jax.random.fold_in(keys[20], 71), 0)
    cotangent = scatter_about(keys[2], (ROWS, D), 1.0, 6.0, ((0, 32),))
    mask_token = scatter_about(keys[3], (D,), 1.0, 6.0)
    first_gain = jnp.clip(1.0 + 0.1 * jax.random.normal(keys[4], (D,), jnp.float32), 0.5, 1.5).astype(jnp.bfloat16)
    first_bias = scatter_about(keys[5], (D,), 0.3, 2.0)
    qkv_weight = scatter_about(keys[6], (D, 3, D), (D // 2) ** -0.5, 0.3125, ((2, 4),))
    query_bias = scatter_about(keys[7], (D,), 0.3, 2.0, ((0, 4),))
    value_bias = scatter_about(keys[8], (D,), 0.3, 2.0, ((0, 4),))
    position_bias = scatter_about(keys[9], (HEADS, LEN, LEN), 0.5, 3.0, ((0, 4),))
    output_weight = scatter_about(keys[10], (D, D), (D // 16) ** -0.5, 0.875, ((0, 4),))
    output_bias = scatter_about(keys[11], (D,), 0.3, 2.0)
    attention_scale = jnp.clip(jax.random.uniform(keys[12], (D,), jnp.float32, 0.5, 1.5), 0.5, 1.5).astype(jnp.bfloat16)
    second_gain = jnp.clip(1.0 + 0.1 * jax.random.normal(keys[13], (D,), jnp.float32), 0.5, 1.5).astype(jnp.bfloat16)
    second_bias = scatter_about(keys[14], (D,), 0.3, 2.0)
    up_weight = scatter_about(keys[15], (D, FF), D ** -0.5, 0.21875, ((1, 4),))
    up_bias = scatter_about(keys[16], (FF,), 0.3, 2.0, ((0, 4),))
    down_weight = scatter_about(keys[17], (FF, D), FF ** -0.5, 0.109375, ((0, 4),))
    down_bias = scatter_about(keys[18], (D,), 0.3, 2.0)
    feedforward_scale = jnp.clip(jax.random.uniform(keys[19], (D,), jnp.float32, 0.5, 1.5), 0.5, 1.5).astype(jnp.bfloat16)
    return dict(tokens=tokens, patch_mask=patch_mask, cotangent=cotangent, mask_token=mask_token, first_gain=first_gain, first_bias=first_bias, qkv_weight=qkv_weight, query_bias=query_bias, value_bias=value_bias, position_bias=position_bias, output_weight=output_weight, output_bias=output_bias, attention_scale=attention_scale, second_gain=second_gain, second_bias=second_bias, up_weight=up_weight, up_bias=up_bias, down_weight=down_weight, down_bias=down_bias, feedforward_scale=feedforward_scale)


EPSILON = 1e-06

@jax.custom_vjp
def low(v):
    return lax.optimization_barrier(v.astype(jnp.bfloat16)).astype(jnp.float32)

@jax.custom_vjp
def low_back(v):
    return v

def low_keep(v):
    return (low(v), None)

def low_pass(kept, grad):
    return (grad,)

def back_keep(v):
    return (v, None)

def back_low(kept, grad):
    return (low(grad),)
low.defvjp(low_keep, low_pass)
low_back.defvjp(back_keep, back_low)

def layer_norm(values, gain, shift):
    average = lax.optimization_barrier(jnp.mean(values, -1, keepdims=True))
    centered = values - average
    variance = lax.optimization_barrier(jnp.mean(centered * centered, -1, keepdims=True))
    return centered * lax.rsqrt(variance + EPSILON) * gain + shift

def matmul(left, right):
    return jnp.dot(left, right, precision=lax.Precision.HIGHEST, preferred_element_type=jnp.float32)

def forward(tokens, selected, mask_token, first_gain, first_bias, qkv_weight, query_bias, value_bias, position_bias, output_weight, output_bias, attention_scale, second_gain, second_bias, up_weight, up_bias, down_weight, down_bias, feedforward_scale):
    started = jnp.where(selected, mask_token[None, :], tokens)
    first_norm = low(layer_norm(started, first_gain, first_bias))
    shifts = jnp.stack([query_bias, jnp.zeros_like(query_bias), value_bias])
    triple = jnp.einsum('rd,dtc->rtc', first_norm, qkv_weight, precision=lax.Precision.HIGHEST) + shifts[None]
    triple = low(low_back(triple))
    image_count = triple.shape[0] // LEN
    split = triple.reshape(image_count, LEN, 3, HEADS, HEAD_DIM)
    scores = jnp.einsum('iqhd,ikhd->ihqk', split[:, :, 0], split[:, :, 1], precision=lax.Precision.HIGHEST)
    scores = low_back(scores * HEAD_DIM ** (-0.5) + position_bias[None])
    weights = low(jax.nn.softmax(scores, axis=-1))
    context = jnp.einsum('ihqk,ikhd->iqhd', weights, split[:, :, 2], precision=lax.Precision.HIGHEST)
    context = low(low_back(context.reshape(image_count * LEN, D)))
    branch = low_back(matmul(context, output_weight) + output_bias)
    middle = started + attention_scale * branch
    second_norm = low(layer_norm(middle, second_gain, second_bias))
    preact = low_back(matmul(second_norm, up_weight) + up_bias)
    activated = low(jax.nn.gelu(preact, approximate=False))
    feed = low_back(matmul(activated, down_weight) + down_bias)
    return middle + feedforward_scale * feed

def reference(tokens, patch_mask, cotangent, mask_token, first_gain, first_bias, qkv_weight, query_bias, value_bias, position_bias, output_weight, output_bias, attention_scale, second_gain, second_bias, up_weight, up_bias, down_weight, down_bias, feedforward_scale):
    params = tuple((p.astype(jnp.float32) for p in (mask_token, first_gain, first_bias, qkv_weight, query_bias, value_bias, position_bias, output_weight, output_bias, attention_scale, second_gain, second_bias, up_weight, up_bias, down_weight, down_bias, feedforward_scale)))
    block_rows = IMG_GRP * LEN
    blocks = tokens.shape[0] // block_rows
    token_blocks = tokens.astype(jnp.float32).reshape(blocks, block_rows, D)
    mask_blocks = patch_mask.reshape(blocks, block_rows)
    grad_blocks = cotangent.astype(jnp.float32).reshape(blocks, block_rows, D)

    def step(totals, block_item):
        token_rows, mask_rows, grad_rows = block_item
        selected = (mask_rows == 1)[:, None]

        def forward_block(inputs, *weights):
            return forward(inputs, selected, *weights)
        result, pullback = jax.vjp(forward_block, token_rows, *params)
        gradients = pullback(grad_rows)
        summed = tuple((t + g for t, g in zip(totals, gradients[1:])))
        return (summed, (result.astype(jnp.bfloat16), gradients[0]))
    initial = tuple((jnp.zeros_like(p) for p in params))
    totals, (results, input_grads) = lax.scan(step, initial, (token_blocks, mask_blocks, grad_blocks))
    return (results.reshape(-1, D), input_grads.reshape(-1, D), totals[0], totals[1], totals[2], totals[3], totals[4], totals[5], totals[6], totals[7], totals[8], totals[9], totals[10], totals[11], totals[12], totals[13], totals[14], totals[15], totals[16])
```

```python
import functools

import jax
import jax.numpy as jnp
from jax import lax
from jax.experimental import pallas as pl
from jax.experimental.pallas import tpu as pltpu
from jax.sharding import PartitionSpec as P

HEAD_DIM = 64
LEN = 197
PAD = 208
KEYS = 256
EPSILON = 1e-06
HALF_ROOT = 0.7071067811865476
DENSITY_FACTOR = 0.3989422804014327
FAR = -1e30
F32 = jnp.float32
BF16 = jnp.bfloat16
MIB = 1024 * 1024

(MASK_TOKEN, FIRST_GAIN, FIRST_BIAS, OUTPUT_BIAS, ATT_SCALE, SECOND_GAIN, SECOND_BIAS, DOWN_BIAS, FEED_SCALE) = range(9)

NT = (((1,), (1,)), ((), ()))
TN = (((0,), (0,)), ((), ()))
NN = (((1,), (0,)), ((), ()))


def mm(left, right, dims=NN):
    return lax.dot_general(left, right, dims, preferred_element_type=F32)


def call(body, out_shape, flops, bytes_accessed, trans=0, vmem=56, **kw):
    return pl.pallas_call(
        body,
        out_shape=out_shape,
        compiler_params=pltpu.CompilerParams(vmem_limit_bytes=vmem * MIB),
        cost_estimate=pl.CostEstimate(
            flops=int(flops), bytes_accessed=int(bytes_accessed), transcendentals=int(trans)
        ),
        **kw,
    )


def sds(shape, dtype):
    return jax.ShapeDtypeStruct(shape, dtype)


def norm_parts(values):
    average = jnp.mean(values, -1, keepdims=True)
    centered = values - average
    inverse_dev = lax.rsqrt(jnp.mean(centered * centered, -1, keepdims=True) + EPSILON)
    return centered * inverse_dev, inverse_dev


def norm_back(grad_rows, normed, inverse_dev, gain):
    scaled = grad_rows * gain
    return inverse_dev * (
        scaled
        - jnp.mean(scaled, -1, keepdims=True)
        - normed * jnp.mean(scaled * normed, -1, keepdims=True)
    )


def colsum(values):
    return jnp.sum(values, 0, keepdims=True)


def prep_body(images, tok, mask, cot, vec, started_o, first_o, g_o, fg_o, sums_o, wide_s, pad_s):
    width = tok.shape[1]
    rows = tok.shape[0]
    picked = mask[...] == 1.0
    for j in range(width // 128):
        lanes = slice(128 * j, 128 * j + 128)
        wide_s[0:rows, lanes] = jnp.where(
            picked, vec[MASK_TOKEN : MASK_TOKEN + 1, lanes], tok[:, lanes].astype(F32)
        )
    for i in range(images):
        pad_s[0:LEN, :] = wide_s[i * LEN : (i + 1) * LEN, :]
        pad_s[LEN:PAD, :] = jnp.zeros((PAD - LEN, width), F32)
        values = pad_s[...]
        normed, _ = norm_parts(values)
        block = slice(i * PAD, (i + 1) * PAD)
        started_o[block, :] = values.astype(BF16)
        first_o[block, :] = (
            normed * vec[FIRST_GAIN : FIRST_GAIN + 1] + vec[FIRST_BIAS : FIRST_BIAS + 1]
        ).astype(BF16)
    wide_s[0:rows, :] = cot[...].astype(F32)
    total = jnp.zeros((1, width), F32)
    for i in range(images):
        pad_s[0:LEN, :] = wide_s[i * LEN : (i + 1) * LEN, :]
        values = pad_s[...]
        block = slice(i * PAD, (i + 1) * PAD)
        g_o[block, :] = values.astype(BF16)
        feed_grad = (values * vec[FEED_SCALE : FEED_SCALE + 1]).astype(BF16)
        fg_o[block, :] = feed_grad
        total += colsum(feed_grad.astype(F32))
    sums_o[0:1, :] = total
    sums_o[1:8, :] = jnp.zeros((7, width), F32)


def prep(tokens, mask_cols, cotangent, vec):
    rows, width = tokens.shape
    images = rows // LEN
    big = images * PAD
    b = sds((big, width), BF16)
    return call(
        functools.partial(prep_body, images),
        (b, b, b, b, sds((8, width), F32)),
        10 * rows * width,
        6 * 2 * rows * width,
        scratch_shapes=[pltpu.VMEM((-(-rows // 8) * 8, width), F32), pltpu.VMEM((PAD, width), F32)],
    )(tokens, mask_cols, cotangent, vec)


def attention_forward_body(images, local, first, pack_a, pack_b, qkv_o, prob_o, ctx_o, w_s, bias_s):
    pair = 2 * local
    heads = local // HEAD_DIM
    width = first.shape[1]
    big = images * PAD
    score_scale = HEAD_DIM ** (-0.5)
    for t in range(3):
        w_s[t, 0:local, :] = pack_a[t * local : (t + 1) * local, :]
        w_s[t, local:pair, :] = pack_b[t * local : (t + 1) * local, :]
    small = 4 * local + PAD
    shift_q = jnp.concatenate(
        [pack_a[small : small + 16, 0:local], pack_b[small : small + 16, 0:local]], 1
    ).astype(F32)
    for h in range(heads):
        bias_s[h] = pack_a[4 * local : 4 * local + PAD, h * KEYS : (h + 1) * KEYS].astype(F32)
        bias_s[heads + h] = pack_b[4 * local : 4 * local + PAD, h * KEYS : (h + 1) * KEYS].astype(F32)
    for t in range(3):
        value = mm(first[...], w_s[t], NT)
        if t == 0:
            value = value + shift_q[1:2]
        if t == 2:
            value = value + shift_q[2:3]
        qkv_o[t, 0:big, :] = value.astype(BF16)
        qkv_o[t, big:, :] = jnp.zeros((KEYS - PAD, pair), BF16)
    lane = lax.broadcasted_iota(jnp.int32, (1, 128), 1)
    first_half = (lane < HEAD_DIM).astype(BF16)
    halves = (first_half, 1 - first_half)

    def image(i, carry):
        row = pl.multiple_of(i * PAD, 16)
        for tile in range(pair // 128):
            lanes = slice(128 * tile, 128 * tile + 128)
            q = qkv_o[0, pl.ds(row, PAD), lanes]
            k = qkv_o[1, pl.ds(row, KEYS), lanes]
            v = qkv_o[2, pl.ds(row, KEYS), lanes]
            context = None
            for half in range(2):
                head = 2 * tile + half
                scores = mm(q * halves[half], k, NT) * score_scale + bias_s[head]
                top = jnp.max(scores, -1, keepdims=True)
                powers = jnp.exp(scores - top)
                share = 1.0 / jnp.sum(powers, -1, keepdims=True)
                probabilities = (powers * share).astype(BF16)
                prob_o[head, pl.ds(row, PAD), :] = probabilities
                part = mm(probabilities, v * halves[half])
                context = part if context is None else context + part
            ctx_o[pl.ds(row, PAD), lanes] = context.astype(BF16)
        return carry

    lax.fori_loop(0, images, image, 0)


def attention_forward(first, pack_a, pack_b, images, local):
    big, width = first.shape
    pair = 2 * local
    heads = pair // HEAD_DIM
    flops = 2 * big * (width * 3 * pair + 2 * KEYS * HEAD_DIM * heads)
    return call(
        functools.partial(attention_forward_body, images, local),
        (
            sds((3, big + KEYS - PAD, pair), BF16),
            sds((heads, big, KEYS), BF16),
            sds((big, pair), BF16),
        ),
        flops * 2,
        2 * big * (width + 4 * pair + heads * KEYS),
        heads * big * KEYS,
        scratch_shapes=[pltpu.VMEM((3, pair, width), BF16), pltpu.VMEM((heads, PAD, KEYS), F32)],
    )(first, pack_a, pack_b)


def middle_body(images, local, ctx_a, ctx_b, p0, p1, p2, p3, started, vec, branch_o, middle_o, second_o, second_t_o, w_s):
    pair = 2 * local
    for at, pack in enumerate((p0, p1, p2, p3)):
        w_s[at * local : (at + 1) * local, :] = pack[3 * local : 4 * local, :]

    def image(i, carry):
        row = pl.multiple_of(i * PAD, 16)
        block = pl.ds(row, PAD)
        branch = (
            mm(ctx_a[block, :], w_s[0:pair, :])
            + mm(ctx_b[block, :], w_s[pair : 2 * pair, :])
            + vec[OUTPUT_BIAS : OUTPUT_BIAS + 1]
        )
        branch_o[block, :] = branch
        middle = started[block, :].astype(F32) + vec[ATT_SCALE : ATT_SCALE + 1] * branch
        middle_o[block, :] = middle
        normed, _ = norm_parts(middle)
        second_o[block, :] = (
            normed * vec[SECOND_GAIN : SECOND_GAIN + 1] + vec[SECOND_BIAS : SECOND_BIAS + 1]
        ).astype(BF16)
        return carry

    lax.fori_loop(0, images, image, 0)
    second_t_o[...] = second_o[...].T


def middle_stage(ctx_a, ctx_b, packs, started, vec, images, local):
    big, width = started.shape
    return call(
        functools.partial(middle_body, images, local),
        (
            sds((big, width), F32),
            sds((big, width), F32),
            sds((big, width), BF16),
            sds((width, big), BF16),
        ),
        2 * big * width * width + 20 * big * width,
        big * width * 16,
        scratch_shapes=[pltpu.VMEM((4 * local, width), BF16)],
    )(ctx_a, ctx_b, *packs, started, vec)


def feed_body(second, second_t, fg, up, down, up_bias, feed_o, sg_o, dup_o, ddown_o, bias_o, feed_s, sg_s):
    step = pl.program_id(0)
    wu = up[...]
    wd = down[...]
    pre = mm(second[...], wu) + up_bias[0:1, :].astype(F32)
    back = mm(fg[...], wd, NT)
    cdf = 0.5 * (1.0 + lax.erf(pre * HALF_ROOT))
    act = (pre * cdf).astype(BF16)
    slope = cdf + pre * (jnp.exp(-0.5 * pre * pre) * DENSITY_FACTOR)
    pg = (back * slope).astype(BF16)
    feed = mm(act, wd)
    sg = mm(pg, wu, NT)

    @pl.when(step == 0)
    def _():
        feed_s[...] = feed
        sg_s[...] = sg

    @pl.when(step > 0)
    def _():
        feed_s[...] += feed
        sg_s[...] += sg

    ddown_o[...] = mm(act, fg[...], TN).astype(BF16)
    dup_o[...] = mm(second_t[...], pg).astype(BF16)
    bias_o[...] = jnp.broadcast_to(colsum(pg.astype(F32)), bias_o.shape)

    @pl.when(step == pl.num_programs(0) - 1)
    def _():
        feed_o[...] = feed_s[...].astype(BF16)
        sg_o[...] = sg_s[...].astype(BF16)


def feed_stage(second, second_t, fg, up, down, up_bias):
    big, width = second.shape
    hidden = up.shape[1]
    block = 256
    whole = lambda shape: pl.BlockSpec(shape, lambda i: (0, 0))
    return call(
        feed_body,
        (
            sds((big, width), BF16),
            sds((big, width), BF16),
            sds((width, hidden), BF16),
            sds((hidden, width), BF16),
            sds((8, hidden), F32),
        ),
        12 * big * width * hidden,
        2 * (5 * big * width + 4 * hidden * width),
        2 * big * hidden,
        grid=(hidden // block,),
        in_specs=[
            whole((big, width)),
            whole((width, big)),
            whole((big, width)),
            pl.BlockSpec((width, block), lambda i: (0, i)),
            pl.BlockSpec((block, width), lambda i: (i, 0)),
            pl.BlockSpec((16, block), lambda i: (0, i)),
        ],
        out_specs=(
            whole((big, width)),
            whole((big, width)),
            pl.BlockSpec((width, block), lambda i: (0, i)),
            pl.BlockSpec((block, width), lambda i: (i, 0)),
            pl.BlockSpec((8, block), lambda i: (0, i)),
        ),
        scratch_shapes=[pltpu.VMEM((big, width), F32), pltpu.VMEM((big, width), F32)],
    )(second, second_t, fg, up, down, up_bias)


def turn_body(images, parts, *refs):
    feeds = refs[0:parts]
    sgs = refs[parts : 2 * parts]
    middle, branch, g, vec, out_o, mg_o, ag_o, sums_o, wide_s = refs[2 * parts :]
    width = middle.shape[1]
    sums_o[...] = jnp.zeros(sums_o.shape, F32)

    for i in range(images):
        block = slice(i * PAD, (i + 1) * PAD)
        feed = vec[DOWN_BIAS : DOWN_BIAS + 1]
        sg = jnp.zeros((PAD, width), F32)
        for at in range(parts):
            feed = feed + feeds[at][block, :].astype(F32)
            sg = sg + sgs[at][block, :].astype(F32)
        rows = g[block, :].astype(F32)
        mid = middle[block, :]
        out = mid + vec[FEED_SCALE : FEED_SCALE + 1] * feed
        wide_s[i * LEN : (i + 1) * LEN, :] = out[0:LEN]
        normed, inverse = norm_parts(mid)
        grad = rows + norm_back(sg, normed, inverse, vec[SECOND_GAIN : SECOND_GAIN + 1])
        mg_o[block, :] = grad
        att = (vec[ATT_SCALE : ATT_SCALE + 1] * grad).astype(BF16)
        ag_o[block, :] = att
        sums_o[0:1, :] += colsum(rows * feed)
        sums_o[1:2, :] += colsum(sg * normed)
        sums_o[2:3, :] += colsum(sg)
        sums_o[3:4, :] += colsum(grad * branch[block, :])
        sums_o[4:5, :] += colsum(att.astype(F32))
    out_o[...] = wide_s[0 : out_o.shape[0], :].astype(BF16)


def turn_stage(feeds, sgs, middle, branch, g, vec, images):
    big, width = middle.shape
    rows = images * LEN
    return call(
        functools.partial(turn_body, images, len(feeds)),
        (sds((rows, width), BF16), sds((big, width), F32), sds((big, width), BF16), sds((8, width), F32)),
        40 * big * width,
        big * width * (18 + 4 * len(feeds)),
        scratch_shapes=[pltpu.VMEM((-(-rows // 8) * 8, width), F32)],
    )(*feeds, *sgs, middle, branch, g, vec)


def attention_backward_body(
    images, local, first, ag, ctx, qkv, prob, pack_a, pack_b, up_a, up_b,
    grad_a, grad_b, fg_o, w_s, cg_s, tg_s, bias_s, wo_s,
):
    pair = 2 * local
    heads = local // HEAD_DIM
    big, width = first.shape
    score_scale = HEAD_DIM ** (-0.5)
    for t in range(3):
        w_s[t * pair : t * pair + local, :] = pack_a[t * local : (t + 1) * local, :]
        w_s[t * pair + local : (t + 1) * pair, :] = pack_b[t * local : (t + 1) * local, :]
    wo_s[0:local, :] = pack_a[3 * local : 4 * local, :]
    wo_s[local:pair, :] = pack_b[3 * local : 4 * local, :]
    cg_s[0:big, :] = mm(ag[...], wo_s[...], NT).astype(BF16)
    d_out = mm(ctx[...], ag[...], TN).astype(BF16)
    grad_a[3 * local : 4 * local, :] = d_out[0:local]
    grad_b[3 * local : 4 * local, :] = d_out[local:pair]
    bias_s[...] = jnp.zeros(bias_s.shape, F32)
    lane = lax.broadcasted_iota(jnp.int32, (1, 128), 1)
    first_half = (lane < HEAD_DIM).astype(BF16)
    halves = (first_half, 1 - first_half)

    def image(i, carry):
        row = pl.multiple_of(i * PAD, 16)
        for tile in range(pair // 128):
            lanes = slice(128 * tile, 128 * tile + 128)
            q = qkv[0, pl.ds(row, PAD), lanes]
            k = qkv[1, pl.ds(row, KEYS), lanes]
            v = qkv[2, pl.ds(row, KEYS), lanes]
            do = cg_s[pl.ds(row, PAD), lanes]
            dq = dk = dv = None
            for half in range(2):
                head = 2 * tile + half
                p = prob[head, pl.ds(row, PAD), :]
                do_half = do * halves[half]
                dp = mm(do_half, v, NT)
                p32 = p.astype(F32)
                ds = p32 * (dp - jnp.sum(dp * p32, -1, keepdims=True))
                bias_s[head] += ds
                ds = ds.astype(BF16)
                dv_part = mm(p, do_half, TN)
                dk_part = mm(ds, q * halves[half], TN)
                dq_part = mm(ds, k * halves[half])
                dq = dq_part if dq is None else dq + dq_part
                dk = dk_part if dk is None else dk + dk_part
                dv = dv_part if dv is None else dv + dv_part
            block = pl.ds(row, PAD)
            tg_s[block, 128 * tile : 128 * tile + 128] = (dq * score_scale).astype(BF16)
            tg_s[block, pair + 128 * tile : pair + 128 * tile + 128] = (dk[0:PAD] * score_scale).astype(BF16)
            tg_s[block, 2 * pair + 128 * tile : 2 * pair + 128 * tile + 128] = dv[0:PAD].astype(BF16)
        return carry

    lax.fori_loop(0, images, image, 0)
    small = 4 * local + PAD
    grad_a[small:, :] = jnp.zeros((grad_a.shape[0] - small, width), BF16)
    grad_b[small:, :] = jnp.zeros((grad_b.shape[0] - small, width), BF16)
    rows_a = [up_a[0:1, :]]
    rows_b = [up_b[0:1, :]]
    filler = jnp.zeros((1, width - local), F32)
    for t in range(3):
        part = tg_s[:, t * pair : (t + 1) * pair]
        dw = mm(part, first[...], TN).astype(BF16)
        grad_a[t * local : (t + 1) * local, :] = dw[0:local]
        grad_b[t * local : (t + 1) * local, :] = dw[local:pair]
        if t != 1:
            sums = colsum(part.astype(F32))
            rows_a.append(jnp.concatenate([sums[:, 0:local], filler], 1))
            rows_b.append(jnp.concatenate([sums[:, local:pair], filler], 1))
    blank = jnp.zeros((13, width), F32)
    grad_a[small : small + 16, :] = jnp.concatenate(rows_a + [blank], 0).astype(BF16)
    grad_b[small : small + 16, :] = jnp.concatenate(rows_b + [blank], 0).astype(BF16)
    for h in range(heads):
        grad_a[4 * local : 4 * local + PAD, h * KEYS : (h + 1) * KEYS] = bias_s[h].astype(BF16)
        grad_b[4 * local : 4 * local + PAD, h * KEYS : (h + 1) * KEYS] = bias_s[heads + h].astype(BF16)
    fg_o[...] = mm(tg_s[...], w_s[...]).astype(BF16)


def attention_backward(first, ag, ctx, qkv, prob, pack_a, pack_b, up_a, up_b, images, local):
    big, width = first.shape
    pair = 2 * local
    heads = pair // HEAD_DIM
    flops = 2 * big * (8 * width * pair + 8 * KEYS * HEAD_DIM * heads)
    pack = sds(pack_a.shape, BF16)
    return call(
        functools.partial(attention_backward_body, images, local),
        (pack, pack, sds((big, width), BF16)),
        flops * 2,
        2 * big * (3 * width + 5 * pair + heads * KEYS) + 8 * pack_a.size,
        scratch_shapes=[
            pltpu.VMEM((3 * pair, width), BF16),
            pltpu.VMEM((big, pair), BF16),
            pltpu.VMEM((big, 3 * pair), BF16),
            pltpu.VMEM((heads, PAD, KEYS), F32),
            pltpu.VMEM((pair, width), BF16),
        ],
    )(first, ag, ctx, qkv, prob, pack_a, pack_b, up_a, up_b)


def finish_body(images, fg_a, fg_b, mg, started, mask, vec, grad_o, sums_o, wide_s):
    width = mg.shape[1]
    rows = grad_o.shape[0]
    sums_o[...] = jnp.zeros(sums_o.shape, F32)
    for i in range(images):
        block = slice(i * PAD, (i + 1) * PAD)
        fgrad = fg_a[block, :].astype(F32) + fg_b[block, :].astype(F32)
        normed, inverse = norm_parts(started[block, :].astype(F32))
        total = mg[block, :] + norm_back(fgrad, normed, inverse, vec[FIRST_GAIN : FIRST_GAIN + 1])
        sums_o[0:1, :] += colsum(fgrad * normed)
        sums_o[1:2, :] += colsum(fgrad)
        wide_s[i * LEN : (i + 1) * LEN, :] = total[0:LEN]
    picked = mask[...] == 1.0
    for j in range(width // 128):
        lanes = slice(128 * j, 128 * j + 128)
        value = wide_s[0:rows, lanes]
        kept = jnp.where(picked, 0.0, value)
        grad_o[:, lanes] = kept
        sums_o[2:3, lanes] = colsum(value - kept)


def finish_stage(fg_a, fg_b, mg, started, mask_cols, vec, images):
    big, width = mg.shape
    rows = images * LEN
    return call(
        functools.partial(finish_body, images),
        (sds((rows, width), F32), sds((8, width), F32)),
        30 * big * width,
        big * width * 14,
        scratch_shapes=[pltpu.VMEM((-(-rows // 8) * 8, width), F32)],
    )(fg_a, fg_b, mg, started, mask_cols, vec)


def flip(value, axis, size, bit):
    return lax.ppermute(value, axis, [(i, i ^ bit) for i in range(size)])


def added(left, right):
    return (left.astype(F32) + right.astype(F32)).astype(BF16)


def wide_sum(value, wide):
    me = lax.axis_index("wide")
    bits = []
    bit = 1
    while bit < wide:
        bits.append(bit)
        bit *= 2
    for bit in bits:
        half = value.shape[0] // 2
        upper = (me & bit) != 0
        low, high = value[:half], value[half:]
        got = flip(jnp.where(upper, low, high), "wide", wide, bit)
        value = added(jnp.where(upper, high, low), got)
    for bit in bits[::-1]:
        upper = (me & bit) != 0
        got = flip(value, "wide", wide, bit)
        value = jnp.where(
            upper, jnp.concatenate([got, value], 0), jnp.concatenate([value, got], 0)
        )
    return value


def per_device(
    wide,
    narrow,
    tokens,
    patch_mask,
    cotangent,
    mask_token,
    first_gain,
    first_bias,
    qkv_weight,
    query_bias,
    value_bias,
    position_bias,
    output_weight,
    output_bias,
    attention_scale,
    second_gain,
    second_bias,
    up_weight,
    up_bias,
    down_weight,
    down_bias,
    feedforward_scale,
):
    rows, width = tokens.shape
    images = rows // LEN
    local = qkv_weight.shape[2]
    heads = local // HEAD_DIM
    core = functools.partial(flip, axis="narrow", size=narrow, bit=1)
    across = functools.partial(flip, axis="narrow", size=narrow, bit=2)

    qkv_rows = qkv_weight.transpose(1, 2, 0).reshape(3 * local, width)
    bias_rows = jnp.pad(position_bias, ((0, 0), (0, PAD - LEN), (0, KEYS - LEN)), constant_values=FAR)
    bias_rows = bias_rows.transpose(1, 0, 2).reshape(PAD, heads * KEYS)
    small_rows = jnp.concatenate(
        [
            up_bias[None],
            jnp.pad(query_bias[None], ((0, 0), (0, width - local))),
            jnp.pad(value_bias[None], ((0, 0), (0, width - local))),
            jnp.zeros((45, width), BF16),
        ],
        0,
    )
    pack0 = jnp.concatenate([qkv_rows, output_weight, bias_rows, small_rows], 0)
    pack1 = core(pack0)
    pack2 = across(pack0)
    pack3 = core(pack2)
    up1 = core(up_weight)
    down1 = core(down_weight)
    up2 = across(up_weight)
    down2 = across(down_weight)
    up3 = core(up2)
    down3 = core(down2)

    vec = jnp.stack(
        [
            mask_token,
            first_gain,
            first_bias,
            output_bias,
            attention_scale,
            second_gain,
            second_bias,
            down_bias,
            feedforward_scale,
        ]
        + [jnp.zeros_like(mask_token)] * 7
    ).astype(F32)
    mask_cols = jnp.broadcast_to(patch_mask.astype(F32)[:, None], (rows, 128))

    started, first, g, fg, sums_a = prep(tokens, mask_cols, cotangent, vec)
    qkv_a, prob_a, ctx_a = attention_forward(first, pack0, pack1, images, local)
    qkv_b, prob_b, ctx_b = attention_forward(first, pack2, pack3, images, local)
    branch, middle, second, second_t = middle_stage(
        ctx_a, ctx_b, (pack0, pack1, pack2, pack3), started, vec, images, local
    )
    small = 4 * local + PAD
    feeds, sgs, dups, ddowns, dbias = [], [], [], [], []
    for up, down, pack in (
        (up3, down3, pack3),
        (up2, down2, pack2),
        (up1, down1, pack1),
        (up_weight, down_weight, pack0),
    ):
        out = feed_stage(second, second_t, fg, up, down, pack[small : small + 16])
        for to, value in zip((feeds, sgs, dups, ddowns, dbias), out):
            to.append(value)

    layer_out, mg, ag, sums_b = turn_stage(feeds, sgs, middle, branch, g, vec, images)
    grad2, grad3, fg_b = attention_backward(
        first, ag, ctx_b, qkv_b, prob_b, pack2, pack3, dbias[1], dbias[0], images, local
    )
    grad0, grad1, fg_a = attention_backward(
        first, ag, ctx_a, qkv_a, prob_a, pack0, pack1, dbias[3], dbias[2], images, local
    )
    input_grad, sums_c = finish_stage(fg_a, fg_b, mg, started, mask_cols, vec, images)

    def reduced(g3, g2, g1, g0):
        far = added(g2, core(g3))
        got = across(far)
        return wide_sum(added(added(g0, core(g1)), got), wide)

    ddown = reduced(*ddowns)
    dup = reduced(*dups)
    dpack = reduced(grad3, grad2, grad1, grad0)

    vectors = jnp.concatenate([sums_a[0:1], sums_b[0:5], sums_c[0:3], jnp.zeros((7, width), F32)], 0)
    for axis, size in (("narrow", narrow), ("wide", wide)):
        bit = 1
        while bit < size:
            vectors = vectors + flip(vectors, axis, size, bit)
            bit *= 2

    dqkv = dpack[0 : 3 * local].reshape(3, local, width).transpose(2, 0, 1).astype(F32)
    dpos = dpack[4 * local : 4 * local + LEN].reshape(LEN, heads, KEYS)[:, :, :LEN]
    dpos = dpos.transpose(1, 0, 2).astype(F32)
    return (
        layer_out,
        input_grad,
        vectors[8],
        vectors[6],
        vectors[7],
        dqkv,
        dpack[small + 1, 0:local].astype(F32),
        dpack[small + 2, 0:local].astype(F32),
        dpos,
        dpack[3 * local : 4 * local].astype(F32),
        vectors[5],
        vectors[4],
        vectors[2],
        vectors[3],
        dup.astype(F32),
        dpack[small].astype(F32),
        ddown.astype(F32),
        vectors[0],
        vectors[1],
    )


def solution(mesh):
    rows = P(("wide", "narrow"), None)
    in_specs = (
        rows,
        P(("wide", "narrow")),
        rows,
        P(),
        P(),
        P(),
        P(None, None, "narrow"),
        P("narrow"),
        P("narrow"),
        P("narrow", None, None),
        P("narrow", None),
        P(),
        P(),
        P(),
        P(),
        P(None, "narrow"),
        P("narrow"),
        P("narrow", None),
        P(),
        P(),
    )
    out_specs = (
        rows,
        rows,
        P(),
        P(),
        P(),
        P(None, None, "narrow"),
        P("narrow"),
        P("narrow"),
        P("narrow", None, None),
        P("narrow", None),
        P(),
        P(),
        P(),
        P(),
        P(None, "narrow"),
        P("narrow"),
        P("narrow", None),
        P(),
        P(),
    )
    body = functools.partial(per_device, mesh.shape["wide"], mesh.shape["narrow"])
    return jax.shard_map(body, mesh=mesh, in_specs=in_specs, out_specs=out_specs, check_vma=False)
```

```python
import functools

import jax
import jax.numpy as jnp
from jax import lax
from jax.experimental import pallas as pl
from jax.experimental.pallas import tpu as pltpu
from jax.sharding import PartitionSpec as P

HEAD_DIM = 64
LEN = 197
PAD = 208
KEYS = 256
EPSILON = 1e-06
HALF_ROOT = 0.7071067811865476
DENSITY_FACTOR = 0.3989422804014327
FAR = -1e30
F32 = jnp.float32
BF16 = jnp.bfloat16
MIB = 1024 * 1024

(MASK_TOKEN, FIRST_GAIN, FIRST_BIAS, OUTPUT_BIAS, ATT_SCALE, SECOND_GAIN, SECOND_BIAS, DOWN_BIAS, FEED_SCALE) = range(9)

NT = (((1,), (1,)), ((), ()))
TN = (((0,), (0,)), ((), ()))
NN = (((1,), (0,)), ((), ()))


def mm(left, right, dims=NN):
    return lax.dot_general(left, right, dims, preferred_element_type=F32)


def call(body, out_shape, flops, bytes_accessed, trans=0, vmem=26, **kw):
    return pl.pallas_call(
        body,
        out_shape=out_shape,
        compiler_params=pltpu.CompilerParams(vmem_limit_bytes=vmem * MIB),
        cost_estimate=pl.CostEstimate(
            flops=int(flops) // 64, bytes_accessed=1024, transcendentals=0
        ),
        **kw,
    )


def sds(shape, dtype):
    return jax.ShapeDtypeStruct(shape, dtype)


def norm_parts(values):
    average = jnp.mean(values, -1, keepdims=True)
    centered = values - average
    inverse_dev = lax.rsqrt(jnp.mean(centered * centered, -1, keepdims=True) + EPSILON)
    return centered * inverse_dev, inverse_dev


def norm_back(grad_rows, normed, inverse_dev, gain):
    scaled = grad_rows * gain
    return inverse_dev * (
        scaled
        - jnp.mean(scaled, -1, keepdims=True)
        - normed * jnp.mean(scaled * normed, -1, keepdims=True)
    )


def colsum(values):
    return jnp.sum(values, 0, keepdims=True)


def prep_body(images, tok, mask, cot, vec, started_o, first_o, g_o, fg_o, sums_o, wide_s, pad_s):
    width = tok.shape[1]
    rows = tok.shape[0]
    picked = mask[...] == 1.0
    for j in range(width // 128):
        lanes = slice(128 * j, 128 * j + 128)
        wide_s[0:rows, lanes] = jnp.where(
            picked, vec[MASK_TOKEN : MASK_TOKEN + 1, lanes], tok[:, lanes].astype(F32)
        )
    for i in range(images):
        pad_s[0:LEN, :] = wide_s[i * LEN : (i + 1) * LEN, :]
        pad_s[LEN:PAD, :] = jnp.zeros((PAD - LEN, width), F32)
        values = pad_s[...]
        normed, _ = norm_parts(values)
        block = slice(i * PAD, (i + 1) * PAD)
        started_o[block, :] = values.astype(BF16)
        first_o[block, :] = (
            normed * vec[FIRST_GAIN : FIRST_GAIN + 1] + vec[FIRST_BIAS : FIRST_BIAS + 1]
        ).astype(BF16)
    wide_s[0:rows, :] = cot[...].astype(F32)
    total = jnp.zeros((1, width), F32)
    for i in range(images):
        pad_s[0:LEN, :] = wide_s[i * LEN : (i + 1) * LEN, :]
        values = pad_s[...]
        block = slice(i * PAD, (i + 1) * PAD)
        g_o[block, :] = values.astype(BF16)
        feed_grad = (values * vec[FEED_SCALE : FEED_SCALE + 1]).astype(BF16)
        fg_o[block, :] = feed_grad
        total += colsum(feed_grad.astype(F32))
    sums_o[0:1, :] = total
    sums_o[1:8, :] = jnp.zeros((7, width), F32)


def prep(tokens, mask_cols, cotangent, vec):
    rows, width = tokens.shape
    images = rows // LEN
    big = images * PAD
    b = sds((big, width), BF16)
    return call(
        functools.partial(prep_body, images),
        (b, b, b, b, sds((8, width), F32)),
        10 * rows * width,
        6 * 2 * rows * width,
        scratch_shapes=[pltpu.VMEM((-(-rows // 8) * 8, width), F32), pltpu.VMEM((PAD, width), F32)],
    )(tokens, mask_cols, cotangent, vec)


CUT = 112


def attention_forward_body(images, local, first, pack_a, pack_b, qkv_o, prob_o, ctx_o, w_s, bias_s):
    pair = 2 * local
    heads = local // HEAD_DIM
    width = first.shape[1]
    big = images * PAD
    score_scale = HEAD_DIM ** (-0.5)
    for t in range(3):
        w_s[t, 0:local, :] = pack_a[t * local : (t + 1) * local, :]
        w_s[t, local:pair, :] = pack_b[t * local : (t + 1) * local, :]
    table, small = 3 * local, 3 * local + PAD
    shift = jnp.concatenate(
        [pack[small : small + 16, 0:local] for pack in (pack_a, pack_b)], 1
    ).astype(F32)
    for at, pack in enumerate((pack_a, pack_b)):
        for h in range(heads):
            bias_s[at * heads + h] = pack[table:small, h * KEYS : (h + 1) * KEYS].astype(F32)
    for t in range(3):
        value = mm(first[...], w_s[t], NT)
        if t == 0:
            value = value + shift[0:1]
        if t == 2:
            value = value + shift[1:2]
        qkv_o[t, 0:big, :] = value.astype(BF16)
        qkv_o[t, big:, :] = jnp.zeros((KEYS - PAD, pair), BF16)
    lane = lax.broadcasted_iota(jnp.int32, (1, 128), 1)
    first_half = (lane < HEAD_DIM).astype(BF16)
    halves = (first_half, 1 - first_half)

    def image(i, carry):
        row = pl.multiple_of(i * PAD, 16)
        for tile in range(pair // 128):
            lanes = slice(128 * tile, 128 * tile + 128)
            q = qkv_o[0, pl.ds(row, PAD), lanes]
            k = qkv_o[1, pl.ds(row, KEYS), lanes]
            v = qkv_o[2, pl.ds(row, KEYS), lanes]
            context = None
            for half in range(2):
                head = 2 * tile + half
                scores = mm(q * halves[half], k, NT) * score_scale + bias_s[head]
                top = jnp.max(scores, -1, keepdims=True)
                powers = jnp.exp(scores - top)
                share = 1.0 / jnp.sum(powers, -1, keepdims=True)
                probabilities = (powers * share).astype(BF16)
                prob_o[head, pl.ds(row, PAD), :] = probabilities
                part = mm(probabilities, v * halves[half])
                context = part if context is None else context + part
            ctx_o[pl.ds(row, PAD), lanes] = context.astype(BF16)
        return carry

    lax.fori_loop(0, images, image, 0)


def attention_forward(first, pack_a, pack_b, images, local):
    big, width = first.shape
    pair = 2 * local
    heads = pair // HEAD_DIM
    flops = 2 * big * (width * 3 * pair + 2 * KEYS * HEAD_DIM * heads)
    return call(
        functools.partial(attention_forward_body, images, local),
        (
            sds((3, big + KEYS - PAD, pair), BF16),
            sds((heads, big, KEYS), BF16),
            sds((big, pair), BF16),
        ),
        flops * 2,
        2 * big * (width + 4 * pair + heads * KEYS),
        heads * big * KEYS,
        scratch_shapes=[pltpu.VMEM((3, pair, width), BF16), pltpu.VMEM((heads, PAD, KEYS), F32)],
    )(first, pack_a, pack_b)


def middle_body(images, local, ctx_a, ctx_b, p0, p1, p2, p3, started, vec, branch_o, middle_o, second_o, w_s):
    pair = 2 * local
    for at, part in enumerate((p0, p1, p2, p3)):
        w_s[at * local : (at + 1) * local, :] = part[...]

    def image(i, carry):
        row = pl.multiple_of(i * PAD, 16)
        block = pl.ds(row, PAD)
        branch = (
            mm(ctx_a[block, :], w_s[0:pair, :])
            + mm(ctx_b[block, :], w_s[pair : 2 * pair, :])
            + vec[OUTPUT_BIAS : OUTPUT_BIAS + 1]
        )
        branch_o[block, :] = branch
        middle = started[block, :].astype(F32) + vec[ATT_SCALE : ATT_SCALE + 1] * branch
        middle_o[block, :] = middle
        normed, _ = norm_parts(middle)
        second_o[block, :] = (
            normed * vec[SECOND_GAIN : SECOND_GAIN + 1] + vec[SECOND_BIAS : SECOND_BIAS + 1]
        ).astype(BF16)
        return carry

    lax.fori_loop(0, images, image, 0)


def middle_stage(ctx_a, ctx_b, packs, started, vec, images, local):
    big, width = started.shape
    return call(
        functools.partial(middle_body, images, local),
        (
            sds((big, width), F32),
            sds((big, width), F32),
            sds((big, width), BF16),
        ),
        2 * big * width * width + 20 * big * width,
        big * width * 16,
        scratch_shapes=[pltpu.VMEM((4 * local, width), BF16)],
    )(ctx_a, ctx_b, *packs, started, vec)


HID = 256
FEED_ROWS = 2 * HID + 16


def feed_body(count, near, place, second, fg, *refs):
    weights = refs[: 1 if near else count]
    feed_o, sg_o, grad_o, bias_o, feed_s, sg_s, w_s = refs[len(weights) :]
    step = pl.program_id(0)
    side = place[0]

    if not near:
        for at, ref in enumerate(weights):

            @pl.when(step == at)
            def _():
                w_s[...] = ref[...]

        block = w_s
    else:
        block = weights[0].at[0]
    wu = block[0:HID, :]
    wd = block[HID : 2 * HID, :]
    pre = mm(second[...], wu, NT) + block[2 * HID : 2 * HID + 16, 0:HID].astype(F32)[0:1]
    back = mm(fg[...], wd, NT)
    cdf = 0.5 * (1.0 + lax.erf(pre * HALF_ROOT))
    act = (pre * cdf).astype(BF16)
    slope = cdf + pre * (jnp.exp(-0.5 * pre * pre) * DENSITY_FACTOR)
    pg = (back * slope).astype(BF16)
    feed = mm(act, wd)
    sg = mm(pg, wu)

    @pl.when(step == 0)
    def _():
        feed_s[...] = feed
        sg_s[...] = sg

    @pl.when(step > 0)
    def _():
        feed_s[...] += feed
        sg_s[...] += sg

    grad_o[side] = mm(pg, second[...], TN).astype(BF16)
    grad_o[1 - side] = mm(act, fg[...], TN).astype(BF16)
    bias_o[...] = jnp.broadcast_to(colsum(pg.astype(F32)), bias_o.shape)

    @pl.when(step == pl.num_programs(0) - 1)
    def _():
        feed_o[...] = feed_s[...].astype(BF16)
        sg_o[...] = sg_s[...].astype(BF16)


def feed_stage(place, second, fg, weights, near):
    big, width = second.shape
    count = weights[0].shape[0] if near else len(weights)
    hidden = count * HID

    def block_of(step, place):
        if near:
            return step
        return jnp.where(step == 0, 0, jnp.where(step == 1, 1 + place[0], 2 - place[0]))

    whole = lambda shape: pl.BlockSpec(shape, lambda i, s: (0,) * len(shape))
    if near:
        weight_specs = [pl.BlockSpec((1, FEED_ROWS, width), lambda i, s: (i, 0, 0))]
    else:
        weight_specs = [whole((FEED_ROWS, width))] * len(weights)
    return pl.pallas_call(
        functools.partial(feed_body, count, near),
        out_shape=(
            sds((big, width), BF16),
            sds((big, width), BF16),
            sds((2, hidden, width), BF16),
            sds((8, hidden), F32),
        ),
        grid_spec=pltpu.PrefetchScalarGridSpec(
            num_scalar_prefetch=1,
            grid=(count,),
            in_specs=[whole((big, width)), whole((big, width))] + weight_specs,
            out_specs=(
                whole((big, width)),
                whole((big, width)),
                pl.BlockSpec((2, HID, width), lambda i, s: (0, block_of(i, s), 0)),
                pl.BlockSpec((8, HID), lambda i, s: (0, block_of(i, s))),
            ),
            scratch_shapes=[
                pltpu.VMEM((big, width), F32),
                pltpu.VMEM((big, width), F32),
                pltpu.VMEM((FEED_ROWS, width), BF16),
            ],
        ),
        compiler_params=pltpu.CompilerParams(vmem_limit_bytes=26 * MIB),
        cost_estimate=pl.CostEstimate(
            flops=big * width * hidden // 4, bytes_accessed=1024, transcendentals=0
        ),
    )(place, second, fg, *weights)


def turn_body(images, parts, *refs):
    feeds = refs[0:parts]
    sgs = refs[parts : 2 * parts]
    middle, branch, g, vec, out_o, mg_o, ag_o, sums_o, wide_s = refs[2 * parts :]
    width = middle.shape[1]
    sums_o[...] = jnp.zeros(sums_o.shape, F32)

    for i in range(images):
        block = slice(i * PAD, (i + 1) * PAD)
        feed = vec[DOWN_BIAS : DOWN_BIAS + 1]
        sg = jnp.zeros((PAD, width), F32)
        for at in range(parts):
            feed = feed + feeds[at][block, :].astype(F32)
            sg = sg + sgs[at][block, :].astype(F32)
        rows = g[block, :].astype(F32)
        mid = middle[block, :]
        out = mid + vec[FEED_SCALE : FEED_SCALE + 1] * feed
        wide_s[i * LEN : (i + 1) * LEN, :] = out[0:LEN]
        normed, inverse = norm_parts(mid)
        grad = rows + norm_back(sg, normed, inverse, vec[SECOND_GAIN : SECOND_GAIN + 1])
        mg_o[block, :] = grad
        att = (vec[ATT_SCALE : ATT_SCALE + 1] * grad).astype(BF16)
        ag_o[block, :] = att
        sums_o[0:1, :] += colsum(rows * feed)
        sums_o[1:2, :] += colsum(sg * normed)
        sums_o[2:3, :] += colsum(sg)
        sums_o[3:4, :] += colsum(grad * branch[block, :])
        sums_o[4:5, :] += colsum(att.astype(F32))
    out_o[...] = wide_s[0 : out_o.shape[0], :].astype(BF16)


def turn_stage(feeds, sgs, middle, branch, g, vec, images):
    big, width = middle.shape
    rows = images * LEN
    return call(
        functools.partial(turn_body, images, len(feeds)),
        (sds((rows, width), BF16), sds((big, width), F32), sds((big, width), BF16), sds((8, width), F32)),
        40 * big * width,
        big * width * (18 + 4 * len(feeds)),
        scratch_shapes=[pltpu.VMEM((-(-rows // 8) * 8, width), F32)],
    )(*feeds, *sgs, middle, branch, g, vec)


def attention_backward_body(
    images, local, place, first, ag, ctx, qkv, prob, pack_a, pack_b, out_a, out_b, up_a, up_b,
    grad_a, grad_b, fg_o, w_s, cg_s, tg_s, bias_s, wo_s,
):
    pair = 2 * local
    heads = local // HEAD_DIM
    big, width = first.shape
    score_scale = HEAD_DIM ** (-0.5)
    side = place[0]
    sides = (side, 1 - side)
    for t in range(3):
        w_s[t * pair : t * pair + local, :] = pack_a[t * local : (t + 1) * local, :]
        w_s[t * pair + local : (t + 1) * pair, :] = pack_b[t * local : (t + 1) * local, :]
    wo_s[0:local, :] = out_a[...]
    wo_s[local:pair, :] = out_b[...]
    cg_s[0:big, :] = mm(ag[...], wo_s[...], NT).astype(BF16)
    d_out = mm(ctx[...], ag[...], TN).astype(BF16)
    grad_a[sides[1], local : 2 * local, :] = d_out[0:local]
    grad_b[sides[1], local : 2 * local, :] = d_out[local:pair]
    bias_s[...] = jnp.zeros(bias_s.shape, F32)
    lane = lax.broadcasted_iota(jnp.int32, (1, 128), 1)
    first_half = (lane < HEAD_DIM).astype(BF16)
    halves = (first_half, 1 - first_half)

    def image(i, carry):
        row = pl.multiple_of(i * PAD, 16)
        for tile in range(pair // 128):
            lanes = slice(128 * tile, 128 * tile + 128)
            q = qkv[0, pl.ds(row, PAD), lanes]
            k = qkv[1, pl.ds(row, KEYS), lanes]
            v = qkv[2, pl.ds(row, KEYS), lanes]
            do = cg_s[pl.ds(row, PAD), lanes]
            dq = dk = dv = None
            for half in range(2):
                head = 2 * tile + half
                p = prob[head, pl.ds(row, PAD), :]
                do_half = do * halves[half]
                dp = mm(do_half, v, NT)
                p32 = p.astype(F32)
                ds = p32 * (dp - jnp.sum(dp * p32, -1, keepdims=True))
                bias_s[head] += ds
                ds = ds.astype(BF16)
                dv_part = mm(p, do_half, TN)
                dk_part = mm(ds, q * halves[half], TN)
                dq_part = mm(ds, k * halves[half])
                dq = dq_part if dq is None else dq + dq_part
                dk = dk_part if dk is None else dk + dk_part
                dv = dv_part if dv is None else dv + dv_part
            block = pl.ds(row, PAD)
            tg_s[block, 128 * tile : 128 * tile + 128] = (dq * score_scale).astype(BF16)
            tg_s[block, pair + 128 * tile : pair + 128 * tile + 128] = (dk[0:PAD] * score_scale).astype(BF16)
            tg_s[block, 2 * pair + 128 * tile : 2 * pair + 128 * tile + 128] = dv[0:PAD].astype(BF16)
        return carry

    lax.fori_loop(0, images, image, 0)
    small = (2 * local + CUT, 2 * local + PAD - CUT)
    filler = jnp.zeros((1, width - local), F32)
    sums = []
    for t, (half, row) in enumerate(((0, 0), (0, local), (1, 0))):
        part = tg_s[:, t * pair : (t + 1) * pair]
        dw = mm(part, first[...], TN).astype(BF16)
        grad_a[sides[half], row : row + local, :] = dw[0:local]
        grad_b[sides[half], row : row + local, :] = dw[local:pair]
        sums.append(colsum(part.astype(F32)))
    for at, (grad, hidden_bias) in enumerate(((grad_a, up_a), (grad_b, up_b))):
        lanes = slice(at * local, (at + 1) * local)
        grad[sides[0], small[0] :, :] = jnp.concatenate(
            [
                jnp.concatenate([sums[0][:, lanes], filler], 1),
                hidden_bias[0:1, :],
                jnp.zeros((14, width), F32),
            ],
            0,
        ).astype(BF16)
        grad[sides[1], small[1] :, :] = jnp.concatenate(
            [jnp.concatenate([sums[2][:, lanes], filler], 1), jnp.zeros((31, width), F32)], 0
        ).astype(BF16)
        for h in range(heads):
            lanes = slice(h * KEYS, (h + 1) * KEYS)
            grad[sides[0], 2 * local : 2 * local + CUT, lanes] = bias_s[at * heads + h, 0:CUT].astype(BF16)
            grad[sides[1], 2 * local : 2 * local + PAD - CUT, lanes] = bias_s[
                at * heads + h, CUT:PAD
            ].astype(BF16)
    fg_o[...] = mm(tg_s[...], w_s[...]).astype(BF16)


def attention_backward(place, first, ag, forward, packs, outs, ups, images, local):
    qkv, prob, ctx = forward
    big, width = first.shape
    pair = 2 * local
    heads = pair // HEAD_DIM
    flops = 2 * big * (8 * width * pair + 8 * KEYS * HEAD_DIM * heads)
    pack = sds((2, 2 * local + CUT + 16, width), BF16)
    return call(
        functools.partial(attention_backward_body, images, local),
        (pack, pack, sds((big, width), BF16)),
        flops * 2,
        2 * big * (3 * width + 5 * pair + heads * KEYS),
        scratch_shapes=[
            pltpu.VMEM((3 * pair, width), BF16),
            pltpu.VMEM((big, pair), BF16),
            pltpu.VMEM((big, 3 * pair), BF16),
            pltpu.VMEM((heads, PAD, KEYS), F32),
            pltpu.VMEM((pair, width), BF16),
        ],
        in_specs=[pl.BlockSpec(memory_space=pltpu.SMEM)] + [pl.BlockSpec(memory_space=pltpu.VMEM)] * 11,
    )(place, first, ag, ctx, qkv, prob, *packs, *outs, *ups)


def finish_body(images, fg_a, fg_b, mg, started, mask, vec, grad_o, sums_o, wide_s):
    width = mg.shape[1]
    rows = grad_o.shape[0]
    sums_o[...] = jnp.zeros(sums_o.shape, F32)
    for i in range(images):
        block = slice(i * PAD, (i + 1) * PAD)
        fgrad = fg_a[block, :].astype(F32) + fg_b[block, :].astype(F32)
        normed, inverse = norm_parts(started[block, :].astype(F32))
        total = mg[block, :] + norm_back(fgrad, normed, inverse, vec[FIRST_GAIN : FIRST_GAIN + 1])
        sums_o[0:1, :] += colsum(fgrad * normed)
        sums_o[1:2, :] += colsum(fgrad)
        wide_s[i * LEN : (i + 1) * LEN, :] = total[0:LEN]
    picked = mask[...] == 1.0
    for j in range(width // 128):
        lanes = slice(128 * j, 128 * j + 128)
        value = wide_s[0:rows, lanes]
        kept = jnp.where(picked, 0.0, value)
        grad_o[:, lanes] = kept
        sums_o[2:3, lanes] = colsum(value - kept)


def finish_stage(fg_a, fg_b, mg, started, mask_cols, vec, images):
    big, width = mg.shape
    rows = images * LEN
    return call(
        functools.partial(finish_body, images),
        (sds((rows, width), F32), sds((8, width), F32)),
        30 * big * width,
        big * width * 14,
        scratch_shapes=[pltpu.VMEM((-(-rows // 8) * 8, width), F32)],
    )(fg_a, fg_b, mg, started, mask_cols, vec)


def flip(value, axis, size, bit):
    return lax.ppermute(value, axis, [(i, i ^ bit) for i in range(size)])


def gathered_body(count, place, *refs):
    *values, out = refs
    rows = out.shape[1]
    for at in range(count):
        block = pl.ds(pl.multiple_of(jnp.bitwise_xor(place[1], at) * rows, 8), rows)
        total = None
        for value in values:
            part = (value[block, :] if len(value.shape) == 2 else value[0, block, :]).astype(F32)
            total = part if total is None else total + part
        out[at] = total.astype(BF16)


def summed_pieces(place, values, count):
    rows, width = values[-1].shape
    specs = [
        pl.BlockSpec((1, rows, width), lambda i: (0, 0, 0))
        if len(v.shape) == 3
        else pl.BlockSpec((rows, width), lambda i: (0, 0))
        for v in values
    ]
    return call(
        functools.partial(gathered_body, count),
        sds((count, rows // count, width), BF16),
        rows * width,
        2 * len(values) * rows * width,
        grid=(1,),
        in_specs=[pl.BlockSpec(memory_space=pltpu.SMEM)] + specs,
        out_specs=pl.BlockSpec((count, rows // count, width), lambda i: (0, 0, 0)),
    )(place, *values)


def placed_body(place, *refs):
    *values, out = refs
    rows = values[0].shape[0]
    for at, value in enumerate(values):
        out[pl.ds(pl.multiple_of(jnp.bitwise_xor(place[1], at) * rows, 8), rows), :] = value[...]


def placed(place, values):
    rows, width = values[0].shape
    return call(
        placed_body,
        sds((rows * len(values), width), BF16),
        rows * width,
        4 * len(values) * rows * width,
        in_specs=[pl.BlockSpec(memory_space=pltpu.SMEM)]
        + [pl.BlockSpec(memory_space=pltpu.VMEM)] * len(values),
    )(place, *values)


def added(left, right):
    return (left.astype(F32) + right.astype(F32)).astype(BF16)


def after(values, *earlier):
    return lax.optimization_barrier((values, earlier))[0]


def sync(*values):
    return lax.optimization_barrier(values)


def wide_groups(wide):
    groups = []
    bit = 2
    while bit < wide:
        size = 4 if 2 * bit < wide else 2
        groups.append((bit, size))
        bit *= size
    return groups


def per_device(
    wide,
    narrow,
    tokens,
    patch_mask,
    cotangent,
    mask_token,
    first_gain,
    first_bias,
    qkv_weight,
    query_bias,
    value_bias,
    position_bias,
    output_weight,
    output_bias,
    attention_scale,
    second_gain,
    second_bias,
    up_weight,
    up_bias,
    down_weight,
    down_bias,
    feedforward_scale,
):
    rows, width = tokens.shape
    images = rows // LEN
    local = qkv_weight.shape[2]
    heads = local // HEAD_DIM
    core = functools.partial(flip, axis="narrow", size=narrow, bit=1)
    across = functools.partial(flip, axis="narrow", size=narrow, bit=2)
    beside = functools.partial(flip, axis="wide", size=wide, bit=1)

    def corner(value):
        pairs = [
            (w * narrow + n, (w ^ 1) * narrow + (n ^ 2)) for w in range(wide) for n in range(narrow)
        ]
        return lax.ppermute(value, ("wide", "narrow"), pairs)

    me = lax.axis_index("wide")
    side = me & 1
    groups = wide_groups(wide)
    places = [jnp.stack([side, (me // bit) & (size - 1)]).astype(jnp.int32) for bit, size in groups]
    place = places[0]

    bias_table = jnp.pad(position_bias, ((0, 0), (0, PAD - LEN), (0, KEYS - LEN)), constant_values=FAR)
    pack0 = jnp.concatenate(
        [
            qkv_weight.transpose(1, 2, 0).reshape(3 * local, width),
            bias_table.transpose(1, 0, 2).reshape(PAD, heads * KEYS),
            jnp.pad(jnp.stack([query_bias, value_bias]), ((0, 14), (0, width - local))),
        ],
        0,
    )
    count = up_weight.shape[1] // HID
    feed0 = jnp.concatenate(
        [
            up_weight.T.reshape(count, HID, width),
            down_weight.reshape(count, HID, width),
            jnp.pad(up_bias.reshape(count, 1, HID), ((0, 0), (0, 15), (0, width - HID))),
        ],
        1,
    )
    pack2 = across(pack0)
    pack1 = core(pack0)
    feed1 = core(feed0)
    out1 = core(output_weight)

    vec = jnp.stack(
        [
            mask_token,
            first_gain,
            first_bias,
            output_bias,
            attention_scale,
            second_gain,
            second_bias,
            down_bias,
            feedforward_scale,
        ]
        + [jnp.zeros_like(mask_token)] * 7
    ).astype(F32)
    mask_cols = jnp.broadcast_to(patch_mask.astype(F32)[:, None], (rows, 128))

    started, first, g, fg, sums_a = prep(tokens, mask_cols, cotangent, vec)
    att_a = attention_forward(first, pack0, pack1, images, local)
    att_a, pack2 = sync(att_a, pack2)
    pack3 = core(pack2)
    out0, mine, block0 = after(
        (output_weight, lax.dynamic_index_in_dim(feed0, 1 + side, 0, keepdims=False), feed0[0]), pack2
    )
    out2 = across(out0)
    got2 = across(mine)
    att_b = attention_forward(first, pack2, pack3, images, local)
    att_b, out2, out1 = sync(att_b, out2, out1)
    out3 = core(out2)
    outs = (output_weight, out1, out2, out3)
    mid = middle_stage(att_a[2], att_b[2], outs, started, vec, images, local)
    (branch, middle, second), got2, feed1, block0 = sync(mid, got2, feed1, block0)
    other2 = beside(got2)
    direct2 = across(block0)
    got3 = core(got2)
    feed_1, sg_1, d1, bias1 = feed_stage(place, second, fg, (feed1,), True)
    fg, d1, direct2, other2 = sync(after(fg, feed_1), d1, direct2, other2)
    from1 = core(d1)
    direct3 = core(direct2)
    other3 = core(other2)
    feed_0, sg_0, d0, bias0 = feed_stage(place, second, fg, (feed0,), True)
    fg, d0, direct3, other3, got3, from1 = sync(after(fg, feed_0), d0, direct3, other3, got3, from1)
    feed_3, sg_3, d3, bias3 = feed_stage(place, second, fg, (direct3, got3, other3), False)
    from3 = core(d3)
    near1 = added(d0[1], from1[1])
    fg, near1 = sync(after(fg, feed_3), near1)
    got_x = beside(near1)
    feed_2, sg_2, d2, bias2 = feed_stage(place, second, fg, (direct2, got2, other2), False)
    far0, far1 = added(d2[0], from3[0]), added(d2[1], from3[1])
    g, far0, far1 = sync(g, far0, far1)
    got_y = across(far0)
    got_d = corner(far1)
    layer_out, mg, ag, sums_b = turn_stage(
        (feed_0, feed_1, feed_2, feed_3), (sg_0, sg_1, sg_2, sg_3), middle, branch, g, vec, images
    )
    back_b = attention_backward(
        place, first, ag, att_b, (pack2, pack3), outs[2:], (bias2, bias3), images, local
    )
    back_b, ag = sync(back_b, ag)
    att_from3 = core(back_b[1])
    back_a = attention_backward(
        place, first, ag, att_a, (pack0, pack1), outs[:2], (bias0, bias1), images, local
    )
    back_a, got_x, got_y, got_d = sync(back_a, got_x, got_y, got_d)
    grad0, grad1, fg_a = back_a
    grad2, _, fg_b = back_b
    att_from1 = core(grad1)

    def pieces_of(level, values):
        bit, size = groups[level]
        pieces = summed_pieces(places[level], values, size)
        return [pieces[0]] + [flip(pieces[at], "wide", wide, bit * at) for at in range(1, size)]

    def total(values):
        return sum(v.astype(F32) for v in values).astype(BF16)

    def spread(level, piece):
        bit, size = groups[level]
        return [piece] + [flip(piece, "wide", wide, bit * at) for at in range(1, size)]

    def scattered(values):
        for level in range(len(groups)):
            values = pieces_of(level, values)
        return values

    def collected(values):
        for level in range(len(groups))[::-1]:
            piece = placed(places[level], values)
            if level:
                values = spread(level - 1, piece)
        return piece

    feed_parts = scattered((d0, from1, got_y, got_d, got_x))
    feed_parts[0], att_from3 = sync(feed_parts[0], att_from3)
    att_far0, att_far1 = added(grad2[0], att_from3[0]), added(grad2[1], att_from3[1])
    att_far0, att_far1, feed_parts[0] = sync(att_far0, att_far1, feed_parts[0])
    att_y = across(att_far0)
    att_d = corner(att_far1)
    near1 = added(grad0[1], att_from1[1])
    fg_a, near1, att_far0, att_far1 = sync(fg_a, near1, att_far0, att_far1)
    att_x = beside(near1)
    input_grad, sums_c = finish_stage(fg_a, fg_b, mg, started, mask_cols, vec, images)
    vectors = jnp.concatenate([sums_a[0:1], sums_b[0:5], sums_c[0:3], jnp.zeros((7, width), F32)], 0)
    steps = []
    for axis, size in (("narrow", narrow), ("wide", wide)):
        bit = 1
        while bit < size:
            steps.append((axis, size, bit))
            bit *= 2

    def exchange_vectors(vectors):
        return vectors, flip(vectors, *steps.pop(0))

    vectors, partner = exchange_vectors(vectors)
    vectors, feed_parts = sync(vectors, feed_parts)
    feed_parts = spread(len(groups) - 1, total(feed_parts))
    feed_parts[0], att_y, att_d, att_x, vectors, partner = sync(
        feed_parts[0], att_y, att_d, att_x, vectors, partner
    )
    vectors, partner = exchange_vectors(vectors + partner)
    att_parts = scattered((grad0, att_from1, att_y, att_d, att_x))
    att_parts[0], feed_parts, vectors, partner = sync(att_parts[0], feed_parts, vectors, partner)
    vectors, partner = exchange_vectors(vectors + partner)
    feed_piece = collected(feed_parts)
    feed_piece, att_parts, vectors, partner = sync(feed_piece, att_parts, vectors, partner)
    vectors, partner = exchange_vectors(vectors + partner)
    feed_beyond = beside(feed_piece)
    att_parts = spread(len(groups) - 1, total(att_parts))
    att_piece = collected(att_parts)
    att_piece, vectors, partner = sync(att_piece, vectors, partner)
    att_beyond = beside(att_piece)
    vectors = vectors + partner
    while steps:
        vectors = sum(exchange_vectors(vectors))

    def ordered(piece, beyond):
        return jnp.where(side == 0, piece, beyond), jnp.where(side == 0, beyond, piece)

    dup, ddown = ordered(feed_piece, feed_beyond)
    dpack_a, dpack_b = ordered(att_piece, att_beyond)

    low = 2 * local
    dqkv = jnp.stack([dpack_a[0:local], dpack_a[local:low], dpack_b[0:local]])
    dqkv = dqkv.transpose(2, 0, 1).astype(F32)
    dpos = jnp.concatenate([dpack_a[low : low + CUT], dpack_b[low : low + LEN - CUT]], 0)
    dpos = dpos.reshape(LEN, heads, KEYS)[:, :, :LEN].transpose(1, 0, 2).astype(F32)
    return (
        layer_out,
        input_grad,
        vectors[8],
        vectors[6],
        vectors[7],
        dqkv,
        dpack_a[low + CUT, 0:local].astype(F32),
        dpack_b[low + PAD - CUT, 0:local].astype(F32),
        dpos,
        dpack_b[local:low].astype(F32),
        vectors[5],
        vectors[4],
        vectors[2],
        vectors[3],
        dup.T.astype(F32),
        dpack_a[low + CUT + 1].astype(F32),
        ddown.astype(F32),
        vectors[0],
        vectors[1],
    )


def solution(mesh):
    rows = P(("wide", "narrow"), None)
    in_specs = (
        rows,
        P(("wide", "narrow")),
        rows,
        P(),
        P(),
        P(),
        P(None, None, "narrow"),
        P("narrow"),
        P("narrow"),
        P("narrow", None, None),
        P("narrow", None),
        P(),
        P(),
        P(),
        P(),
        P(None, "narrow"),
        P("narrow"),
        P("narrow", None),
        P(),
        P(),
    )
    out_specs = (
        rows,
        rows,
        P(),
        P(),
        P(),
        P(None, None, "narrow"),
        P("narrow"),
        P("narrow"),
        P("narrow", None, None),
        P("narrow", None),
        P(),
        P(),
        P(),
        P(),
        P(None, "narrow"),
        P("narrow"),
        P("narrow", None),
        P(),
        P(),
    )
    body = functools.partial(per_device, mesh.shape["wide"], mesh.shape["narrow"])
    return jax.shard_map(body, mesh=mesh, in_specs=in_specs, out_specs=out_specs, check_vma=False)
```

```python
import functools

import jax
import jax.numpy as jnp
from jax import lax
from jax.experimental import pallas as pl
from jax.experimental.pallas import tpu as pltpu
from jax.sharding import PartitionSpec as P

HEAD_DIM = 64
LEN = 197
PAD = 208
KEYS = 256
EPSILON = 1e-06
HALF_ROOT = 0.7071067811865476
DENSITY_FACTOR = 0.3989422804014327
FAR = -1e30
F32 = jnp.float32
BF16 = jnp.bfloat16
MIB = 1024 * 1024

(MASK_TOKEN, FIRST_GAIN, FIRST_BIAS, OUTPUT_BIAS, ATT_SCALE, SECOND_GAIN, SECOND_BIAS, DOWN_BIAS, FEED_SCALE) = range(9)

NT = (((1,), (1,)), ((), ()))
TN = (((0,), (0,)), ((), ()))
NN = (((1,), (0,)), ((), ()))


def mm(left, right, dims=NN):
    return lax.dot_general(left, right, dims, preferred_element_type=F32)


def call(body, out_shape, flops, bytes_accessed, trans=0, vmem=16, **kw):
    return pl.pallas_call(
        body,
        out_shape=out_shape,
        compiler_params=pltpu.CompilerParams(vmem_limit_bytes=vmem * MIB),
        cost_estimate=pl.CostEstimate(
            flops=int(flops) // 64, bytes_accessed=1024, transcendentals=0
        ),
        **kw,
    )


def sds(shape, dtype):
    return jax.ShapeDtypeStruct(shape, dtype)


def norm_parts(values):
    average = jnp.mean(values, -1, keepdims=True)
    centered = values - average
    inverse_dev = lax.rsqrt(jnp.mean(centered * centered, -1, keepdims=True) + EPSILON)
    return centered * inverse_dev, inverse_dev


def norm_back(grad_rows, normed, inverse_dev, gain):
    scaled = grad_rows * gain
    return inverse_dev * (
        scaled
        - jnp.mean(scaled, -1, keepdims=True)
        - normed * jnp.mean(scaled * normed, -1, keepdims=True)
    )


def colsum(values):
    return jnp.sum(values, 0, keepdims=True)


def prep_body(images, tok, mask, cot, *refs):
    *vectors, started_o, first_o, g_o, fg_o, sums_o, vec, wide_s, pad_s = refs
    vec[...] = jnp.zeros(vec.shape, F32)
    for at, vector in enumerate(vectors):
        vec[at : at + 1, :] = vector[...].astype(F32)[None]
    width = tok.shape[1]
    rows = tok.shape[0]
    picked = mask[...] == 1.0
    for j in range(width // 128):
        lanes = slice(128 * j, 128 * j + 128)
        wide_s[0:rows, lanes] = jnp.where(
            picked, vec[MASK_TOKEN : MASK_TOKEN + 1, lanes], tok[:, lanes].astype(F32)
        )
    for i in range(images):
        pad_s[0:LEN, :] = wide_s[i * LEN : (i + 1) * LEN, :]
        pad_s[LEN:PAD, :] = jnp.zeros((PAD - LEN, width), F32)
        values = pad_s[...]
        normed, _ = norm_parts(values)
        block = slice(i * PAD, (i + 1) * PAD)
        started_o[block, :] = values.astype(BF16)
        first_o[block, :] = (
            normed * vec[FIRST_GAIN : FIRST_GAIN + 1] + vec[FIRST_BIAS : FIRST_BIAS + 1]
        ).astype(BF16)
    wide_s[0:rows, :] = cot[...].astype(F32)
    total = jnp.zeros((1, width), F32)
    for i in range(images):
        pad_s[0:LEN, :] = wide_s[i * LEN : (i + 1) * LEN, :]
        values = pad_s[...]
        block = slice(i * PAD, (i + 1) * PAD)
        g_o[block, :] = values.astype(BF16)
        feed_grad = (values * vec[FEED_SCALE : FEED_SCALE + 1]).astype(BF16)
        fg_o[block, :] = feed_grad
        total += colsum(feed_grad.astype(F32))
    sums_o[0:1, :] = total
    sums_o[1:8, :] = jnp.zeros((7, width), F32)


def prep(tokens, mask_cols, cotangent, vectors):
    rows, width = tokens.shape
    images = rows // LEN
    big = images * PAD
    b = sds((big, width), BF16)
    return call(
        functools.partial(prep_body, images),
        (b, b, b, b, sds((8, width), F32), sds((16, width), F32)),
        10 * rows * width,
        6 * 2 * rows * width,
        scratch_shapes=[pltpu.VMEM((-(-rows // 8) * 8, width), F32), pltpu.VMEM((PAD, width), F32)],
    )(tokens, mask_cols, cotangent, *vectors)


THIRD = 80
CUT = 112
HID = 256


def three(refs, near):
    if near:
        return [[ref.at[at] for at in range(3)] for ref in refs]
    return [refs[0:3], refs[3:6]]


def spots_of(near, side):
    return (0, 1, 2) if near else (0, 1 + side, 2 - side)


def gather_weights(w_s, shards, near, side, local):
    for at, blocks in enumerate(shards):
        for block, spot in zip(blocks, spots_of(near, side)):
            row = spot * 2 * local + at * local
            row = row if near else pl.multiple_of(row, 64)
            w_s[pl.ds(row, local), :] = block[0:local, :]


def attention_rows_body(local, place, qkv, table, query_bias, value_bias, out, pack_o, mine_o, direct_o, table_s):
    heads, length, _ = table.shape
    width = qkv.shape[2]
    side = place[0]
    filler = jnp.zeros((1, width - local), F32)
    for h in range(heads):
        table_s[h] = jnp.full(table_s.shape[1:], FAR, F32)
        table_s[h, 0:length, 0:length] = table[h].astype(F32)

    def store(to, t):
        to[0:local, :] = qkv[t]
        rows = min(THIRD, PAD - t * THIRD)
        for h in range(heads):
            to[local : local + rows, h * KEYS : (h + 1) * KEYS] = table_s[
                h, t * THIRD : t * THIRD + rows, :
            ].astype(BF16)
        if rows < THIRD:
            tile = [
                jnp.concatenate([bias[...].astype(F32)[None], filler], 1)
                for bias in (query_bias, value_bias)
            ]
            tile.append(jnp.zeros((THIRD - rows - 2, width), F32))
            to[local + rows : local + THIRD, :] = jnp.concatenate(tile, 0).astype(BF16)

    for t in range(3):
        store(pack_o.at[t], t)
    store(direct_o, 0)
    direct_o[local + THIRD :, :] = out[...]
    for t in (1, 2):

        @pl.when(side == t - 1)
        def _():
            store(mine_o, t)


def attention_rows(place, qkv_rows, table, query_bias, value_bias, out):
    _, local, width = qkv_rows.shape
    block = (local + THIRD, width)
    return call(
        functools.partial(attention_rows_body, local),
        (sds((3,) + block, BF16), sds(block, BF16), sds((block[0] + local, width), BF16)),
        0,
        0,
        in_specs=[pl.BlockSpec(memory_space=pltpu.SMEM)] + [pl.BlockSpec(memory_space=pltpu.VMEM)] * 5,
        scratch_shapes=[pltpu.VMEM((table.shape[0], PAD, KEYS), F32)],
    )(place, qkv_rows, table, query_bias, value_bias, out)


def hidden_rows_body(place, up, down, bias, feed_o, mine_o, direct_o):
    count = feed_o.shape[0]
    width = up.shape[0]
    side = place[0]
    for at in range(count):
        hidden = slice(at * HID, (at + 1) * HID)
        out = feed_o.at[at]
        out[0:HID, :] = up[:, hidden].T
        out[HID : 2 * HID, :] = down[hidden, :]
        row = jnp.concatenate([bias[...].astype(F32)[None][:, hidden], jnp.zeros((1, width - HID), F32)], 1)
        out[2 * HID :, :] = jnp.concatenate([row, jnp.zeros((15, width), F32)], 0).astype(BF16)
    direct_o[...] = feed_o[0]
    mine_o[...] = feed_o[1 + side]


def hidden_rows(place, up, down, bias):
    width, hidden = up.shape
    block = (2 * HID + 16, width)
    return call(
        hidden_rows_body,
        (sds((hidden // HID,) + block, BF16), sds(block, BF16), sds(block, BF16)),
        0,
        0,
        in_specs=[pl.BlockSpec(memory_space=pltpu.SMEM)] + [pl.BlockSpec(memory_space=pltpu.VMEM)] * 3,
    )(place, up, down, bias)


def attention_forward_body(images, local, near, place, first, *refs):
    packs = refs[: 2 if near else 6]
    qkv_o, prob_o, ctx_o, w_s, bias_s = refs[len(packs) :]
    pair = 2 * local
    heads = local // HEAD_DIM
    big = images * PAD
    score_scale = HEAD_DIM ** (-0.5)
    side = place[0]
    shards = three(packs, near)
    gather_weights(w_s, shards, near, side, local)
    small = local + PAD - 2 * THIRD
    tiles = []
    for at, blocks in enumerate(shards):
        for block, spot in zip(blocks, spots_of(near, side)):
            row = spot * THIRD
            row = row if near else pl.multiple_of(row, 16)
            for h in range(heads):
                bias_s[at * heads + h, pl.ds(row, THIRD), :] = block[
                    local : local + THIRD, h * KEYS : (h + 1) * KEYS
                ].astype(F32)
        last = [block[small : small + 16, 0:local].astype(F32) for block in blocks[1:]]
        tiles.append(last[1] if near else jnp.where(side == 0, last[1], last[0]))
    shift = jnp.concatenate(tiles, 1)
    for t in range(3):
        value = mm(first[...], w_s[t * pair : (t + 1) * pair, :], NT)
        if t == 0:
            value = value + shift[0:1]
        if t == 2:
            value = value + shift[1:2]
        qkv_o[t, 0:big, :] = value.astype(BF16)
        qkv_o[t, big:, :] = jnp.zeros((KEYS - PAD, pair), BF16)
    lane = lax.broadcasted_iota(jnp.int32, (1, 128), 1)
    first_half = (lane < HEAD_DIM).astype(BF16)
    halves = (first_half, 1 - first_half)

    def image(i, carry):
        row = pl.multiple_of(i * PAD, 16)
        for tile in range(pair // 128):
            lanes = slice(128 * tile, 128 * tile + 128)
            q = qkv_o[0, pl.ds(row, PAD), lanes]
            k = qkv_o[1, pl.ds(row, KEYS), lanes]
            v = qkv_o[2, pl.ds(row, KEYS), lanes]
            context = None
            for half in range(2):
                head = 2 * tile + half
                scores = mm(q * halves[half], k, NT) * score_scale + bias_s[head, 0:PAD, :]
                top = jnp.max(scores, -1, keepdims=True)
                powers = jnp.exp(scores - top)
                share = 1.0 / jnp.sum(powers, -1, keepdims=True)
                probabilities = (powers * share).astype(BF16)
                prob_o[head, pl.ds(row, PAD), :] = probabilities
                part = mm(probabilities, v * halves[half])
                context = part if context is None else context + part
            ctx_o[pl.ds(row, PAD), lanes] = context.astype(BF16)
        return carry

    lax.fori_loop(0, images, image, 0)


def attention_forward(place, first, packs, near, images, local):
    big, width = first.shape
    pair = 2 * local
    heads = pair // HEAD_DIM
    flops = 2 * big * (width * 3 * pair + 2 * KEYS * HEAD_DIM * heads)
    return call(
        functools.partial(attention_forward_body, images, local, near),
        (
            sds((3, big + KEYS - PAD, pair), BF16),
            sds((heads, big, KEYS), BF16),
            sds((big, pair), BF16),
        ),
        flops * 2,
        0,
        in_specs=[pl.BlockSpec(memory_space=pltpu.SMEM)]
        + [pl.BlockSpec(memory_space=pltpu.VMEM)] * (1 + len(packs)),
        scratch_shapes=[pltpu.VMEM((3 * pair, width), BF16), pltpu.VMEM((heads, 3 * THIRD, KEYS), F32)],
    )(place, first, *packs)


def middle_body(images, local, ctx_a, ctx_b, p0, p1, p2, p3, started, vec, branch_o, second_o, w_s):
    pair = 2 * local
    for at, part in enumerate((p0, p1, p2, p3)):
        w_s[at * local : (at + 1) * local, :] = part[part.shape[0] - local :, :]

    def image(i, carry):
        row = pl.multiple_of(i * PAD, 16)
        block = pl.ds(row, PAD)
        branch = (
            mm(ctx_a[block, :], w_s[0:pair, :])
            + mm(ctx_b[block, :], w_s[pair : 2 * pair, :])
            + vec[OUTPUT_BIAS : OUTPUT_BIAS + 1]
        )
        branch_o[block, :] = branch
        middle = started[block, :].astype(F32) + vec[ATT_SCALE : ATT_SCALE + 1] * branch
        normed, _ = norm_parts(middle)
        second_o[block, :] = (
            normed * vec[SECOND_GAIN : SECOND_GAIN + 1] + vec[SECOND_BIAS : SECOND_BIAS + 1]
        ).astype(BF16)
        return carry

    lax.fori_loop(0, images, image, 0)


def middle_stage(ctx_a, ctx_b, packs, started, vec, images, local):
    big, width = started.shape
    return call(
        functools.partial(middle_body, images, local),
        (
            sds((big, width), F32),
            sds((big, width), BF16),
        ),
        2 * big * width * width,
        big * width * 16,
        scratch_shapes=[pltpu.VMEM((4 * local, width), BF16)],
    )(ctx_a, ctx_b, *packs, started, vec)


def feed_body(count, near, place, second, fg, *refs):
    weights = refs[: 1 if near else count]
    feed_o, sg_o, grad_o, bias_o, wu_s, wd_s, act_s, pg_s = refs[len(weights) :]
    width = second.shape[1]
    side = place[0]
    blocks = [weights[0].at[at] for at in range(count)] if near else weights
    wholes = [slice(HID * at, HID * at + HID) for at in range(count)]
    for block, rows in zip(blocks, wholes):
        wu_s[rows, :] = block[0:HID, :]
        wd_s[rows, :] = block[HID : 2 * HID, :]
    sums = []
    for block, rows in zip(blocks, wholes):
        shift = block[2 * HID : 2 * HID + 16, 0:HID].astype(F32)[0:1]
        pre = mm(second[...], wu_s[rows, :], NT) + shift
        back = mm(fg[...], wd_s[rows, :], NT)
        cdf = 0.5 * (1.0 + lax.erf(pre * HALF_ROOT))
        act_s[:, rows] = (pre * cdf).astype(BF16)
        slope = cdf + pre * (jnp.exp(-0.5 * pre * pre) * DENSITY_FACTOR)
        pg = (back * slope).astype(BF16)
        pg_s[:, rows] = pg
        sums.append(colsum(pg.astype(F32)))
    for at in range(0, width, HID):
        lanes = slice(at, at + HID)
        feed_o[:, lanes] = mm(act_s[...], wd_s[:, lanes]).astype(BF16)
        sg_o[:, lanes] = mm(pg_s[...], wu_s[:, lanes]).astype(BF16)
    for at, rows in enumerate(wholes):
        if near or at == 0:
            spot = at
        else:
            spot = 1 + side if at == 1 else 2 - side
        target = pl.ds(pl.multiple_of(spot * HID, HID), HID)
        grad_o[side, target, :] = mm(pg_s[:, rows], second[...], TN).astype(BF16)
        grad_o[1 - side, target, :] = mm(act_s[:, rows], fg[...], TN).astype(BF16)
    if not near:
        sums = [
            sums[0],
            jnp.where(side == 0, sums[1], sums[2]),
            jnp.where(side == 0, sums[2], sums[1]),
        ]
    for rows, value in zip(wholes, sums):
        bias_o[:, rows] = jnp.broadcast_to(value, (8, HID))


def feed_stage(place, second, fg, weights, near):
    big, width = second.shape
    count = weights[0].shape[0] if near else len(weights)
    hidden = count * HID
    return call(
        functools.partial(feed_body, count, near),
        (
            sds((big, width), BF16),
            sds((big, width), BF16),
            sds((2, hidden, width), BF16),
            sds((8, hidden), F32),
        ),
        12 * big * width * hidden,
        0,
        in_specs=[pl.BlockSpec(memory_space=pltpu.SMEM)]
        + [pl.BlockSpec(memory_space=pltpu.VMEM)] * (2 + len(weights)),
        scratch_shapes=[
            pltpu.VMEM((hidden, width), BF16),
            pltpu.VMEM((hidden, width), BF16),
            pltpu.VMEM((big, hidden), BF16),
            pltpu.VMEM((big, hidden), BF16),
        ],
    )(place, second, fg, *weights)


def turn_body(images, parts, *refs):
    feeds = refs[0:parts]
    sgs = refs[parts : 2 * parts]
    started, branch, g, vec, out_o, mg_o, ag_o, sums_o, wide_s = refs[2 * parts :]
    width = branch.shape[1]
    sums_o[...] = jnp.zeros(sums_o.shape, F32)

    for i in range(images):
        block = slice(i * PAD, (i + 1) * PAD)
        feed = vec[DOWN_BIAS : DOWN_BIAS + 1]
        sg = jnp.zeros((PAD, width), F32)
        for at in range(parts):
            feed = feed + feeds[at][block, :].astype(F32)
            sg = sg + sgs[at][block, :].astype(F32)
        rows = g[block, :].astype(F32)
        mid = started[block, :].astype(F32) + vec[ATT_SCALE : ATT_SCALE + 1] * branch[block, :]
        out = mid + vec[FEED_SCALE : FEED_SCALE + 1] * feed
        wide_s[i * LEN : (i + 1) * LEN, :] = out[0:LEN]
        normed, inverse = norm_parts(mid)
        grad = rows + norm_back(sg, normed, inverse, vec[SECOND_GAIN : SECOND_GAIN + 1])
        mg_o[block, :] = grad
        att = (vec[ATT_SCALE : ATT_SCALE + 1] * grad).astype(BF16)
        ag_o[block, :] = att
        sums_o[0:1, :] += colsum(rows * feed)
        sums_o[1:2, :] += colsum(sg * normed)
        sums_o[2:3, :] += colsum(sg)
        sums_o[3:4, :] += colsum(grad * branch[block, :])
        sums_o[4:5, :] += colsum(att.astype(F32))
    out_o[...] = wide_s[0 : out_o.shape[0], :].astype(BF16)


def turn_stage(feeds, sgs, started, branch, g, vec, images):
    big, width = branch.shape
    rows = images * LEN
    return call(
        functools.partial(turn_body, images, len(feeds)),
        (sds((rows, width), BF16), sds((big, width), F32), sds((big, width), BF16), sds((8, width), F32)),
        40 * big * width,
        big * width * (18 + 4 * len(feeds)),
        scratch_shapes=[pltpu.VMEM((-(-rows // 8) * 8, width), F32)],
    )(*feeds, *sgs, started, branch, g, vec)


def attention_backward_body(images, local, near, place, first, ag, ctx, qkv, prob, *refs):
    packs = refs[: 2 if near else 6]
    out_a, out_b, up_a, up_b, grad_a, grad_b, fg_o, w_s, cg_s, tg_s, bias_s, wo_s = refs[len(packs) :]
    pair = 2 * local
    heads = local // HEAD_DIM
    big, width = first.shape
    score_scale = HEAD_DIM ** (-0.5)
    side = place[0]
    sides = (side, 1 - side)
    gather_weights(w_s, three(packs, near), near, side, local)
    wo_s[0:local, :] = out_a[out_a.shape[0] - local :, :]
    wo_s[local:pair, :] = out_b[out_b.shape[0] - local :, :]
    cg_s[0:big, :] = mm(ag[...], wo_s[...], NT).astype(BF16)
    d_out = mm(ctx[...], ag[...], TN).astype(BF16)
    grad_a[sides[1], local : 2 * local, :] = d_out[0:local]
    grad_b[sides[1], local : 2 * local, :] = d_out[local:pair]
    bias_s[...] = jnp.zeros(bias_s.shape, F32)
    lane = lax.broadcasted_iota(jnp.int32, (1, 128), 1)
    first_half = (lane < HEAD_DIM).astype(BF16)
    halves = (first_half, 1 - first_half)

    def image(i, carry):
        row = pl.multiple_of(i * PAD, 16)
        for tile in range(pair // 128):
            lanes = slice(128 * tile, 128 * tile + 128)
            q = qkv[0, pl.ds(row, PAD), lanes]
            k = qkv[1, pl.ds(row, KEYS), lanes]
            v = qkv[2, pl.ds(row, KEYS), lanes]
            do = cg_s[pl.ds(row, PAD), lanes]
            dq = dk = dv = None
            for half in range(2):
                head = 2 * tile + half
                p = prob[head, pl.ds(row, PAD), :]
                do_half = do * halves[half]
                dp = mm(do_half, v, NT)
                p32 = p.astype(F32)
                ds = p32 * (dp - jnp.sum(dp * p32, -1, keepdims=True))
                bias_s[head] += ds
                ds = ds.astype(BF16)
                dv_part = mm(p, do_half, TN)
                dk_part = mm(ds, q * halves[half], TN)
                dq_part = mm(ds, k * halves[half])
                dq = dq_part if dq is None else dq + dq_part
                dk = dk_part if dk is None else dk + dk_part
                dv = dv_part if dv is None else dv + dv_part
            block = pl.ds(row, PAD)
            tg_s[block, 128 * tile : 128 * tile + 128] = (dq * score_scale).astype(BF16)
            tg_s[block, pair + 128 * tile : pair + 128 * tile + 128] = (dk[0:PAD] * score_scale).astype(BF16)
            tg_s[block, 2 * pair + 128 * tile : 2 * pair + 128 * tile + 128] = dv[0:PAD].astype(BF16)
        return carry

    lax.fori_loop(0, images, image, 0)
    small = (2 * local + CUT, 2 * local + PAD - CUT)
    filler = jnp.zeros((1, width - local), F32)
    sums = []
    for t, (half, row) in enumerate(((0, 0), (0, local), (1, 0))):
        part = tg_s[:, t * pair : (t + 1) * pair]
        dw = mm(part, first[...], TN).astype(BF16)
        grad_a[sides[half], row : row + local, :] = dw[0:local]
        grad_b[sides[half], row : row + local, :] = dw[local:pair]
        sums.append(colsum(part.astype(F32)))
    for at, (grad, hidden_bias) in enumerate(((grad_a, up_a), (grad_b, up_b))):
        lanes = slice(at * local, (at + 1) * local)
        grad[sides[0], small[0] :, :] = jnp.concatenate(
            [
                jnp.concatenate([sums[0][:, lanes], filler], 1),
                hidden_bias[0:1, :],
                jnp.zeros((14, width), F32),
            ],
            0,
        ).astype(BF16)
        grad[sides[1], small[1] :, :] = jnp.concatenate(
            [jnp.concatenate([sums[2][:, lanes], filler], 1), jnp.zeros((31, width), F32)], 0
        ).astype(BF16)
        for h in range(heads):
            lanes = slice(h * KEYS, (h + 1) * KEYS)
            grad[sides[0], 2 * local : 2 * local + CUT, lanes] = bias_s[at * heads + h, 0:CUT].astype(BF16)
            grad[sides[1], 2 * local : 2 * local + PAD - CUT, lanes] = bias_s[
                at * heads + h, CUT:PAD
            ].astype(BF16)
    fg_o[...] = mm(tg_s[...], w_s[...]).astype(BF16)


def attention_backward(place, first, ag, forward, packs, near, outs, ups, images, local):
    qkv, prob, ctx = forward
    big, width = first.shape
    pair = 2 * local
    heads = pair // HEAD_DIM
    flops = 2 * big * (8 * width * pair + 8 * KEYS * HEAD_DIM * heads)
    pack = sds((2, 2 * local + CUT + 16, width), BF16)
    return call(
        functools.partial(attention_backward_body, images, local, near),
        (pack, pack, sds((big, width), BF16)),
        flops * 2,
        2 * big * (3 * width + 5 * pair + heads * KEYS),
        scratch_shapes=[
            pltpu.VMEM((3 * pair, width), BF16),
            pltpu.VMEM((big, pair), BF16),
            pltpu.VMEM((big, 3 * pair), BF16),
            pltpu.VMEM((heads, PAD, KEYS), F32),
            pltpu.VMEM((pair, width), BF16),
        ],
        in_specs=[pl.BlockSpec(memory_space=pltpu.SMEM)] + [pl.BlockSpec(memory_space=pltpu.VMEM)] * (9 + len(packs)),
    )(place, first, ag, ctx, qkv, prob, *packs, *outs, *ups)


def finish_body(images, fg_a, fg_b, mg, started, mask, vec, grad_o, sums_o, wide_s):
    width = mg.shape[1]
    rows = grad_o.shape[0]
    sums_o[...] = jnp.zeros(sums_o.shape, F32)
    for i in range(images):
        block = slice(i * PAD, (i + 1) * PAD)
        fgrad = fg_a[block, :].astype(F32) + fg_b[block, :].astype(F32)
        normed, inverse = norm_parts(started[block, :].astype(F32))
        total = mg[block, :] + norm_back(fgrad, normed, inverse, vec[FIRST_GAIN : FIRST_GAIN + 1])
        sums_o[0:1, :] += colsum(fgrad * normed)
        sums_o[1:2, :] += colsum(fgrad)
        wide_s[i * LEN : (i + 1) * LEN, :] = total[0:LEN]
    picked = mask[...] == 1.0
    for j in range(width // 128):
        lanes = slice(128 * j, 128 * j + 128)
        value = wide_s[0:rows, lanes]
        kept = jnp.where(picked, 0.0, value)
        grad_o[:, lanes] = kept
        sums_o[2:3, lanes] = colsum(value - kept)


def finish_stage(fg_a, fg_b, mg, started, mask_cols, vec, images):
    big, width = mg.shape
    rows = images * LEN
    return call(
        functools.partial(finish_body, images),
        (sds((rows, width), F32), sds((8, width), F32)),
        30 * big * width,
        big * width * 14,
        scratch_shapes=[pltpu.VMEM((-(-rows // 8) * 8, width), F32)],
    )(fg_a, fg_b, mg, started, mask_cols, vec)


def feed_final_body(place, piece, beyond, up_o, down_o):
    near = place[0] == 0
    up_o[...] = jnp.where(near, piece[...], beyond[...]).T.astype(F32)
    down_o[...] = jnp.where(near, beyond[...], piece[...]).astype(F32)


def feed_final(place, piece, beyond):
    hidden, width = piece.shape
    return call(
        feed_final_body,
        (sds((width, hidden), F32), sds((hidden, width), F32)),
        0,
        0,
        in_specs=[pl.BlockSpec(memory_space=pltpu.SMEM)] + [pl.BlockSpec(memory_space=pltpu.VMEM)] * 2,
    )(place, piece, beyond)


def attention_final_body(local, place, piece, beyond, qkv_o, out_o, table_o, query_o, value_o, hidden_o):
    near = place[0] == 0
    heads, length, _ = table_o.shape
    first = lambda rows: jnp.where(near, piece[rows, :], beyond[rows, :]).astype(F32)
    second = lambda rows: jnp.where(near, beyond[rows, :], piece[rows, :]).astype(F32)
    qkv_o[0] = first(slice(0, local))
    qkv_o[1] = first(slice(local, 2 * local))
    qkv_o[2] = second(slice(0, local))
    out_o[...] = second(slice(local, 2 * local))
    at = 2 * local
    top, low = first(slice(at, at + CUT)), second(slice(at, at + PAD - CUT))
    for h in range(heads):
        table_o[h, 0:CUT, :] = top[:, h * KEYS : h * KEYS + length]
        table_o[h, CUT:length, :] = low[0 : length - CUT, h * KEYS : h * KEYS + length]
    tile = first(slice(at + CUT, at + CUT + 16))
    query_o[...] = tile[0, 0:local]
    hidden_o[...] = tile[1, :]
    tile = second(slice(at + PAD - CUT, at + PAD - CUT + 16))
    value_o[...] = tile[0, 0:local]


def attention_final(place, piece, beyond, local, heads):
    width = piece.shape[1]
    return call(
        functools.partial(attention_final_body, local),
        (
            sds((3, local, width), F32),
            sds((local, width), F32),
            sds((heads, LEN, LEN), F32),
            sds((local,), F32),
            sds((local,), F32),
            sds((width,), F32),
        ),
        0,
        0,
        in_specs=[pl.BlockSpec(memory_space=pltpu.SMEM)] + [pl.BlockSpec(memory_space=pltpu.VMEM)] * 2,
    )(place, piece, beyond)


def flip(value, axis, size, bit):
    return lax.ppermute(value, axis, [(i, i ^ bit) for i in range(size)])


def gathered_body(count, place, *refs):
    *values, out = refs
    rows = out.shape[1]
    for at in range(count):
        block = pl.ds(pl.multiple_of(jnp.bitwise_xor(place[1], at) * rows, 8), rows)
        total = None
        for value in values:
            part = (value[block, :] if len(value.shape) == 2 else value[0, block, :]).astype(F32)
            total = part if total is None else total + part
        out[at] = total.astype(BF16)


def summed_pieces(place, values, count):
    rows, width = values[-1].shape
    specs = [
        pl.BlockSpec((1, rows, width), lambda i: (0, 0, 0))
        if len(v.shape) == 3
        else pl.BlockSpec((rows, width), lambda i: (0, 0))
        for v in values
    ]
    return call(
        functools.partial(gathered_body, count),
        sds((count, rows // count, width), BF16),
        2**39,
        0,
        grid=(1,),
        in_specs=[pl.BlockSpec(memory_space=pltpu.SMEM)] + specs,
        out_specs=pl.BlockSpec((count, rows // count, width), lambda i: (0, 0, 0)),
    )(place, *values)


def placed_body(place, *refs):
    *values, out = refs
    rows = values[0].shape[0]
    for at, value in enumerate(values):
        out[pl.ds(pl.multiple_of(jnp.bitwise_xor(place[1], at) * rows, 8), rows), :] = value[...]


def placed(place, values):
    rows, width = values[0].shape
    return call(
        placed_body,
        sds((rows * len(values), width), BF16),
        rows * width,
        4 * len(values) * rows * width,
        in_specs=[pl.BlockSpec(memory_space=pltpu.SMEM)]
        + [pl.BlockSpec(memory_space=pltpu.VMEM)] * len(values),
    )(place, *values)


def added(left, right):
    return (left.astype(F32) + right.astype(F32)).astype(BF16)


def total(values):
    return sum(v.astype(F32) for v in values).astype(BF16)


def after(values, *earlier):
    return lax.optimization_barrier((values, earlier))[0]


def sync(*values):
    return lax.optimization_barrier(values)


def wide_groups(wide, most):
    groups = []
    bit = 2
    while bit < wide:
        size = min(most, wide // bit)
        groups.append((bit, size))
        bit *= size
    return groups


def per_device(
    wide,
    narrow,
    tokens,
    patch_mask,
    cotangent,
    mask_token,
    first_gain,
    first_bias,
    qkv_weight,
    query_bias,
    value_bias,
    position_bias,
    output_weight,
    output_bias,
    attention_scale,
    second_gain,
    second_bias,
    up_weight,
    up_bias,
    down_weight,
    down_bias,
    feedforward_scale,
):
    rows, width = tokens.shape
    images = rows // LEN
    local = qkv_weight.shape[2]
    heads = local // HEAD_DIM
    core = functools.partial(flip, axis="narrow", size=narrow, bit=1)
    across = functools.partial(flip, axis="narrow", size=narrow, bit=2)
    beside = functools.partial(flip, axis="wide", size=wide, bit=1)

    def corner(value):
        pairs = [
            (w * narrow + n, (w ^ 1) * narrow + (n ^ 2)) for w in range(wide) for n in range(narrow)
        ]
        return lax.ppermute(value, ("wide", "narrow"), pairs)

    me = lax.axis_index("wide")
    side = me & 1
    feed_groups, att_groups = [
        [
            (bit, size, jnp.stack([side, (me // bit) & (size - 1)]).astype(jnp.int32))
            for bit, size in wide_groups(wide, most)
        ]
        for most in (2, 2)
    ]
    place = feed_groups[0][2]

    pack0, mine, direct = attention_rows(
        place, qkv_weight.transpose(1, 2, 0), position_bias, query_bias, value_bias, output_weight
    )
    pack_got2 = across(mine)
    pack_direct2 = across(direct)
    pack1 = core(pack0)
    out1 = core(output_weight)
    feed0, mine, direct = hidden_rows(place, up_weight, down_weight, up_bias)

    vectors = (
        mask_token,
        first_gain,
        first_bias,
        output_bias,
        attention_scale,
        second_gain,
        second_bias,
        down_bias,
        feedforward_scale,
    )
    mask_cols = jnp.broadcast_to(patch_mask.astype(F32)[:, None], (rows, 128))

    started, first, g, fg, sums_a, vec = prep(tokens, mask_cols, cotangent, vectors)
    first, pack_got2, pack1, mine, direct, feed0 = sync(first, pack_got2, pack1, mine, direct, feed0)
    pack_other2 = beside(pack_got2)
    pack_got3 = core(pack_got2)
    feed1 = core(feed0)
    att_a = attention_forward(place, first, (pack0, pack1), True, images, local)
    got2 = across(mine)
    att_a, pack_direct2, pack_other2, out1 = sync(att_a, pack_direct2, pack_other2, out1)
    pack_direct3 = core(pack_direct2)
    pack_other3 = core(pack_other2)
    far_packs = (pack_direct2, pack_got2, pack_other2, pack_direct3, pack_got3, pack_other3)
    att_b = attention_forward(place, first, far_packs, False, images, local)
    outs = (output_weight, out1, pack_direct2, pack_direct3)
    branch, second = middle_stage(att_a[2], att_b[2], outs, started, vec, images, local)
    second, feed1, got2 = sync(second, feed1, got2)
    direct2 = across(after(direct, got2))
    other2 = beside(got2)
    got3 = core(got2)
    feed_1, sg_1, d1, bias1 = feed_stage(place, second, fg, (feed1,), True)
    fg, d1 = sync(after(fg, feed_1), d1)
    from1 = core(d1)
    feed_0, sg_0, d0, bias0 = feed_stage(place, second, fg, (feed0,), True)
    fg, d0, direct2, other2, got3 = sync(after(fg, feed_0), d0, direct2, other2, got3)
    direct3 = core(direct2)
    other3 = core(other2)
    feed_2, sg_2, d2, bias2 = feed_stage(place, second, fg, (direct2, got2, other2), False)
    fg, d2, direct3, other3 = sync(after(fg, feed_2), d2, direct3, other3)
    feed_3, sg_3, d3, bias3 = feed_stage(place, second, fg, (direct3, got3, other3), False)
    g, d3 = sync(after(g, feed_3), d3)
    from3 = core(d3)
    layer_out, mg, ag, sums_b = turn_stage(
        (feed_0, feed_1, feed_2, feed_3), (sg_0, sg_1, sg_2, sg_3), started, branch, g, vec, images
    )
    ag, from3 = sync(ag, from3)
    far = [added(d2[at], from3[at]) for at in range(2)]
    ag, far, from1 = sync(ag, far, from1)
    got_y = across(far[0])
    got_d = corner(far[1])
    near1 = added(d0[1], from1[1])
    ag, near1 = sync(ag, near1)
    got_x = beside(near1)
    back_b = attention_backward(
        place, first, ag, att_b, far_packs, False, outs[2:], (bias2, bias3), images, local
    )
    ag, back_b = sync(ag, back_b)
    att_from3 = core(back_b[1])
    back_a = attention_backward(
        place, first, ag, att_a, (pack0, pack1), True, outs[:2], (bias0, bias1), images, local
    )
    grad0, grad1, fg_a = back_a
    grad2, _, fg_b = back_b
    att_from1 = core(grad1)
    input_grad, sums_c = finish_stage(fg_a, fg_b, mg, started, mask_cols, vec, images)

    def gradient_chain(groups, kept, coming, final):
        values = yield kept, coming
        for bit, size, spot in groups:
            pieces = summed_pieces(spot, values, size)
            values = yield pieces[0], [flip(pieces[at], "wide", wide, bit * at) for at in range(1, size)]
        piece = total(values)
        for bit, size, spot in groups[::-1]:
            values = yield piece, [flip(piece, "wide", wide, bit * at) for at in range(1, size)]
            piece = placed(spot, values)
        piece, beyond = yield piece, [beside(piece)]
        yield final(place, piece, beyond), []

    def vector_chain(vectors):
        for axis, size in (("narrow", narrow), ("wide", wide)):
            bit = 1
            while bit < size:
                vectors, partner = yield vectors, [flip(vectors, axis, size, bit)]
                vectors = vectors + partner
                bit *= 2
        yield vectors, []

    vectors = jnp.concatenate([sums_a[0:1], sums_b[0:5], sums_c[0:3], jnp.zeros((7, width), F32)], 0)
    chains = {
        "feed": gradient_chain(feed_groups, [d0, from1], [got_x, got_y, got_d], feed_final),
        "vectors": vector_chain(vectors),
    }
    live = {name: next(chain) for name, chain in chains.items()}

    def advance(name):
        kept, coming = live[name]
        if not coming:
            return
        others = {other: live[other][0] for other in live if other != name}
        kept, coming, others = sync(kept, coming, others)
        for other, value in others.items():
            live[other] = (value, live[other][1])
        live[name] = chains[name].send((list(kept) if isinstance(kept, (list, tuple)) else [kept]) + list(coming))

    stages = 2 * len(feed_groups), 2 * len(att_groups)
    advance("feed")
    kept, att_from3 = sync(live["feed"][0], att_from3)
    att_far = [added(grad2[at], att_from3[at]) for at in range(2)]
    kept, att_far, att_from1 = sync(kept, att_far, att_from1)
    live["feed"] = (kept, live["feed"][1])
    chains["att"] = gradient_chain(
        att_groups,
        [grad0, att_from1],
        [across(att_far[0]), corner(att_far[1]), beside(added(grad0[1], att_from1[1]))],
        functools.partial(attention_final, local=local, heads=heads),
    )
    live["att"] = next(chains["att"])
    order = ["vectors", "feed"] + ["vectors", "att", "feed"] * (stages[0] - 1)
    order += ["vectors", "att"] * (stages[1] + 1 - (stages[0] - 1)) + ["vectors"] * 8 + ["feed", "att"]
    for name in order:
        advance(name)

    dup, ddown = live["feed"][0]
    dqkv, dout, dpos, dquery, dvalue, dhidden = live["att"][0]
    vectors = live["vectors"][0]
    return (
        layer_out,
        input_grad,
        vectors[8],
        vectors[6],
        vectors[7],
        dqkv.transpose(2, 0, 1),
        dquery,
        dvalue,
        dpos,
        dout,
        vectors[5],
        vectors[4],
        vectors[2],
        vectors[3],
        dup,
        dhidden,
        ddown,
        vectors[0],
        vectors[1],
    )


def solution(mesh):
    rows = P(("wide", "narrow"), None)
    in_specs = (
        rows,
        P(("wide", "narrow")),
        rows,
        P(),
        P(),
        P(),
        P(None, None, "narrow"),
        P("narrow"),
        P("narrow"),
        P("narrow", None, None),
        P("narrow", None),
        P(),
        P(),
        P(),
        P(),
        P(None, "narrow"),
        P("narrow"),
        P("narrow", None),
        P(),
        P(),
    )
    out_specs = (
        rows,
        rows,
        P(),
        P(),
        P(),
        P(None, None, "narrow"),
        P("narrow"),
        P("narrow"),
        P("narrow", None, None),
        P("narrow", None),
        P(),
        P(),
        P(),
        P(),
        P(None, "narrow"),
        P("narrow"),
        P("narrow", None),
        P(),
        P(),
    )
    body = functools.partial(per_device, mesh.shape["wide"], mesh.shape["narrow"])
    return jax.shard_map(body, mesh=mesh, in_specs=in_specs, out_specs=out_specs, check_vma=False)
```

```python
import functools

import jax
import jax.numpy as jnp
from jax import lax
from jax.experimental import pallas as pl
from jax.experimental.pallas import tpu as pltpu
from jax.sharding import PartitionSpec as P

HEAD_DIM = 64
LEN = 197
PAD = 208
KEYS = 256
EPSILON = 1e-06
HALF_ROOT = 0.7071067811865476
DENSITY_FACTOR = 0.3989422804014327
FAR = -1e30
F32 = jnp.float32
BF16 = jnp.bfloat16
MIB = 1024 * 1024

(MASK_TOKEN, FIRST_GAIN, FIRST_BIAS, OUTPUT_BIAS, ATT_SCALE, SECOND_GAIN, SECOND_BIAS, DOWN_BIAS, FEED_SCALE) = range(9)

NT = (((1,), (1,)), ((), ()))
TN = (((0,), (0,)), ((), ()))
NN = (((1,), (0,)), ((), ()))


def mm(left, right, dims=NN):
    return lax.dot_general(left, right, dims, preferred_element_type=F32)


def call(body, out_shape, flops, bytes_accessed, trans=0, vmem=16, **kw):
    return pl.pallas_call(
        body,
        out_shape=out_shape,
        compiler_params=pltpu.CompilerParams(vmem_limit_bytes=vmem * MIB),
        cost_estimate=pl.CostEstimate(
            flops=int(flops) // 64, bytes_accessed=1024, transcendentals=0
        ),
        **kw,
    )


def sds(shape, dtype):
    return jax.ShapeDtypeStruct(shape, dtype)


def norm_parts(values):
    average = jnp.mean(values, -1, keepdims=True)
    centered = values - average
    inverse_dev = lax.rsqrt(jnp.mean(centered * centered, -1, keepdims=True) + EPSILON)
    return centered * inverse_dev, inverse_dev


def norm_back(grad_rows, normed, inverse_dev, gain):
    scaled = grad_rows * gain
    return inverse_dev * (
        scaled
        - jnp.mean(scaled, -1, keepdims=True)
        - normed * jnp.mean(scaled * normed, -1, keepdims=True)
    )


def colsum(values):
    return jnp.sum(values, 0, keepdims=True)


def prep_body(images, tok, mask, cot, *refs):
    *vectors, started_o, first_o, g_o, fg_o, sums_o, vec, wide_s, pad_s = refs
    vec[...] = jnp.zeros(vec.shape, F32)
    for at, vector in enumerate(vectors):
        vec[at : at + 1, :] = vector[...].astype(F32)[None]
    width = tok.shape[1]
    rows = tok.shape[0]
    picked = mask[...] == 1.0
    for j in range(width // 128):
        lanes = slice(128 * j, 128 * j + 128)
        wide_s[0:rows, lanes] = jnp.where(
            picked, vec[MASK_TOKEN : MASK_TOKEN + 1, lanes], tok[:, lanes].astype(F32)
        )
    for i in range(images):
        pad_s[0:LEN, :] = wide_s[i * LEN : (i + 1) * LEN, :]
        pad_s[LEN:PAD, :] = jnp.zeros((PAD - LEN, width), F32)
        values = pad_s[...]
        normed, _ = norm_parts(values)
        block = slice(i * PAD, (i + 1) * PAD)
        started_o[block, :] = values.astype(BF16)
        first_o[block, :] = (
            normed * vec[FIRST_GAIN : FIRST_GAIN + 1] + vec[FIRST_BIAS : FIRST_BIAS + 1]
        ).astype(BF16)
    wide_s[0:rows, :] = cot[...].astype(F32)
    total = jnp.zeros((1, width), F32)
    for i in range(images):
        pad_s[0:LEN, :] = wide_s[i * LEN : (i + 1) * LEN, :]
        values = pad_s[...]
        block = slice(i * PAD, (i + 1) * PAD)
        g_o[block, :] = values.astype(BF16)
        feed_grad = (values * vec[FEED_SCALE : FEED_SCALE + 1]).astype(BF16)
        fg_o[block, :] = feed_grad
        total += colsum(feed_grad.astype(F32))
    sums_o[0:1, :] = total
    sums_o[1:8, :] = jnp.zeros((7, width), F32)


def prep(tokens, mask_cols, cotangent, vectors):
    rows, width = tokens.shape
    images = rows // LEN
    big = images * PAD
    b = sds((big, width), BF16)
    return call(
        functools.partial(prep_body, images),
        (b, b, b, b, sds((8, width), F32), sds((16, width), F32)),
        10 * rows * width,
        6 * 2 * rows * width,
        scratch_shapes=[pltpu.VMEM((-(-rows // 8) * 8, width), F32), pltpu.VMEM((PAD, width), F32)],
    )(tokens, mask_cols, cotangent, *vectors)


THIRD = 80
CUT = 112
HID = 256


def three(refs, near):
    if near:
        return [[ref.at[at] for at in range(3)] for ref in refs]
    return [refs[0:3], refs[3:6]]


def spots_of(near, side):
    return (0, 1, 2) if near else (0, 1 + side, 2 - side)


def gather_weights(w_s, shards, near, side, local):
    for at, blocks in enumerate(shards):
        for block, spot in zip(blocks, spots_of(near, side)):
            row = spot * 2 * local + at * local
            row = row if near else pl.multiple_of(row, 64)
            w_s[pl.ds(row, local), :] = block[0:local, :]


def attention_rows_body(local, place, qkv, table, query_bias, value_bias, out, pack_o, mine_o, direct_o, table_s):
    heads, length, _ = table.shape
    width = qkv.shape[2]
    side = place[0]
    filler = jnp.zeros((1, width - local), F32)
    for h in range(heads):
        table_s[h] = jnp.full(table_s.shape[1:], FAR, F32)
        table_s[h, 0:length, 0:length] = table[h].astype(F32)

    def store(to, t):
        to[0:local, :] = qkv[t]
        rows = min(THIRD, PAD - t * THIRD)
        for h in range(heads):
            to[local : local + rows, h * KEYS : (h + 1) * KEYS] = table_s[
                h, t * THIRD : t * THIRD + rows, :
            ].astype(BF16)
        if rows < THIRD:
            tile = [
                jnp.concatenate([bias[...].astype(F32)[None], filler], 1)
                for bias in (query_bias, value_bias)
            ]
            tile.append(jnp.zeros((THIRD - rows - 2, width), F32))
            to[local + rows : local + THIRD, :] = jnp.concatenate(tile, 0).astype(BF16)

    for t in range(3):
        store(pack_o.at[t], t)
    store(direct_o, 0)
    direct_o[local + THIRD :, :] = out[...]
    for t in (1, 2):

        @pl.when(side == t - 1)
        def _():
            store(mine_o, t)


def attention_rows(place, qkv_rows, table, query_bias, value_bias, out):
    _, local, width = qkv_rows.shape
    block = (local + THIRD, width)
    return call(
        functools.partial(attention_rows_body, local),
        (sds((3,) + block, BF16), sds(block, BF16), sds((block[0] + local, width), BF16)),
        0,
        0,
        in_specs=[pl.BlockSpec(memory_space=pltpu.SMEM)] + [pl.BlockSpec(memory_space=pltpu.VMEM)] * 5,
        scratch_shapes=[pltpu.VMEM((table.shape[0], PAD, KEYS), F32)],
    )(place, qkv_rows, table, query_bias, value_bias, out)


def hidden_rows_body(place, up, down, bias, feed_o, mine_o, direct_o):
    count = feed_o.shape[0]
    width = up.shape[0]
    side = place[0]
    for at in range(count):
        hidden = slice(at * HID, (at + 1) * HID)
        out = feed_o.at[at]
        out[0:HID, :] = up[:, hidden].T
        out[HID : 2 * HID, :] = down[hidden, :]
        row = jnp.concatenate([bias[...].astype(F32)[None][:, hidden], jnp.zeros((1, width - HID), F32)], 1)
        out[2 * HID :, :] = jnp.concatenate([row, jnp.zeros((15, width), F32)], 0).astype(BF16)
    direct_o[...] = feed_o[0]
    mine_o[...] = feed_o[1 + side]


def hidden_rows(place, up, down, bias):
    width, hidden = up.shape
    block = (2 * HID + 16, width)
    return call(
        hidden_rows_body,
        (sds((hidden // HID,) + block, BF16), sds(block, BF16), sds(block, BF16)),
        0,
        0,
        in_specs=[pl.BlockSpec(memory_space=pltpu.SMEM)] + [pl.BlockSpec(memory_space=pltpu.VMEM)] * 3,
    )(place, up, down, bias)


def attention_forward_body(images, local, near, place, first, *refs):
    packs = refs[: 2 if near else 6]
    qkv_o, prob_o, ctx_o, w_s, bias_s = refs[len(packs) :]
    pair = 2 * local
    heads = local // HEAD_DIM
    big = images * PAD
    score_scale = HEAD_DIM ** (-0.5)
    side = place[0]
    shards = three(packs, near)
    gather_weights(w_s, shards, near, side, local)
    small = local + PAD - 2 * THIRD
    tiles = []
    for at, blocks in enumerate(shards):
        for block, spot in zip(blocks, spots_of(near, side)):
            row = spot * THIRD
            row = row if near else pl.multiple_of(row, 16)
            for h in range(heads):
                bias_s[at * heads + h, pl.ds(row, THIRD), :] = block[
                    local : local + THIRD, h * KEYS : (h + 1) * KEYS
                ].astype(F32)
        last = [block[small : small + 16, 0:local].astype(F32) for block in blocks[1:]]
        tiles.append(last[1] if near else jnp.where(side == 0, last[1], last[0]))
    shift = jnp.concatenate(tiles, 1)
    for t in range(3):
        value = mm(first[...], w_s[t * pair : (t + 1) * pair, :], NT)
        if t == 0:
            value = value + shift[0:1]
        if t == 2:
            value = value + shift[1:2]
        qkv_o[t, 0:big, :] = value.astype(BF16)
        qkv_o[t, big:, :] = jnp.zeros((KEYS - PAD, pair), BF16)
    lane = lax.broadcasted_iota(jnp.int32, (1, 128), 1)
    first_half = (lane < HEAD_DIM).astype(BF16)
    halves = (first_half, 1 - first_half)

    def image(i, carry):
        row = pl.multiple_of(i * PAD, 16)
        for tile in range(pair // 128):
            lanes = slice(128 * tile, 128 * tile + 128)
            q = qkv_o[0, pl.ds(row, PAD), lanes]
            k = qkv_o[1, pl.ds(row, KEYS), lanes]
            v = qkv_o[2, pl.ds(row, KEYS), lanes]
            context = None
            for half in range(2):
                head = 2 * tile + half
                scores = mm(q * halves[half], k, NT) * score_scale + bias_s[head, 0:PAD, :]
                top = jnp.max(scores, -1, keepdims=True)
                powers = jnp.exp(scores - top)
                share = 1.0 / jnp.sum(powers, -1, keepdims=True)
                probabilities = (powers * share).astype(BF16)
                prob_o[head, pl.ds(row, PAD), :] = probabilities
                part = mm(probabilities, v * halves[half])
                context = part if context is None else context + part
            ctx_o[pl.ds(row, PAD), lanes] = context.astype(BF16)
        return carry

    lax.fori_loop(0, images, image, 0)


def attention_forward(place, first, packs, near, images, local):
    big, width = first.shape
    pair = 2 * local
    heads = pair // HEAD_DIM
    flops = 2 * big * (width * 3 * pair + 2 * KEYS * HEAD_DIM * heads)
    return call(
        functools.partial(attention_forward_body, images, local, near),
        (
            sds((3, big + KEYS - PAD, pair), BF16),
            sds((heads, big, KEYS), BF16),
            sds((big, pair), BF16),
        ),
        flops * 2,
        0,
        in_specs=[pl.BlockSpec(memory_space=pltpu.SMEM)]
        + [pl.BlockSpec(memory_space=pltpu.VMEM)] * (1 + len(packs)),
        scratch_shapes=[pltpu.VMEM((3 * pair, width), BF16), pltpu.VMEM((heads, 3 * THIRD, KEYS), F32)],
    )(place, first, *packs)


def middle_body(images, local, ctx_a, ctx_b, p0, p1, p2, p3, started, vec, branch_o, second_o, w_s):
    pair = 2 * local
    for at, part in enumerate((p0, p1, p2, p3)):
        w_s[at * local : (at + 1) * local, :] = part[part.shape[0] - local :, :]

    def image(i, carry):
        row = pl.multiple_of(i * PAD, 16)
        block = pl.ds(row, PAD)
        branch = (
            mm(ctx_a[block, :], w_s[0:pair, :])
            + mm(ctx_b[block, :], w_s[pair : 2 * pair, :])
            + vec[OUTPUT_BIAS : OUTPUT_BIAS + 1]
        )
        branch_o[block, :] = branch
        middle = started[block, :].astype(F32) + vec[ATT_SCALE : ATT_SCALE + 1] * branch
        normed, _ = norm_parts(middle)
        second_o[block, :] = (
            normed * vec[SECOND_GAIN : SECOND_GAIN + 1] + vec[SECOND_BIAS : SECOND_BIAS + 1]
        ).astype(BF16)
        return carry

    lax.fori_loop(0, images, image, 0)


def middle_stage(ctx_a, ctx_b, packs, started, vec, images, local):
    big, width = started.shape
    return call(
        functools.partial(middle_body, images, local),
        (
            sds((big, width), F32),
            sds((big, width), BF16),
        ),
        2 * big * width * width,
        big * width * 16,
        scratch_shapes=[pltpu.VMEM((4 * local, width), BF16)],
    )(ctx_a, ctx_b, *packs, started, vec)


def feed_body(groups, near, cut, place, second, fg, *refs):
    count = sum(groups)
    weights = refs[: 1 if near else count]
    feed_o, sg_o, *refs = refs[len(weights) :]
    parts = 2 * groups[0] if cut else 0
    pieces, refs = refs[:parts], refs[parts:]
    grads, refs = refs[: len(groups) - bool(cut)], refs[len(groups) - bool(cut) :]
    biases, refs = refs[: len(groups)], refs[len(groups) :]
    wu_s, wd_s, act_s, pg_s, *whole_s = refs
    grads = [*whole_s, *grads]
    width = second.shape[1]
    side = place[0]
    blocks = [weights[0].at[at] for at in range(count)] if near else weights
    wholes = [slice(HID * at, HID * at + HID) for at in range(count)]
    for block, rows in zip(blocks, wholes):
        wu_s[rows, :] = block[0:HID, :]
        wd_s[rows, :] = block[HID : 2 * HID, :]
    sums = []
    for block, rows in zip(blocks, wholes):
        shift = block[2 * HID : 2 * HID + 16, 0:HID].astype(F32)[0:1]
        pre = mm(second[...], wu_s[rows, :], NT) + shift
        back = mm(fg[...], wd_s[rows, :], NT)
        cdf = 0.5 * (1.0 + lax.erf(pre * HALF_ROOT))
        act_s[:, rows] = (pre * cdf).astype(BF16)
        slope = cdf + pre * (jnp.exp(-0.5 * pre * pre) * DENSITY_FACTOR)
        pg = (back * slope).astype(BF16)
        pg_s[:, rows] = pg
        sums.append(colsum(pg.astype(F32)))
    for at in range(0, width, HID):
        lanes = slice(at, at + HID)
        feed_o[:, lanes] = mm(act_s[...], wd_s[:, lanes]).astype(BF16)
        sg_o[:, lanes] = mm(pg_s[...], wu_s[:, lanes]).astype(BF16)
    at = 0
    for grad, bias, group in zip(grads, biases, groups):
        for local in range(group):
            target = slice(HID * local, HID * local + HID)
            grad[side, target, :] = mm(pg_s[:, wholes[at]], second[...], TN).astype(BF16)
            grad[1 - side, target, :] = mm(act_s[:, wholes[at]], fg[...], TN).astype(BF16)
            bias[:, target] = jnp.broadcast_to(sums[at], (8, HID))
            at += 1
    for at, piece in enumerate(pieces):
        block = at % groups[0]
        piece[...] = grads[0][at // groups[0], block * HID : (block + 1) * HID, :]


def feed_stage(place, second, fg, weights, groups, near, cut=False):
    big, width = second.shape
    hidden = sum(groups) * HID
    return call(
        functools.partial(feed_body, groups, near, cut),
        (
            sds((big, width), BF16),
            sds((big, width), BF16),
            *[sds((HID, width), BF16)] * (2 * groups[0] if cut else 0),
            *[sds((2, group * HID, width), BF16) for group in groups[cut:]],
            *[sds((8, group * HID), F32) for group in groups],
        ),
        12 * big * width * hidden,
        0,
        in_specs=[pl.BlockSpec(memory_space=pltpu.SMEM)]
        + [pl.BlockSpec(memory_space=pltpu.VMEM)] * (2 + len(weights)),
        scratch_shapes=[
            pltpu.VMEM((hidden, width), BF16),
            pltpu.VMEM((hidden, width), BF16),
            pltpu.VMEM((big, hidden), BF16),
            pltpu.VMEM((big, hidden), BF16),
        ]
        + ([pltpu.VMEM((2, groups[0] * HID, width), BF16)] if cut else []),
    )(place, second, fg, *weights)


def turn_body(images, parts, *refs):
    feeds = refs[0:parts]
    sgs = refs[parts : 2 * parts]
    started, branch, g, vec, out_o, mg_o, ag_o, sums_o, wide_s = refs[2 * parts :]
    width = branch.shape[1]
    sums_o[...] = jnp.zeros(sums_o.shape, F32)

    for i in range(images):
        block = slice(i * PAD, (i + 1) * PAD)
        feed = vec[DOWN_BIAS : DOWN_BIAS + 1]
        sg = jnp.zeros((PAD, width), F32)
        for at in range(parts):
            feed = feed + feeds[at][block, :].astype(F32)
            sg = sg + sgs[at][block, :].astype(F32)
        rows = g[block, :].astype(F32)
        mid = started[block, :].astype(F32) + vec[ATT_SCALE : ATT_SCALE + 1] * branch[block, :]
        out = mid + vec[FEED_SCALE : FEED_SCALE + 1] * feed
        wide_s[i * LEN : (i + 1) * LEN, :] = out[0:LEN]
        normed, inverse = norm_parts(mid)
        grad = rows + norm_back(sg, normed, inverse, vec[SECOND_GAIN : SECOND_GAIN + 1])
        mg_o[block, :] = grad
        att = (vec[ATT_SCALE : ATT_SCALE + 1] * grad).astype(BF16)
        ag_o[block, :] = att
        sums_o[0:1, :] += colsum(rows * feed)
        sums_o[1:2, :] += colsum(sg * normed)
        sums_o[2:3, :] += colsum(sg)
        sums_o[3:4, :] += colsum(grad * branch[block, :])
        sums_o[4:5, :] += colsum(att.astype(F32))
    out_o[...] = wide_s[0 : out_o.shape[0], :].astype(BF16)


def turn_stage(feeds, sgs, started, branch, g, vec, images):
    big, width = branch.shape
    rows = images * LEN
    return call(
        functools.partial(turn_body, images, len(feeds)),
        (sds((rows, width), BF16), sds((big, width), F32), sds((big, width), BF16), sds((8, width), F32)),
        40 * big * width,
        big * width * (18 + 4 * len(feeds)),
        scratch_shapes=[pltpu.VMEM((-(-rows // 8) * 8, width), F32)],
    )(*feeds, *sgs, started, branch, g, vec)


def attention_backward_body(images, local, near, place, first, ag, ctx, qkv, prob, *refs):
    packs = refs[: 2 if near else 6]
    out_a, out_b, *refs = refs[len(packs) :]
    if near:
        (up_a, up_b), refs = [ref[0:1, :] for ref in refs[:2]], refs[2:]
    else:
        ups = []
        for shared, rest in (refs[0:2], refs[2:4]):
            shared, short, other = shared[0:1, :], rest[0:1, 0:HID], rest[0:1, HID:]
            low = jnp.where(place[0] == 0, shared, other)
            ups.append(jnp.concatenate([short, low, jnp.where(place[0] == 0, other, shared)], 1))
        (up_a, up_b), refs = ups, refs[4:]
    grad_a, *refs = refs
    parts, (fg_o, w_s, cg_s, tg_s, bias_s, wo_s, *grad_b) = (refs[:1], refs[1:]) if near else (refs[:2], refs[2:])
    grad_b = parts[0] if near else grad_b[0]
    pair = 2 * local
    heads = local // HEAD_DIM
    big, width = first.shape
    score_scale = HEAD_DIM ** (-0.5)
    side = place[0]
    sides = (side, 1 - side)
    gather_weights(w_s, three(packs, near), near, side, local)
    wo_s[0:local, :] = out_a[out_a.shape[0] - local :, :]
    wo_s[local:pair, :] = out_b[out_b.shape[0] - local :, :]
    cg_s[0:big, :] = mm(ag[...], wo_s[...], NT).astype(BF16)
    d_out = mm(ctx[...], ag[...], TN).astype(BF16)
    grad_a[sides[1], local : 2 * local, :] = d_out[0:local]
    grad_b[sides[1], local : 2 * local, :] = d_out[local:pair]
    bias_s[...] = jnp.zeros(bias_s.shape, F32)
    lane = lax.broadcasted_iota(jnp.int32, (1, 128), 1)
    first_half = (lane < HEAD_DIM).astype(BF16)
    halves = (first_half, 1 - first_half)

    def image(i, carry):
        row = pl.multiple_of(i * PAD, 16)
        for tile in range(pair // 128):
            lanes = slice(128 * tile, 128 * tile + 128)
            q = qkv[0, pl.ds(row, PAD), lanes]
            k = qkv[1, pl.ds(row, KEYS), lanes]
            v = qkv[2, pl.ds(row, KEYS), lanes]
            do = cg_s[pl.ds(row, PAD), lanes]
            dq = dk = dv = None
            for half in range(2):
                head = 2 * tile + half
                p = prob[head, pl.ds(row, PAD), :]
                do_half = do * halves[half]
                dp = mm(do_half, v, NT)
                p32 = p.astype(F32)
                ds = p32 * (dp - jnp.sum(dp * p32, -1, keepdims=True))
                bias_s[head] += ds
                ds = ds.astype(BF16)
                dv_part = mm(p, do_half, TN)
                dk_part = mm(ds, q * halves[half], TN)
                dq_part = mm(ds, k * halves[half])
                dq = dq_part if dq is None else dq + dq_part
                dk = dk_part if dk is None else dk + dk_part
                dv = dv_part if dv is None else dv + dv_part
            block = pl.ds(row, PAD)
            tg_s[block, 128 * tile : 128 * tile + 128] = (dq * score_scale).astype(BF16)
            tg_s[block, pair + 128 * tile : pair + 128 * tile + 128] = (dk[0:PAD] * score_scale).astype(BF16)
            tg_s[block, 2 * pair + 128 * tile : 2 * pair + 128 * tile + 128] = dv[0:PAD].astype(BF16)
        return carry

    lax.fori_loop(0, images, image, 0)
    small = (2 * local + CUT, 2 * local + PAD - CUT)
    filler = jnp.zeros((1, width - local), F32)
    sums = []
    for t, (half, row) in enumerate(((0, 0), (0, local), (1, 0))):
        part = tg_s[:, t * pair : (t + 1) * pair]
        dw = mm(part, first[...], TN).astype(BF16)
        grad_a[sides[half], row : row + local, :] = dw[0:local]
        grad_b[sides[half], row : row + local, :] = dw[local:pair]
        sums.append(colsum(part.astype(F32)))
    for at, (grad, hidden_bias) in enumerate(((grad_a, up_a), (grad_b, up_b))):
        lanes = slice(at * local, (at + 1) * local)
        grad[sides[0], small[0] :, :] = jnp.concatenate(
            [
                jnp.concatenate([sums[0][:, lanes], filler], 1),
                hidden_bias,
                jnp.zeros((14, width), F32),
            ],
            0,
        ).astype(BF16)
        grad[sides[1], small[1] :, :] = jnp.concatenate(
            [jnp.concatenate([sums[2][:, lanes], filler], 1), jnp.zeros((31, width), F32)], 0
        ).astype(BF16)
        for h in range(heads):
            lanes = slice(h * KEYS, (h + 1) * KEYS)
            grad[sides[0], 2 * local : 2 * local + CUT, lanes] = bias_s[at * heads + h, 0:CUT].astype(BF16)
            grad[sides[1], 2 * local : 2 * local + PAD - CUT, lanes] = bias_s[
                at * heads + h, CUT:PAD
            ].astype(BF16)
    fg_o[...] = mm(tg_s[...], w_s[...]).astype(BF16)
    if not near:
        for at, to in enumerate(parts):
            to[...] = grad_b[at]


def attention_backward(place, first, ag, forward, packs, near, outs, ups, images, local):
    qkv, prob, ctx = forward
    big, width = first.shape
    pair = 2 * local
    heads = pair // HEAD_DIM
    flops = 2 * big * (8 * width * pair + 8 * KEYS * HEAD_DIM * heads)
    half = 2 * local + CUT + 16
    pack = sds((2, half, width), BF16)
    piece = sds((half, width), BF16)
    return call(
        functools.partial(attention_backward_body, images, local, near),
        (pack,) + ((pack,) if near else (piece,) * 2) + (sds((big, width), BF16),),
        flops * 2,
        2 * big * (3 * width + 5 * pair + heads * KEYS),
        scratch_shapes=[
            pltpu.VMEM((3 * pair, width), BF16),
            pltpu.VMEM((big, pair), BF16),
            pltpu.VMEM((big, 3 * pair), BF16),
            pltpu.VMEM((heads, PAD, KEYS), F32),
            pltpu.VMEM((pair, width), BF16),
        ]
        + ([] if near else [pltpu.VMEM((2, half, width), BF16)]),
        in_specs=[pl.BlockSpec(memory_space=pltpu.SMEM)] + [pl.BlockSpec(memory_space=pltpu.VMEM)] * (7 + len(packs) + len(ups)),
    )(place, first, ag, ctx, qkv, prob, *packs, *outs, *ups)


def finish_body(images, fg_a, fg_b, mg, started, mask, vec, grad_o, sums_o, wide_s):
    width = mg.shape[1]
    rows = grad_o.shape[0]
    sums_o[...] = jnp.zeros(sums_o.shape, F32)
    for i in range(images):
        block = slice(i * PAD, (i + 1) * PAD)
        fgrad = fg_a[block, :].astype(F32) + fg_b[block, :].astype(F32)
        normed, inverse = norm_parts(started[block, :].astype(F32))
        total = mg[block, :] + norm_back(fgrad, normed, inverse, vec[FIRST_GAIN : FIRST_GAIN + 1])
        sums_o[0:1, :] += colsum(fgrad * normed)
        sums_o[1:2, :] += colsum(fgrad)
        wide_s[i * LEN : (i + 1) * LEN, :] = total[0:LEN]
    picked = mask[...] == 1.0
    for j in range(width // 128):
        lanes = slice(128 * j, 128 * j + 128)
        value = wide_s[0:rows, lanes]
        kept = jnp.where(picked, 0.0, value)
        grad_o[:, lanes] = kept
        sums_o[2:3, lanes] = colsum(value - kept)


def finish_stage(fg_a, fg_b, mg, started, mask_cols, vec, images):
    big, width = mg.shape
    rows = images * LEN
    return call(
        functools.partial(finish_body, images),
        (sds((rows, width), F32), sds((8, width), F32)),
        30 * big * width,
        big * width * 14,
        scratch_shapes=[pltpu.VMEM((-(-rows // 8) * 8, width), F32)],
    )(fg_a, fg_b, mg, started, mask_cols, vec)


def feed_final_body(place, piece, beyond, up_o, down_o):
    near = place[0] == 0
    up_o[...] = jnp.where(near, piece[...], beyond[...]).T.astype(F32)
    down_o[...] = jnp.where(near, beyond[...], piece[...]).astype(F32)


def feed_final(place, piece, beyond):
    hidden, width = piece.shape
    return call(
        feed_final_body,
        (sds((width, hidden), F32), sds((hidden, width), F32)),
        0,
        0,
        in_specs=[pl.BlockSpec(memory_space=pltpu.SMEM)] + [pl.BlockSpec(memory_space=pltpu.VMEM)] * 2,
    )(place, piece, beyond)


def attention_final_body(local, place, piece, beyond, qkv_o, out_o, table_o, query_o, value_o, hidden_o):
    near = place[0] == 0
    heads, length, _ = table_o.shape
    first = lambda rows: jnp.where(near, piece[rows, :], beyond[rows, :]).astype(F32)
    second = lambda rows: jnp.where(near, beyond[rows, :], piece[rows, :]).astype(F32)
    qkv_o[0] = first(slice(0, local))
    qkv_o[1] = first(slice(local, 2 * local))
    qkv_o[2] = second(slice(0, local))
    out_o[...] = second(slice(local, 2 * local))
    at = 2 * local
    top, low = first(slice(at, at + CUT)), second(slice(at, at + PAD - CUT))
    for h in range(heads):
        table_o[h, 0:CUT, :] = top[:, h * KEYS : h * KEYS + length]
        table_o[h, CUT:length, :] = low[0 : length - CUT, h * KEYS : h * KEYS + length]
    tile = first(slice(at + CUT, at + CUT + 16))
    query_o[...] = tile[0, 0:local]
    hidden_o[...] = tile[1, :]
    tile = second(slice(at + PAD - CUT, at + PAD - CUT + 16))
    value_o[...] = tile[0, 0:local]


def attention_final(place, piece, beyond, local, heads):
    width = piece.shape[1]
    return call(
        functools.partial(attention_final_body, local),
        (
            sds((3, local, width), F32),
            sds((local, width), F32),
            sds((heads, LEN, LEN), F32),
            sds((local,), F32),
            sds((local,), F32),
            sds((width,), F32),
        ),
        0,
        0,
        in_specs=[pl.BlockSpec(memory_space=pltpu.SMEM)] + [pl.BlockSpec(memory_space=pltpu.VMEM)] * 2,
    )(place, piece, beyond)


def flip(value, axis, size, bit):
    return lax.ppermute(value, axis, [(i, i ^ bit) for i in range(size)])


def gathered_body(count, place, *refs):
    *values, out = refs
    rows = out.shape[1]
    for at in range(count):
        block = pl.ds(pl.multiple_of(jnp.bitwise_xor(place[1], at) * rows, 16 if rows % 16 == 0 else 8), rows)
        total = None
        for value in values:
            part = (value[block, :] if len(value.shape) == 2 else value[0, block, :]).astype(F32)
            total = part if total is None else total + part
        out[at] = total.astype(BF16)


def summed_pieces(place, values, count):
    rows, width = values[-1].shape
    specs = [
        pl.BlockSpec((1, rows, width), lambda i: (0, 0, 0))
        if len(v.shape) == 3
        else pl.BlockSpec((rows, width), lambda i: (0, 0))
        for v in values
    ]
    return call(
        functools.partial(gathered_body, count),
        sds((count, rows // count, width), BF16),
        0,
        0,
        grid=(1,),
        in_specs=[pl.BlockSpec(memory_space=pltpu.SMEM)] + specs,
        out_specs=pl.BlockSpec((count, rows // count, width), lambda i: (0, 0, 0)),
    )(place, *values)


def feed_merged_body(count, place, near_a, near_b, got_x, y_shared, d_shared, y_rest, d_rest, out, sum_s):
    side = place[0]
    sum_s[...] = near_a[0].astype(F32) + near_b[0].astype(F32) + got_x[...].astype(F32)
    ours = pl.ds(pl.multiple_of((1 + side) * HID, HID), HID)
    theirs = pl.ds(pl.multiple_of((2 - side) * HID, HID), HID)
    sum_s[0:HID, :] += y_rest[0:HID, :].astype(F32) + d_rest[0:HID, :].astype(F32)
    sum_s[ours, :] += y_shared[...].astype(F32) + d_rest[HID:, :].astype(F32)
    sum_s[theirs, :] += d_shared[...].astype(F32) + y_rest[HID:, :].astype(F32)
    rows = out.shape[1]
    for at in range(count):
        block = pl.ds(pl.multiple_of(jnp.bitwise_xor(place[1], at) * rows, 8), rows)
        out[at] = sum_s[block, :].astype(BF16)


def feed_merged(place, values, count):
    rows, width = values[2].shape
    near = pl.BlockSpec((1, rows, width), lambda i: (0, 0, 0))
    flat = [pl.BlockSpec(v.shape, lambda i: (0, 0)) for v in values[2:]]
    return call(
        functools.partial(feed_merged_body, count),
        sds((count, rows // count, width), BF16),
        0,
        0,
        grid=(1,),
        in_specs=[pl.BlockSpec(memory_space=pltpu.SMEM), near, near] + flat,
        out_specs=pl.BlockSpec((count, rows // count, width), lambda i: (0, 0, 0)),
        scratch_shapes=[pltpu.VMEM((rows, width), F32)],
    )(place, *values)


def placed_body(place, *refs):
    *values, out = refs
    rows = values[0].shape[0]
    for at, value in enumerate(values):
        out[pl.ds(pl.multiple_of(jnp.bitwise_xor(place[1], at) * rows, 16 if rows % 16 == 0 else 8), rows), :] = value[...]


def placed(place, values):
    rows, width = values[0].shape
    return call(
        placed_body,
        sds((rows * len(values), width), BF16),
        rows * width,
        4 * len(values) * rows * width,
        in_specs=[pl.BlockSpec(memory_space=pltpu.SMEM)]
        + [pl.BlockSpec(memory_space=pltpu.VMEM)] * len(values),
    )(place, *values)


def added(left, right):
    return (left.astype(F32) + right.astype(F32)).astype(BF16)


def total(values):
    return sum(v.astype(F32) for v in values).astype(BF16)


def joined(parts, half):
    return jnp.concatenate(parts[2 * half : 2 * half + 2], 0)


def after(values, *earlier):
    return lax.optimization_barrier((values, earlier))[0]


def sync(*values):
    return lax.optimization_barrier(values)


def wide_groups(wide, most):
    groups = []
    bit = 2
    while bit < wide:
        size = min(most, wide // bit)
        groups.append((bit, size))
        bit *= size
    return groups


def per_device(
    wide,
    narrow,
    tokens,
    patch_mask,
    cotangent,
    mask_token,
    first_gain,
    first_bias,
    qkv_weight,
    query_bias,
    value_bias,
    position_bias,
    output_weight,
    output_bias,
    attention_scale,
    second_gain,
    second_bias,
    up_weight,
    up_bias,
    down_weight,
    down_bias,
    feedforward_scale,
):
    rows, width = tokens.shape
    images = rows // LEN
    local = qkv_weight.shape[2]
    heads = local // HEAD_DIM
    core = functools.partial(flip, axis="narrow", size=narrow, bit=1)
    across = functools.partial(flip, axis="narrow", size=narrow, bit=2)
    beside = functools.partial(flip, axis="wide", size=wide, bit=1)

    def corner(value):
        pairs = [
            (w * narrow + n, (w ^ 1) * narrow + (n ^ 2)) for w in range(wide) for n in range(narrow)
        ]
        return lax.ppermute(value, ("wide", "narrow"), pairs)

    me = lax.axis_index("wide")
    side = me & 1
    feed_groups, att_groups = [
        [
            (bit, size, jnp.stack([side, (me // bit) & (size - 1)]).astype(jnp.int32))
            for bit, size in wide_groups(wide, most)
        ]
        for most in (2, 2)
    ]
    place = feed_groups[0][2]

    count = up_weight.shape[1] // HID
    pack0, mine, direct = attention_rows(
        place, qkv_weight.transpose(1, 2, 0), position_bias, query_bias, value_bias, output_weight
    )
    pack_got2 = across(mine)
    pack_direct2 = across(direct)
    pack1 = core(pack0)
    out1 = core(output_weight)
    feed0, mine, direct = hidden_rows(place, up_weight, down_weight, up_bias)

    vectors = (
        mask_token,
        first_gain,
        first_bias,
        output_bias,
        attention_scale,
        second_gain,
        second_bias,
        down_bias,
        feedforward_scale,
    )
    mask_cols = jnp.broadcast_to(patch_mask.astype(F32)[:, None], (rows, 128))

    started, first, g, fg, sums_a, vec = prep(tokens, mask_cols, cotangent, vectors)
    first, pack_got2, pack1, mine, direct, feed0 = sync(first, pack_got2, pack1, mine, direct, feed0)
    pack_other2 = beside(pack_got2)
    pack_got3 = core(pack_got2)
    feed1 = core(feed0)
    att_a = attention_forward(place, first, (pack0, pack1), True, images, local)
    got2 = across(mine)
    att_a, pack_direct2, pack_other2, out1 = sync(att_a, pack_direct2, pack_other2, out1)
    pack_direct3 = core(pack_direct2)
    pack_other3 = core(pack_other2)
    far_packs = (pack_direct2, pack_got2, pack_other2, pack_direct3, pack_got3, pack_other3)
    att_b = attention_forward(place, first, far_packs, False, images, local)
    outs = (output_weight, out1, pack_direct2, pack_direct3)
    branch, second = middle_stage(att_a[2], att_b[2], outs, started, vec, images, local)
    second, feed1, got2 = sync(second, feed1, got2)
    direct2 = across(after(direct, got2))
    other2 = beside(got2)
    got3 = core(got2)
    second, got3 = sync(second, got3)
    feed_s, sg_s, *g3, g2, bias3s, bias2s = feed_stage(
        place, second, fg, (got3, got2), (1, 1), False, True
    )
    fg, g3 = sync(after(fg, feed_s), g3)
    from3s = [core(part) for part in g3]
    feed_1, sg_1, d1, bias1 = feed_stage(place, second, fg, (feed1,), (count,), True)
    fg, from3s = sync(after(fg, feed_1), from3s)
    far = [added(g2[at], from3s[at]) for at in range(2)]
    fg, far = sync(fg, far)
    y_shared = across(far[0])
    d_shared = corner(far[1])
    feed_0, sg_0, d0, bias0 = feed_stage(place, second, fg, (feed0,), (count,), True)
    fg, d0, d1, direct2, other2 = sync(after(fg, feed_0), d0, d1, direct2, other2)
    direct3 = core(direct2)
    other3 = core(other2)
    fg, direct3, other3 = sync(fg, direct3, other3)
    from1 = core(after(d1, direct3))
    feed_3, sg_3, *d3, bias3 = feed_stage(
        place, second, fg, (direct3, other3), (count - 1,), False, True
    )
    fg, d3 = sync(after(fg, feed_3), d3)
    from3 = [core(part) for part in d3]
    near1 = added(d0[1], after(from1, d3)[1])
    fg, near1 = sync(fg, near1)
    got_x = beside(near1)
    feed_2, sg_2, d2, bias2 = feed_stage(place, second, fg, (direct2, other2), (count - 1,), False)
    d2, y_shared, d_shared = sync(d2, y_shared, d_shared)
    d2, from3 = sync(d2, from3)
    far = [added(d2[at], joined(from3, at)) for at in range(2)]
    g, far = sync(g, far)
    y_rest = across(far[0])
    d_rest = corner(far[1])
    layer_out, mg, ag, sums_b = turn_stage(
        (feed_0, feed_1, feed_2, feed_3, feed_s),
        (sg_0, sg_1, sg_2, sg_3, sg_s),
        started,
        branch,
        g,
        vec,
        images,
    )
    back_b = attention_backward(
        place, first, ag, att_b, far_packs, False, outs[2:], (bias2s, bias2, bias3s, bias3), images, local
    )
    ag, back_b, got_x = sync(ag, back_b, got_x)
    att_from3 = [core(part) for part in back_b[1:3]]
    back_a = attention_backward(
        place, first, ag, att_a, (pack0, pack1), True, outs[:2], (bias0, bias1), images, local
    )
    grad0, fg_a = back_a[0], back_a[2]
    grad2, fg_b = back_b[0], back_b[3]

    def gradient_chain(groups, kept, coming, final, merged=summed_pieces):
        values = yield kept, coming
        for bit, size, spot in groups:
            pieces = merged(spot, values, size)
            merged = summed_pieces
            values = yield pieces[0], [flip(pieces[at], "wide", wide, bit * at) for at in range(1, size)]
        piece = total(values)
        for bit, size, spot in groups[::-1]:
            values = yield piece, [flip(piece, "wide", wide, bit * at) for at in range(1, size)]
            piece = placed(spot, values)
        piece, beyond = yield piece, [beside(piece)]
        yield final(place, piece, beyond), []

    def vector_chain(vectors):
        for axis, size in (("narrow", narrow), ("wide", wide)):
            bit = 1
            while bit < size:
                vectors, partner = yield vectors, [flip(vectors, axis, size, bit)]
                vectors = vectors + partner
                bit *= 2
        yield vectors, []

    chains = {
        "feed": gradient_chain(
            feed_groups,
            [d0, from1, got_x, y_shared, d_shared],
            [y_rest, d_rest],
            feed_final,
            feed_merged,
        ),
    }
    live = {name: next(chain) for name, chain in chains.items()}

    def advance(name):
        kept, coming = live[name]
        if not coming:
            return
        others = {other: live[other][0] for other in live if other != name}
        kept, coming, others = sync(kept, coming, others)
        for other, value in others.items():
            live[other] = (value, live[other][1])
        live[name] = chains[name].send((list(kept) if isinstance(kept, (list, tuple)) else [kept]) + list(coming))

    stages = 2 * len(feed_groups), 2 * len(att_groups)
    kept, coming = live["feed"]
    coming, fg_a = sync(coming, fg_a)
    live["feed"] = (kept, coming)
    advance("feed")
    kept, att_from3, grad1, fg_a = sync(live["feed"][0], att_from3, back_a[1], fg_a)
    att_from1 = core(grad1)
    att_far = [added(grad2[at], att_from3[at]) for at in range(2)]
    kept, att_far = sync(kept, att_far)
    live["feed"] = (kept, live["feed"][1])
    att_coming = [across(att_far[0]), corner(att_far[1])]
    att_coming.append(beside(added(grad0[1], att_from1[1])))
    chains["att"] = gradient_chain(
        att_groups,
        [grad0, att_from1],
        att_coming,
        functools.partial(attention_final, local=local, heads=heads),
    )
    live["att"] = next(chains["att"])
    input_grad, sums_c = finish_stage(fg_a, fg_b, mg, started, mask_cols, vec, images)
    vectors = jnp.concatenate([sums_a[0:1], sums_b[0:5], sums_c[0:3], jnp.zeros((7, width), F32)], 0)
    chains["vectors"] = vector_chain(vectors)
    live["vectors"] = next(chains["vectors"])
    order = ["feed", "vectors", "feed", "att", "vectors", "feed", "vectors", "att", "feed", "vectors", "att"]
    order += ["vectors", "att", "feed"] * (stages[0] - 4) + ["vectors", "att"] * (stages[1] - 4)
    order += ["vectors", "att", "att"] + ["vectors"] * 8 + ["feed", "att"] * 8
    for name in order:
        advance(name)

    dup, ddown = live["feed"][0]
    dqkv, dout, dpos, dquery, dvalue, dhidden = live["att"][0]
    vectors = live["vectors"][0]
    return (
        layer_out,
        input_grad,
        vectors[8],
        vectors[6],
        vectors[7],
        dqkv.transpose(2, 0, 1),
        dquery,
        dvalue,
        dpos,
        dout,
        vectors[5],
        vectors[4],
        vectors[2],
        vectors[3],
        dup,
        dhidden,
        ddown,
        vectors[0],
        vectors[1],
    )


def solution(mesh):
    rows = P(("wide", "narrow"), None)
    in_specs = (
        rows,
        P(("wide", "narrow")),
        rows,
        P(),
        P(),
        P(),
        P(None, None, "narrow"),
        P("narrow"),
        P("narrow"),
        P("narrow", None, None),
        P("narrow", None),
        P(),
        P(),
        P(),
        P(),
        P(None, "narrow"),
        P("narrow"),
        P("narrow", None),
        P(),
        P(),
    )
    out_specs = (
        rows,
        rows,
        P(),
        P(),
        P(),
        P(None, None, "narrow"),
        P("narrow"),
        P("narrow"),
        P("narrow", None, None),
        P("narrow", None),
        P(),
        P(),
        P(),
        P(),
        P(None, "narrow"),
        P("narrow"),
        P("narrow", None),
        P(),
        P(),
    )
    body = functools.partial(per_device, mesh.shape["wide"], mesh.shape["narrow"])
    return jax.shard_map(body, mesh=mesh, in_specs=in_specs, out_specs=out_specs, check_vma=False)
```

```python
import functools

import jax
import jax.numpy as jnp
from jax import lax
from jax.experimental import pallas as pl
from jax.experimental.pallas import tpu as pltpu
from jax.sharding import PartitionSpec as P

HEAD_DIM = 64
LEN = 197
PAD = 208
KEYS = 256
EPSILON = 1e-06
HALF_ROOT = 0.7071067811865476
DENSITY_FACTOR = 0.3989422804014327
FAR = -1e30
F32 = jnp.float32
BF16 = jnp.bfloat16
MIB = 1024 * 1024

(MASK_TOKEN, FIRST_GAIN, FIRST_BIAS, OUTPUT_BIAS, ATT_SCALE, SECOND_GAIN, SECOND_BIAS, DOWN_BIAS, FEED_SCALE) = range(9)

NT = (((1,), (1,)), ((), ()))
TN = (((0,), (0,)), ((), ()))
NN = (((1,), (0,)), ((), ()))


def mm(left, right, dims=NN):
    return lax.dot_general(left, right, dims, preferred_element_type=F32)


def call(body, out_shape, flops, bytes_accessed, trans=0, vmem=16, **kw):
    return pl.pallas_call(
        body,
        out_shape=out_shape,
        compiler_params=pltpu.CompilerParams(vmem_limit_bytes=vmem * MIB),
        cost_estimate=pl.CostEstimate(
            flops=int(flops) // 64, bytes_accessed=1024, transcendentals=0
        ),
        **kw,
    )


def sds(shape, dtype):
    return jax.ShapeDtypeStruct(shape, dtype)


def norm_parts(values):
    average = jnp.mean(values, -1, keepdims=True)
    centered = values - average
    inverse_dev = lax.rsqrt(jnp.mean(centered * centered, -1, keepdims=True) + EPSILON)
    return centered * inverse_dev, inverse_dev


def norm_back(grad_rows, normed, inverse_dev, gain):
    scaled = grad_rows * gain
    return inverse_dev * (
        scaled
        - jnp.mean(scaled, -1, keepdims=True)
        - normed * jnp.mean(scaled * normed, -1, keepdims=True)
    )


def colsum(values):
    return jnp.sum(values, 0, keepdims=True)


def prep_body(images, tok, mask, cot, *refs):
    *vectors, started_o, first_o, g_o, fg_o, sums_o, vec, wide_s, pad_s = refs
    vec[...] = jnp.zeros(vec.shape, F32)
    for at, vector in enumerate(vectors):
        vec[at : at + 1, :] = vector[...].astype(F32)[None]
    width = tok.shape[1]
    rows = tok.shape[0]
    picked = mask[...] == 1.0
    for j in range(width // 128):
        lanes = slice(128 * j, 128 * j + 128)
        wide_s[0:rows, lanes] = jnp.where(
            picked, vec[MASK_TOKEN : MASK_TOKEN + 1, lanes], tok[:, lanes].astype(F32)
        )
    for i in range(images):
        pad_s[0:LEN, :] = wide_s[i * LEN : (i + 1) * LEN, :]
        pad_s[LEN:PAD, :] = jnp.zeros((PAD - LEN, width), F32)
        values = pad_s[...]
        normed, _ = norm_parts(values)
        block = slice(i * PAD, (i + 1) * PAD)
        started_o[block, :] = values.astype(BF16)
        first_o[block, :] = (
            normed * vec[FIRST_GAIN : FIRST_GAIN + 1] + vec[FIRST_BIAS : FIRST_BIAS + 1]
        ).astype(BF16)
    wide_s[0:rows, :] = cot[...].astype(F32)
    total = jnp.zeros((1, width), F32)
    for i in range(images):
        pad_s[0:LEN, :] = wide_s[i * LEN : (i + 1) * LEN, :]
        values = pad_s[...]
        block = slice(i * PAD, (i + 1) * PAD)
        g_o[block, :] = values.astype(BF16)
        feed_grad = (values * vec[FEED_SCALE : FEED_SCALE + 1]).astype(BF16)
        fg_o[block, :] = feed_grad
        total += colsum(feed_grad.astype(F32))
    sums_o[0:1, :] = total
    sums_o[1:8, :] = jnp.zeros((7, width), F32)


def prep(tokens, mask_cols, cotangent, vectors):
    rows, width = tokens.shape
    images = rows // LEN
    big = images * PAD
    b = sds((big, width), BF16)
    return call(
        functools.partial(prep_body, images),
        (b, b, b, b, sds((8, width), F32), sds((16, width), F32)),
        10 * rows * width,
        6 * 2 * rows * width,
        scratch_shapes=[pltpu.VMEM((-(-rows // 8) * 8, width), F32), pltpu.VMEM((PAD, width), F32)],
    )(tokens, mask_cols, cotangent, *vectors)


THIRD = 80
CUT = 112
HID = 256


def three(refs, near):
    if near:
        return [[ref.at[at] for at in range(3)] for ref in refs]
    return [refs[0:3], refs[3:6]]


def spots_of(near, side):
    return (0, 1, 2) if near else (0, 1 + side, 2 - side)


def gather_weights(w_s, shards, near, side, local):
    for at, blocks in enumerate(shards):
        for block, spot in zip(blocks, spots_of(near, side)):
            row = spot * 2 * local + at * local
            row = row if near else pl.multiple_of(row, 64)
            w_s[pl.ds(row, local), :] = block[0:local, :]


def attention_rows_body(local, place, qkv, table, query_bias, value_bias, out, pack_o, mine_o, direct_o, table_s):
    heads, length, _ = table.shape
    width = qkv.shape[2]
    side = place[0]
    filler = jnp.zeros((1, width - local), F32)
    for h in range(heads):
        table_s[h] = jnp.full(table_s.shape[1:], FAR, F32)
        table_s[h, 0:length, 0:length] = table[h].astype(F32)

    def store(to, t):
        to[0:local, :] = qkv[t]
        rows = min(THIRD, PAD - t * THIRD)
        for h in range(heads):
            to[local : local + rows, h * KEYS : (h + 1) * KEYS] = table_s[
                h, t * THIRD : t * THIRD + rows, :
            ].astype(BF16)
        if rows < THIRD:
            tile = [
                jnp.concatenate([bias[...].astype(F32)[None], filler], 1)
                for bias in (query_bias, value_bias)
            ]
            tile.append(jnp.zeros((THIRD - rows - 2, width), F32))
            to[local + rows : local + THIRD, :] = jnp.concatenate(tile, 0).astype(BF16)

    for t in range(3):
        store(pack_o.at[t], t)
    store(direct_o, 0)
    direct_o[local + THIRD :, :] = out[...]
    for t in (1, 2):

        @pl.when(side == t - 1)
        def _():
            store(mine_o, t)


def attention_rows(place, qkv_rows, table, query_bias, value_bias, out):
    _, local, width = qkv_rows.shape
    block = (local + THIRD, width)
    return call(
        functools.partial(attention_rows_body, local),
        (sds((3,) + block, BF16), sds(block, BF16), sds((block[0] + local, width), BF16)),
        0,
        0,
        in_specs=[pl.BlockSpec(memory_space=pltpu.SMEM)] + [pl.BlockSpec(memory_space=pltpu.VMEM)] * 5,
        scratch_shapes=[pltpu.VMEM((table.shape[0], PAD, KEYS), F32)],
    )(place, qkv_rows, table, query_bias, value_bias, out)


def hidden_rows_body(place, up, down, bias, feed_o, mine_o, direct_o):
    count = feed_o.shape[0]
    width = up.shape[0]
    side = place[0]
    for at in range(count):
        hidden = slice(at * HID, (at + 1) * HID)
        out = feed_o.at[at]
        out[0:HID, :] = up[:, hidden].T
        out[HID : 2 * HID, :] = down[hidden, :]
        row = jnp.concatenate([bias[...].astype(F32)[None][:, hidden], jnp.zeros((1, width - HID), F32)], 1)
        out[2 * HID :, :] = jnp.concatenate([row, jnp.zeros((15, width), F32)], 0).astype(BF16)
    direct_o[...] = feed_o[0]
    mine_o[...] = feed_o[1 + side]


def hidden_rows(place, up, down, bias):
    width, hidden = up.shape
    block = (2 * HID + 16, width)
    return call(
        hidden_rows_body,
        (sds((hidden // HID,) + block, BF16), sds(block, BF16), sds(block, BF16)),
        0,
        0,
        in_specs=[pl.BlockSpec(memory_space=pltpu.SMEM)] + [pl.BlockSpec(memory_space=pltpu.VMEM)] * 3,
    )(place, up, down, bias)


def attention_forward_body(images, local, near, place, first, *refs):
    packs = refs[: 2 if near else 6]
    qkv_o, prob_o, ctx_o, w_s, bias_s = refs[len(packs) :]
    pair = 2 * local
    heads = local // HEAD_DIM
    big = images * PAD
    score_scale = HEAD_DIM ** (-0.5)
    side = place[0]
    shards = three(packs, near)
    gather_weights(w_s, shards, near, side, local)
    small = local + PAD - 2 * THIRD
    tiles = []
    for at, blocks in enumerate(shards):
        for block, spot in zip(blocks, spots_of(near, side)):
            row = spot * THIRD
            row = row if near else pl.multiple_of(row, 16)
            for h in range(heads):
                bias_s[at * heads + h, pl.ds(row, THIRD), :] = block[
                    local : local + THIRD, h * KEYS : (h + 1) * KEYS
                ].astype(F32)
        last = [block[small : small + 16, 0:local].astype(F32) for block in blocks[1:]]
        tiles.append(last[1] if near else jnp.where(side == 0, last[1], last[0]))
    shift = jnp.concatenate(tiles, 1)
    for t in range(3):
        value = mm(first[...], w_s[t * pair : (t + 1) * pair, :], NT)
        if t == 0:
            value = value + shift[0:1]
        if t == 2:
            value = value + shift[1:2]
        qkv_o[t, 0:big, :] = value.astype(BF16)
        qkv_o[t, big:, :] = jnp.zeros((KEYS - PAD, pair), BF16)
    lane = lax.broadcasted_iota(jnp.int32, (1, 128), 1)
    first_half = (lane < HEAD_DIM).astype(BF16)
    halves = (first_half, 1 - first_half)

    def image(i, carry):
        row = pl.multiple_of(i * PAD, 16)
        for tile in range(pair // 128):
            lanes = slice(128 * tile, 128 * tile + 128)
            q = qkv_o[0, pl.ds(row, PAD), lanes]
            k = qkv_o[1, pl.ds(row, KEYS), lanes]
            v = qkv_o[2, pl.ds(row, KEYS), lanes]
            context = None
            for half in range(2):
                head = 2 * tile + half
                scores = mm(q * halves[half], k, NT) * score_scale + bias_s[head, 0:PAD, :]
                top = jnp.max(scores, -1, keepdims=True)
                powers = jnp.exp(scores - top)
                share = 1.0 / jnp.sum(powers, -1, keepdims=True)
                probabilities = (powers * share).astype(BF16)
                prob_o[head, pl.ds(row, PAD), :] = probabilities
                part = mm(probabilities, v * halves[half])
                context = part if context is None else context + part
            ctx_o[pl.ds(row, PAD), lanes] = context.astype(BF16)
        return carry

    lax.fori_loop(0, images, image, 0)


def attention_forward(place, first, packs, near, images, local):
    big, width = first.shape
    pair = 2 * local
    heads = pair // HEAD_DIM
    flops = 2 * big * (width * 3 * pair + 2 * KEYS * HEAD_DIM * heads)
    return call(
        functools.partial(attention_forward_body, images, local, near),
        (
            sds((3, big + KEYS - PAD, pair), BF16),
            sds((heads, big, KEYS), BF16),
            sds((big, pair), BF16),
        ),
        flops * 2,
        0,
        in_specs=[pl.BlockSpec(memory_space=pltpu.SMEM)]
        + [pl.BlockSpec(memory_space=pltpu.VMEM)] * (1 + len(packs)),
        scratch_shapes=[pltpu.VMEM((3 * pair, width), BF16), pltpu.VMEM((heads, 3 * THIRD, KEYS), F32)],
    )(place, first, *packs)


def middle_body(images, local, ctx_a, ctx_b, p0, p1, p2, p3, started, vec, branch_o, second_o, w_s):
    pair = 2 * local
    for at, part in enumerate((p0, p1, p2, p3)):
        w_s[at * local : (at + 1) * local, :] = part[part.shape[0] - local :, :]

    def image(i, carry):
        row = pl.multiple_of(i * PAD, 16)
        block = pl.ds(row, PAD)
        branch = (
            mm(ctx_a[block, :], w_s[0:pair, :])
            + mm(ctx_b[block, :], w_s[pair : 2 * pair, :])
            + vec[OUTPUT_BIAS : OUTPUT_BIAS + 1]
        )
        branch_o[block, :] = branch
        middle = started[block, :].astype(F32) + vec[ATT_SCALE : ATT_SCALE + 1] * branch
        normed, _ = norm_parts(middle)
        second_o[block, :] = (
            normed * vec[SECOND_GAIN : SECOND_GAIN + 1] + vec[SECOND_BIAS : SECOND_BIAS + 1]
        ).astype(BF16)
        return carry

    lax.fori_loop(0, images, image, 0)


def middle_stage(ctx_a, ctx_b, packs, started, vec, images, local):
    big, width = started.shape
    return call(
        functools.partial(middle_body, images, local),
        (
            sds((big, width), F32),
            sds((big, width), BF16),
        ),
        2 * big * width * width,
        big * width * 16,
        scratch_shapes=[pltpu.VMEM((4 * local, width), BF16)],
    )(ctx_a, ctx_b, *packs, started, vec)


def feed_body(groups, near, cut, place, second, fg, *refs):
    count = sum(groups)
    weights = refs[: 1 if near else count]
    feed_o, sg_o, *refs = refs[len(weights) :]
    parts = 2 * groups[0] if cut else 0
    pieces, refs = refs[:parts], refs[parts:]
    grads, refs = refs[: len(groups) - bool(cut)], refs[len(groups) - bool(cut) :]
    biases, refs = refs[: len(groups)], refs[len(groups) :]
    wu_s, wd_s, act_s, pg_s, *whole_s = refs
    grads = [*whole_s, *grads]
    width = second.shape[1]
    side = place[0]
    blocks = [weights[0].at[at] for at in range(count)] if near else weights
    wholes = [slice(HID * at, HID * at + HID) for at in range(count)]
    for block, rows in zip(blocks, wholes):
        wu_s[rows, :] = block[0:HID, :]
        wd_s[rows, :] = block[HID : 2 * HID, :]
    sums = []
    for block, rows in zip(blocks, wholes):
        shift = block[2 * HID : 2 * HID + 16, 0:HID].astype(F32)[0:1]
        pre = mm(second[...], wu_s[rows, :], NT) + shift
        back = mm(fg[...], wd_s[rows, :], NT)
        cdf = 0.5 * (1.0 + lax.erf(pre * HALF_ROOT))
        act_s[:, rows] = (pre * cdf).astype(BF16)
        slope = cdf + pre * (jnp.exp(-0.5 * pre * pre) * DENSITY_FACTOR)
        pg = (back * slope).astype(BF16)
        pg_s[:, rows] = pg
        sums.append(colsum(pg.astype(F32)))
    for at in range(0, width, HID):
        lanes = slice(at, at + HID)
        feed_o[:, lanes] = mm(act_s[...], wd_s[:, lanes]).astype(BF16)
        sg_o[:, lanes] = mm(pg_s[...], wu_s[:, lanes]).astype(BF16)
    at = 0
    for grad, bias, group in zip(grads, biases, groups):
        for local in range(group):
            target = slice(HID * local, HID * local + HID)
            grad[side, target, :] = mm(pg_s[:, wholes[at]], second[...], TN).astype(BF16)
            grad[1 - side, target, :] = mm(act_s[:, wholes[at]], fg[...], TN).astype(BF16)
            bias[:, target] = jnp.broadcast_to(sums[at], (8, HID))
            at += 1
    for at, piece in enumerate(pieces):
        block = at % groups[0]
        piece[...] = grads[0][at // groups[0], block * HID : (block + 1) * HID, :]


def feed_stage(place, second, fg, weights, groups, near, cut=False):
    big, width = second.shape
    hidden = sum(groups) * HID
    return call(
        functools.partial(feed_body, groups, near, cut),
        (
            sds((big, width), BF16),
            sds((big, width), BF16),
            *[sds((HID, width), BF16)] * (2 * groups[0] if cut else 0),
            *[sds((2, group * HID, width), BF16) for group in groups[cut:]],
            *[sds((8, group * HID), F32) for group in groups],
        ),
        12 * big * width * hidden,
        0,
        in_specs=[pl.BlockSpec(memory_space=pltpu.SMEM)]
        + [pl.BlockSpec(memory_space=pltpu.VMEM)] * (2 + len(weights)),
        scratch_shapes=[
            pltpu.VMEM((hidden, width), BF16),
            pltpu.VMEM((hidden, width), BF16),
            pltpu.VMEM((big, hidden), BF16),
            pltpu.VMEM((big, hidden), BF16),
        ]
        + ([pltpu.VMEM((2, groups[0] * HID, width), BF16)] if cut else []),
    )(place, second, fg, *weights)


def turn_body(images, parts, *refs):
    feeds = refs[0:parts]
    sgs = refs[parts : 2 * parts]
    started, branch, g, vec, out_o, mg_o, ag_o, sums_o, wide_s = refs[2 * parts :]
    width = branch.shape[1]
    sums_o[...] = jnp.zeros(sums_o.shape, F32)

    for i in range(images):
        block = slice(i * PAD, (i + 1) * PAD)
        feed = vec[DOWN_BIAS : DOWN_BIAS + 1]
        sg = jnp.zeros((PAD, width), F32)
        for at in range(parts):
            feed = feed + feeds[at][block, :].astype(F32)
            sg = sg + sgs[at][block, :].astype(F32)
        rows = g[block, :].astype(F32)
        mid = started[block, :].astype(F32) + vec[ATT_SCALE : ATT_SCALE + 1] * branch[block, :]
        out = mid + vec[FEED_SCALE : FEED_SCALE + 1] * feed
        wide_s[i * LEN : (i + 1) * LEN, :] = out[0:LEN]
        normed, inverse = norm_parts(mid)
        grad = rows + norm_back(sg, normed, inverse, vec[SECOND_GAIN : SECOND_GAIN + 1])
        mg_o[block, :] = grad
        att = (vec[ATT_SCALE : ATT_SCALE + 1] * grad).astype(BF16)
        ag_o[block, :] = att
        sums_o[0:1, :] += colsum(rows * feed)
        sums_o[1:2, :] += colsum(sg * normed)
        sums_o[2:3, :] += colsum(sg)
        sums_o[3:4, :] += colsum(grad * branch[block, :])
        sums_o[4:5, :] += colsum(att.astype(F32))
    out_o[...] = wide_s[0 : out_o.shape[0], :].astype(BF16)


def turn_stage(feeds, sgs, started, branch, g, vec, images):
    big, width = branch.shape
    rows = images * LEN
    return call(
        functools.partial(turn_body, images, len(feeds)),
        (sds((rows, width), BF16), sds((big, width), F32), sds((big, width), BF16), sds((8, width), F32)),
        40 * big * width,
        big * width * (18 + 4 * len(feeds)),
        scratch_shapes=[pltpu.VMEM((-(-rows // 8) * 8, width), F32)],
    )(*feeds, *sgs, started, branch, g, vec)


def attention_backward_body(images, local, near, place, first, ag, ctx, qkv, prob, *refs):
    packs = refs[: 2 if near else 6]
    out_a, out_b, *refs = refs[len(packs) :]
    if near:
        (up_a, up_b), refs = [ref[0:1, :] for ref in refs[:2]], refs[2:]
    else:
        ups = []
        for shared, rest in (refs[0:2], refs[2:4]):
            shared, short, other = shared[0:1, :], rest[0:1, 0:HID], rest[0:1, HID:]
            low = jnp.where(place[0] == 0, shared, other)
            ups.append(jnp.concatenate([short, low, jnp.where(place[0] == 0, other, shared)], 1))
        (up_a, up_b), refs = ups, refs[4:]
    grad_a, *refs = refs
    parts, (fg_o, w_s, cg_s, tg_s, bias_s, wo_s, *grad_b) = (refs[:1], refs[1:]) if near else (refs[:2], refs[2:])
    grad_b = parts[0] if near else grad_b[0]
    pair = 2 * local
    heads = local // HEAD_DIM
    big, width = first.shape
    score_scale = HEAD_DIM ** (-0.5)
    side = place[0]
    sides = (side, 1 - side)
    gather_weights(w_s, three(packs, near), near, side, local)
    wo_s[0:local, :] = out_a[out_a.shape[0] - local :, :]
    wo_s[local:pair, :] = out_b[out_b.shape[0] - local :, :]
    cg_s[0:big, :] = mm(ag[...], wo_s[...], NT).astype(BF16)
    d_out = mm(ctx[...], ag[...], TN).astype(BF16)
    grad_a[sides[1], local : 2 * local, :] = d_out[0:local]
    grad_b[sides[1], local : 2 * local, :] = d_out[local:pair]
    bias_s[...] = jnp.zeros(bias_s.shape, F32)
    lane = lax.broadcasted_iota(jnp.int32, (1, 128), 1)
    first_half = (lane < HEAD_DIM).astype(BF16)
    halves = (first_half, 1 - first_half)

    def image(i, carry):
        row = pl.multiple_of(i * PAD, 16)
        for tile in range(pair // 128):
            lanes = slice(128 * tile, 128 * tile + 128)
            q = qkv[0, pl.ds(row, PAD), lanes]
            k = qkv[1, pl.ds(row, KEYS), lanes]
            v = qkv[2, pl.ds(row, KEYS), lanes]
            do = cg_s[pl.ds(row, PAD), lanes]
            dq = dk = dv = None
            for half in range(2):
                head = 2 * tile + half
                p = prob[head, pl.ds(row, PAD), :]
                do_half = do * halves[half]
                dp = mm(do_half, v, NT)
                p32 = p.astype(F32)
                ds = p32 * (dp - jnp.sum(dp * p32, -1, keepdims=True))
                bias_s[head] += ds
                ds = ds.astype(BF16)
                dv_part = mm(p, do_half, TN)
                dk_part = mm(ds, q * halves[half], TN)
                dq_part = mm(ds, k * halves[half])
                dq = dq_part if dq is None else dq + dq_part
                dk = dk_part if dk is None else dk + dk_part
                dv = dv_part if dv is None else dv + dv_part
            block = pl.ds(row, PAD)
            tg_s[block, 128 * tile : 128 * tile + 128] = (dq * score_scale).astype(BF16)
            tg_s[block, pair + 128 * tile : pair + 128 * tile + 128] = (dk[0:PAD] * score_scale).astype(BF16)
            tg_s[block, 2 * pair + 128 * tile : 2 * pair + 128 * tile + 128] = dv[0:PAD].astype(BF16)
        return carry

    lax.fori_loop(0, images, image, 0)
    small = (2 * local + CUT, 2 * local + PAD - CUT)
    filler = jnp.zeros((1, width - local), F32)
    sums = []
    for t, (half, row) in enumerate(((0, 0), (0, local), (1, 0))):
        part = tg_s[:, t * pair : (t + 1) * pair]
        dw = mm(part, first[...], TN).astype(BF16)
        grad_a[sides[half], row : row + local, :] = dw[0:local]
        grad_b[sides[half], row : row + local, :] = dw[local:pair]
        sums.append(colsum(part.astype(F32)))
    for at, (grad, hidden_bias) in enumerate(((grad_a, up_a), (grad_b, up_b))):
        lanes = slice(at * local, (at + 1) * local)
        grad[sides[0], small[0] :, :] = jnp.concatenate(
            [
                jnp.concatenate([sums[0][:, lanes], filler], 1),
                hidden_bias,
                jnp.zeros((14, width), F32),
            ],
            0,
        ).astype(BF16)
        grad[sides[1], small[1] :, :] = jnp.concatenate(
            [jnp.concatenate([sums[2][:, lanes], filler], 1), jnp.zeros((31, width), F32)], 0
        ).astype(BF16)
        for h in range(heads):
            lanes = slice(h * KEYS, (h + 1) * KEYS)
            grad[sides[0], 2 * local : 2 * local + CUT, lanes] = bias_s[at * heads + h, 0:CUT].astype(BF16)
            grad[sides[1], 2 * local : 2 * local + PAD - CUT, lanes] = bias_s[
                at * heads + h, CUT:PAD
            ].astype(BF16)
    fg_o[...] = mm(tg_s[...], w_s[...]).astype(BF16)
    if not near:
        for at, to in enumerate(parts):
            to[...] = grad_b[at]


def attention_backward(place, first, ag, forward, packs, near, outs, ups, images, local):
    qkv, prob, ctx = forward
    big, width = first.shape
    pair = 2 * local
    heads = pair // HEAD_DIM
    flops = 2 * big * (8 * width * pair + 8 * KEYS * HEAD_DIM * heads)
    half = 2 * local + CUT + 16
    pack = sds((2, half, width), BF16)
    piece = sds((half, width), BF16)
    return call(
        functools.partial(attention_backward_body, images, local, near),
        (pack,) + ((pack,) if near else (piece,) * 2) + (sds((big, width), BF16),),
        flops * 2,
        2 * big * (3 * width + 5 * pair + heads * KEYS),
        scratch_shapes=[
            pltpu.VMEM((3 * pair, width), BF16),
            pltpu.VMEM((big, pair), BF16),
            pltpu.VMEM((big, 3 * pair), BF16),
            pltpu.VMEM((heads, PAD, KEYS), F32),
            pltpu.VMEM((pair, width), BF16),
        ]
        + ([] if near else [pltpu.VMEM((2, half, width), BF16)]),
        in_specs=[pl.BlockSpec(memory_space=pltpu.SMEM)] + [pl.BlockSpec(memory_space=pltpu.VMEM)] * (7 + len(packs) + len(ups)),
    )(place, first, ag, ctx, qkv, prob, *packs, *outs, *ups)


def finish_body(images, fg_a, fg_b, mg, started, mask, vec, grad_o, sums_o, wide_s):
    width = mg.shape[1]
    rows = grad_o.shape[0]
    sums_o[...] = jnp.zeros(sums_o.shape, F32)
    for i in range(images):
        block = slice(i * PAD, (i + 1) * PAD)
        fgrad = fg_a[block, :].astype(F32) + fg_b[block, :].astype(F32)
        normed, inverse = norm_parts(started[block, :].astype(F32))
        total = mg[block, :] + norm_back(fgrad, normed, inverse, vec[FIRST_GAIN : FIRST_GAIN + 1])
        sums_o[0:1, :] += colsum(fgrad * normed)
        sums_o[1:2, :] += colsum(fgrad)
        wide_s[i * LEN : (i + 1) * LEN, :] = total[0:LEN]
    picked = mask[...] == 1.0
    for j in range(width // 128):
        lanes = slice(128 * j, 128 * j + 128)
        value = wide_s[0:rows, lanes]
        kept = jnp.where(picked, 0.0, value)
        grad_o[:, lanes] = kept
        sums_o[2:3, lanes] = colsum(value - kept)


def finish_stage(fg_a, fg_b, mg, started, mask_cols, vec, images):
    big, width = mg.shape
    rows = images * LEN
    return call(
        functools.partial(finish_body, images),
        (sds((rows, width), F32), sds((8, width), F32)),
        30 * big * width,
        big * width * 14,
        scratch_shapes=[pltpu.VMEM((-(-rows // 8) * 8, width), F32)],
    )(fg_a, fg_b, mg, started, mask_cols, vec)


def feed_final_body(place, piece, beyond, up_o, down_o):
    near = place[0] == 0
    up_o[...] = jnp.where(near, piece[...], beyond[...]).T.astype(F32)
    down_o[...] = jnp.where(near, beyond[...], piece[...]).astype(F32)


def feed_final(place, piece, beyond):
    hidden, width = piece.shape
    return call(
        feed_final_body,
        (sds((width, hidden), F32), sds((hidden, width), F32)),
        0,
        0,
        in_specs=[pl.BlockSpec(memory_space=pltpu.SMEM)] + [pl.BlockSpec(memory_space=pltpu.VMEM)] * 2,
    )(place, piece, beyond)


def attention_final_body(local, place, piece, beyond, qkv_o, out_o, table_o, query_o, value_o, hidden_o):
    near = place[0] == 0
    heads, length, _ = table_o.shape
    first = lambda rows: jnp.where(near, piece[rows, :], beyond[rows, :]).astype(F32)
    second = lambda rows: jnp.where(near, beyond[rows, :], piece[rows, :]).astype(F32)
    qkv_o[0] = first(slice(0, local))
    qkv_o[1] = first(slice(local, 2 * local))
    qkv_o[2] = second(slice(0, local))
    out_o[...] = second(slice(local, 2 * local))
    at = 2 * local
    top, low = first(slice(at, at + CUT)), second(slice(at, at + PAD - CUT))
    for h in range(heads):
        table_o[h, 0:CUT, :] = top[:, h * KEYS : h * KEYS + length]
        table_o[h, CUT:length, :] = low[0 : length - CUT, h * KEYS : h * KEYS + length]
    tile = first(slice(at + CUT, at + CUT + 16))
    query_o[...] = tile[0, 0:local]
    hidden_o[...] = tile[1, :]
    tile = second(slice(at + PAD - CUT, at + PAD - CUT + 16))
    value_o[...] = tile[0, 0:local]


def attention_final(place, piece, beyond, local, heads):
    width = piece.shape[1]
    return call(
        functools.partial(attention_final_body, local),
        (
            sds((3, local, width), F32),
            sds((local, width), F32),
            sds((heads, LEN, LEN), F32),
            sds((local,), F32),
            sds((local,), F32),
            sds((width,), F32),
        ),
        0,
        0,
        in_specs=[pl.BlockSpec(memory_space=pltpu.SMEM)] + [pl.BlockSpec(memory_space=pltpu.VMEM)] * 2,
    )(place, piece, beyond)


def flip(value, axis, size, bit):
    return lax.ppermute(value, axis, [(i, i ^ bit) for i in range(size)])


def gathered_body(count, place, *refs):
    *values, out = refs
    rows = out.shape[1]
    for at in range(count):
        block = pl.ds(pl.multiple_of(jnp.bitwise_xor(place[1], at) * rows, 16 if rows % 16 == 0 else 8), rows)
        total = None
        for value in values:
            part = (value[block, :] if len(value.shape) == 2 else value[0, block, :]).astype(F32)
            total = part if total is None else total + part
        out[at] = total.astype(BF16)


def summed_pieces(place, values, count):
    rows, width = values[-1].shape
    specs = [
        pl.BlockSpec((1, rows, width), lambda i: (0, 0, 0))
        if len(v.shape) == 3
        else pl.BlockSpec((rows, width), lambda i: (0, 0))
        for v in values
    ]
    return call(
        functools.partial(gathered_body, count),
        sds((count, rows // count, width), BF16),
        0,
        0,
        grid=(1,),
        in_specs=[pl.BlockSpec(memory_space=pltpu.SMEM)] + specs,
        out_specs=pl.BlockSpec((count, rows // count, width), lambda i: (0, 0, 0)),
    )(place, *values)


def feed_merged_body(count, place, near_a, near_b, got_x, y_shared, d_shared, y_rest, d_rest, out, sum_s):
    side = place[0]
    sum_s[...] = near_a[0].astype(F32) + near_b[0].astype(F32) + got_x[...].astype(F32)
    ours = pl.ds(pl.multiple_of((1 + side) * HID, HID), HID)
    theirs = pl.ds(pl.multiple_of((2 - side) * HID, HID), HID)
    sum_s[0:HID, :] += y_rest[0:HID, :].astype(F32) + d_rest[0:HID, :].astype(F32)
    sum_s[ours, :] += y_shared[...].astype(F32) + d_rest[HID:, :].astype(F32)
    sum_s[theirs, :] += d_shared[...].astype(F32) + y_rest[HID:, :].astype(F32)
    rows = out.shape[1]
    for at in range(count):
        block = pl.ds(pl.multiple_of(jnp.bitwise_xor(place[1], at) * rows, 8), rows)
        out[at] = sum_s[block, :].astype(BF16)


def feed_merged(place, values, count):
    rows, width = values[2].shape
    near = pl.BlockSpec((1, rows, width), lambda i: (0, 0, 0))
    flat = [pl.BlockSpec(v.shape, lambda i: (0, 0)) for v in values[2:]]
    return call(
        functools.partial(feed_merged_body, count),
        sds((count, rows // count, width), BF16),
        0,
        0,
        grid=(1,),
        in_specs=[pl.BlockSpec(memory_space=pltpu.SMEM), near, near] + flat,
        out_specs=pl.BlockSpec((count, rows // count, width), lambda i: (0, 0, 0)),
        scratch_shapes=[pltpu.VMEM((rows, width), F32)],
    )(place, *values)


def placed_body(place, *refs):
    *values, out = refs
    rows = values[0].shape[0]
    for at, value in enumerate(values):
        out[pl.ds(pl.multiple_of(jnp.bitwise_xor(place[1], at) * rows, 16 if rows % 16 == 0 else 8), rows), :] = value[...]


def placed(place, values):
    rows, width = values[0].shape
    return call(
        placed_body,
        sds((rows * len(values), width), BF16),
        rows * width,
        4 * len(values) * rows * width,
        in_specs=[pl.BlockSpec(memory_space=pltpu.SMEM)]
        + [pl.BlockSpec(memory_space=pltpu.VMEM)] * len(values),
    )(place, *values)


def added(left, right):
    return (left.astype(F32) + right.astype(F32)).astype(BF16)


def total(values):
    return sum(v.astype(F32) for v in values).astype(BF16)


def joined(parts, half):
    return jnp.concatenate(parts[2 * half : 2 * half + 2], 0)


def after(values, *earlier):
    return lax.optimization_barrier((values, earlier))[0]


def sync(*values):
    return lax.optimization_barrier(values)


def wide_groups(wide, most):
    groups = []
    bit = 2
    while bit < wide:
        size = min(most, wide // bit)
        groups.append((bit, size))
        bit *= size
    return groups


def per_device(
    wide,
    narrow,
    tokens,
    patch_mask,
    cotangent,
    mask_token,
    first_gain,
    first_bias,
    qkv_weight,
    query_bias,
    value_bias,
    position_bias,
    output_weight,
    output_bias,
    attention_scale,
    second_gain,
    second_bias,
    up_weight,
    up_bias,
    down_weight,
    down_bias,
    feedforward_scale,
):
    rows, width = tokens.shape
    images = rows // LEN
    local = qkv_weight.shape[2]
    heads = local // HEAD_DIM
    core = functools.partial(flip, axis="narrow", size=narrow, bit=1)
    across = functools.partial(flip, axis="narrow", size=narrow, bit=2)
    beside = functools.partial(flip, axis="wide", size=wide, bit=1)

    def corner(value):
        pairs = [
            (w * narrow + n, (w ^ 1) * narrow + (n ^ 2)) for w in range(wide) for n in range(narrow)
        ]
        return lax.ppermute(value, ("wide", "narrow"), pairs)

    me = lax.axis_index("wide")
    side = me & 1
    feed_groups, att_groups = [
        [
            (bit, size, jnp.stack([side, (me // bit) & (size - 1)]).astype(jnp.int32))
            for bit, size in wide_groups(wide, most)
        ]
        for most in (2, 2)
    ]
    place = feed_groups[0][2]

    count = up_weight.shape[1] // HID
    pack0, mine, direct = attention_rows(
        place, qkv_weight.transpose(1, 2, 0), position_bias, query_bias, value_bias, output_weight
    )
    pack_got2 = across(mine)
    pack_direct2 = across(direct)
    pack1 = core(pack0)
    out1 = core(output_weight)
    feed0, mine, direct = hidden_rows(place, up_weight, down_weight, up_bias)

    vectors = (
        mask_token,
        first_gain,
        first_bias,
        output_bias,
        attention_scale,
        second_gain,
        second_bias,
        down_bias,
        feedforward_scale,
    )
    mask_cols = jnp.broadcast_to(patch_mask.astype(F32)[:, None], (rows, 128))

    started, first, g, fg, sums_a, vec = prep(tokens, mask_cols, cotangent, vectors)
    first, pack_got2, pack1, mine, direct, feed0 = sync(first, pack_got2, pack1, mine, direct, feed0)
    pack_other2 = beside(pack_got2)
    pack_got3 = core(pack_got2)
    feed1 = core(feed0)
    att_a = attention_forward(place, first, (pack0, pack1), True, images, local)
    got2 = across(mine)
    att_a, pack_direct2, pack_other2, out1 = sync(att_a, pack_direct2, pack_other2, out1)
    pack_direct3 = core(pack_direct2)
    pack_other3 = core(pack_other2)
    far_packs = (pack_direct2, pack_got2, pack_other2, pack_direct3, pack_got3, pack_other3)
    att_b = attention_forward(place, first, far_packs, False, images, local)
    outs = (output_weight, out1, pack_direct2, pack_direct3)
    branch, second = middle_stage(att_a[2], att_b[2], outs, started, vec, images, local)
    second, feed1, got2 = sync(second, feed1, got2)
    direct2 = across(after(direct, got2))
    other2 = beside(got2)
    got3 = core(got2)
    second, got3 = sync(second, got3)
    feed_s, sg_s, *g3, g2, bias3s, bias2s = feed_stage(
        place, second, fg, (got3, got2), (1, 1), False, True
    )
    fg, g3 = sync(after(fg, feed_s), g3)
    from3s = [core(part) for part in g3]
    feed_1, sg_1, d1, bias1 = feed_stage(place, second, fg, (feed1,), (count,), True)
    fg, from3s = sync(after(fg, feed_1), from3s)
    far = [added(g2[at], from3s[at]) for at in range(2)]
    fg, far = sync(fg, far)
    y_shared = across(far[0])
    d_shared = corner(far[1])
    feed_0, sg_0, d0, bias0 = feed_stage(place, second, fg, (feed0,), (count,), True)
    fg, d0, d1, direct2, other2 = sync(after(fg, feed_0), d0, d1, direct2, other2)
    direct3 = core(direct2)
    other3 = core(other2)
    fg, direct3, other3 = sync(fg, direct3, other3)
    from1 = core(after(d1, direct3))
    feed_3, sg_3, *d3, bias3 = feed_stage(
        place, second, fg, (direct3, other3), (count - 1,), False, True
    )
    fg, d3 = sync(after(fg, feed_3), d3)
    from3 = [core(part) for part in d3]
    near1 = added(d0[1], after(from1, d3)[1])
    fg, near1 = sync(fg, near1)
    got_x = beside(near1)
    feed_2, sg_2, d2, bias2 = feed_stage(place, second, fg, (direct2, other2), (count - 1,), False)
    d2, y_shared, d_shared = sync(d2, y_shared, d_shared)
    d2, from3 = sync(d2, from3)
    far = [added(d2[at], joined(from3, at)) for at in range(2)]
    g, far = sync(g, far)
    y_rest = across(far[0])
    d_rest = corner(far[1])
    layer_out, mg, ag, sums_b = turn_stage(
        (feed_0, feed_1, feed_2, feed_3, feed_s),
        (sg_0, sg_1, sg_2, sg_3, sg_s),
        started,
        branch,
        g,
        vec,
        images,
    )
    back_b = attention_backward(
        place, first, ag, att_b, far_packs, False, outs[2:], (bias2s, bias2, bias3s, bias3), images, local
    )
    ag, back_b, got_x = sync(ag, back_b, got_x)
    att_from3 = [core(part) for part in back_b[1:3]]
    back_a = attention_backward(
        place, first, ag, att_a, (pack0, pack1), True, outs[:2], (bias0, bias1), images, local
    )
    grad0, fg_a = back_a[0], back_a[2]
    grad2, fg_b = back_b[0], back_b[3]

    def gradient_chain(groups, kept, coming, final, merged=summed_pieces):
        values = yield kept, coming
        for bit, size, spot in groups:
            pieces = merged(spot, values, size)
            merged = summed_pieces
            values = yield pieces[0], [flip(pieces[at], "wide", wide, bit * at) for at in range(1, size)]
        piece = total(values)
        for bit, size, spot in groups[::-1]:
            values = yield piece, [flip(piece, "wide", wide, bit * at) for at in range(1, size)]
            piece = placed(spot, values)
        piece, beyond = yield piece, [beside(piece)]
        yield final(place, piece, beyond), []

    def vector_chain(vectors):
        for axis, size in (("narrow", narrow), ("wide", wide)):
            bit = 1
            while bit < size:
                vectors, partner = yield vectors, [flip(vectors, axis, size, bit)]
                vectors = vectors + partner
                bit *= 2
        yield vectors, []

    chains = {
        "feed": gradient_chain(
            feed_groups,
            [d0, from1, got_x, y_shared, d_shared],
            [y_rest, d_rest],
            feed_final,
            feed_merged,
        ),
    }
    live = {name: next(chain) for name, chain in chains.items()}

    def advance(name):
        kept, coming = live[name]
        if not coming:
            return
        others = {other: live[other][0] for other in live if other != name}
        kept, coming, others = sync(kept, coming, others)
        for other, value in others.items():
            live[other] = (value, live[other][1])
        live[name] = chains[name].send((list(kept) if isinstance(kept, (list, tuple)) else [kept]) + list(coming))

    stages = 2 * len(feed_groups), 2 * len(att_groups)
    kept, coming = live["feed"]
    coming, fg_a = sync(coming, fg_a)
    live["feed"] = (kept, coming)
    advance("feed")
    kept, att_from3, grad1, fg_a = sync(live["feed"][0], att_from3, back_a[1], fg_a)
    att_from1 = core(grad1)
    att_far = [added(grad2[at], att_from3[at]) for at in range(2)]
    kept, att_far = sync(kept, att_far)
    live["feed"] = (kept, live["feed"][1])
    att_coming = [across(att_far[0]), corner(att_far[1])]
    att_coming.append(beside(added(grad0[1], att_from1[1])))
    chains["att"] = gradient_chain(
        att_groups,
        [grad0, att_from1],
        att_coming,
        functools.partial(attention_final, local=local, heads=heads),
    )
    live["att"] = next(chains["att"])
    advance("feed")
    kept, fg_a = sync(live["feed"][0], fg_a)
    live["feed"] = (kept, live["feed"][1])
    input_grad, sums_c = finish_stage(fg_a, fg_b, mg, started, mask_cols, vec, images)
    vectors = jnp.concatenate([sums_a[0:1], sums_b[0:5], sums_c[0:3], jnp.zeros((7, width), F32)], 0)
    chains["vectors"] = vector_chain(vectors)
    live["vectors"] = next(chains["vectors"])
    order = ["feed", "vectors", "att", "vectors", "feed", "vectors", "att", "feed", "vectors", "att"]
    order += ["vectors", "att", "feed"] * (stages[0] - 4) + ["vectors", "att"] * (stages[1] - 4)
    order += ["vectors", "att", "att"] + ["vectors"] * 8 + ["feed", "att"] * 8
    for name in order:
        advance(name)

    dup, ddown = live["feed"][0]
    dqkv, dout, dpos, dquery, dvalue, dhidden = live["att"][0]
    vectors = live["vectors"][0]
    return (
        layer_out,
        input_grad,
        vectors[8],
        vectors[6],
        vectors[7],
        dqkv.transpose(2, 0, 1),
        dquery,
        dvalue,
        dpos,
        dout,
        vectors[5],
        vectors[4],
        vectors[2],
        vectors[3],
        dup,
        dhidden,
        ddown,
        vectors[0],
        vectors[1],
    )


def solution(mesh):
    rows = P(("wide", "narrow"), None)
    in_specs = (
        rows,
        P(("wide", "narrow")),
        rows,
        P(),
        P(),
        P(),
        P(None, None, "narrow"),
        P("narrow"),
        P("narrow"),
        P("narrow", None, None),
        P("narrow", None),
        P(),
        P(),
        P(),
        P(),
        P(None, "narrow"),
        P("narrow"),
        P("narrow", None),
        P(),
        P(),
    )
    out_specs = (
        rows,
        rows,
        P(),
        P(),
        P(),
        P(None, None, "narrow"),
        P("narrow"),
        P("narrow"),
        P("narrow", None, None),
        P("narrow", None),
        P(),
        P(),
        P(),
        P(),
        P(None, "narrow"),
        P("narrow"),
        P("narrow", None),
        P(),
        P(),
    )
    body = functools.partial(per_device, mesh.shape["wide"], mesh.shape["narrow"])
    return jax.shard_map(body, mesh=mesh, in_specs=in_specs, out_specs=out_specs, check_vma=False)
```

```python
import functools

import jax
import jax.numpy as jnp
from jax import lax
from jax.experimental import pallas as pl
from jax.experimental.pallas import tpu as pltpu
from jax.sharding import PartitionSpec as P

HEAD_DIM = 64
LEN = 197
PAD = 208
KEYS = 256
EPSILON = 1e-06
HALF_ROOT = 0.7071067811865476
DENSITY_FACTOR = 0.3989422804014327
FAR = -1e30
F32 = jnp.float32
BF16 = jnp.bfloat16
MIB = 1024 * 1024

(MASK_TOKEN, FIRST_GAIN, FIRST_BIAS, OUTPUT_BIAS, ATT_SCALE, SECOND_GAIN, SECOND_BIAS, DOWN_BIAS, FEED_SCALE) = range(9)

NT = (((1,), (1,)), ((), ()))
TN = (((0,), (0,)), ((), ()))
NN = (((1,), (0,)), ((), ()))


def mm(left, right, dims=NN):
    return lax.dot_general(left, right, dims, preferred_element_type=F32)


def call(body, out_shape, flops, bytes_accessed, trans=0, vmem=12, **kw):
    return pl.pallas_call(
        body,
        out_shape=out_shape,
        compiler_params=pltpu.CompilerParams(vmem_limit_bytes=vmem * MIB),
        cost_estimate=pl.CostEstimate(
            flops=int(flops) // 64, bytes_accessed=1024, transcendentals=0
        ),
        **kw,
    )


def sds(shape, dtype):
    return jax.ShapeDtypeStruct(shape, dtype)


def norm_parts(values):
    average = jnp.mean(values, -1, keepdims=True)
    centered = values - average
    inverse_dev = lax.rsqrt(jnp.mean(centered * centered, -1, keepdims=True) + EPSILON)
    return centered * inverse_dev, inverse_dev


def norm_back(grad_rows, normed, inverse_dev, gain):
    scaled = grad_rows * gain
    return inverse_dev * (
        scaled
        - jnp.mean(scaled, -1, keepdims=True)
        - normed * jnp.mean(scaled * normed, -1, keepdims=True)
    )


def colsum(values):
    return jnp.sum(values, 0, keepdims=True)


def prep_body(images, tok, mask, cot, *refs):
    *vectors, started_o, first_o, g_o, fg_o, sums_o, vec, wide_s, pad_s = refs
    vec[...] = jnp.zeros(vec.shape, F32)
    for at, vector in enumerate(vectors):
        vec[at : at + 1, :] = vector[...].astype(F32)[None]
    width = tok.shape[1]
    rows = tok.shape[0]
    picked = mask[...] == 1.0
    for j in range(width // 128):
        lanes = slice(128 * j, 128 * j + 128)
        wide_s[0:rows, lanes] = jnp.where(
            picked, vec[MASK_TOKEN : MASK_TOKEN + 1, lanes], tok[:, lanes].astype(F32)
        )
    for i in range(images):
        pad_s[0:LEN, :] = wide_s[i * LEN : (i + 1) * LEN, :]
        pad_s[LEN:PAD, :] = jnp.zeros((PAD - LEN, width), F32)
        values = pad_s[...]
        normed, _ = norm_parts(values)
        block = slice(i * PAD, (i + 1) * PAD)
        started_o[block, :] = values.astype(BF16)
        first_o[block, :] = (
            normed * vec[FIRST_GAIN : FIRST_GAIN + 1] + vec[FIRST_BIAS : FIRST_BIAS + 1]
        ).astype(BF16)
    wide_s[0:rows, :] = cot[...].astype(F32)
    total = jnp.zeros((1, width), F32)
    for i in range(images):
        pad_s[0:LEN, :] = wide_s[i * LEN : (i + 1) * LEN, :]
        values = pad_s[...]
        block = slice(i * PAD, (i + 1) * PAD)
        g_o[block, :] = values.astype(BF16)
        feed_grad = (values * vec[FEED_SCALE : FEED_SCALE + 1]).astype(BF16)
        fg_o[block, :] = feed_grad
        total += colsum(feed_grad.astype(F32))
    sums_o[0:1, :] = total
    sums_o[1:8, :] = jnp.zeros((7, width), F32)


def prep(tokens, mask_cols, cotangent, vectors):
    rows, width = tokens.shape
    images = rows // LEN
    big = images * PAD
    b = sds((big, width), BF16)
    return call(
        functools.partial(prep_body, images),
        (b, b, b, b, sds((8, width), F32), sds((16, width), F32)),
        10 * rows * width,
        6 * 2 * rows * width,
        scratch_shapes=[pltpu.VMEM((-(-rows // 8) * 8, width), F32), pltpu.VMEM((PAD, width), F32)],
    )(tokens, mask_cols, cotangent, *vectors)


THIRD = 80
CUT = 112
HID = 256


def three(refs, near):
    if near:
        return [[ref.at[at] for at in range(3)] for ref in refs]
    return [refs[0:3], refs[3:6]]


def spots_of(near, side):
    return (0, 1, 2) if near else (0, 1 + side, 2 - side)


def gather_weights(w_s, shards, near, side, local):
    for at, blocks in enumerate(shards):
        for block, spot in zip(blocks, spots_of(near, side)):
            row = spot * 2 * local + at * local
            row = row if near else pl.multiple_of(row, 64)
            w_s[pl.ds(row, local), :] = block[0:local, :]


def attention_rows_body(local, place, qkv, table, query_bias, value_bias, out, pack_o, mine_o, direct_o, table_s):
    heads, length, _ = table.shape
    width = qkv.shape[2]
    side = place[0]
    filler = jnp.zeros((1, width - local), F32)
    for h in range(heads):
        table_s[h] = jnp.full(table_s.shape[1:], FAR, F32)
        table_s[h, 0:length, 0:length] = table[h].astype(F32)

    def store(to, t):
        to[0:local, :] = qkv[t]
        rows = min(THIRD, PAD - t * THIRD)
        for h in range(heads):
            to[local : local + rows, h * KEYS : (h + 1) * KEYS] = table_s[
                h, t * THIRD : t * THIRD + rows, :
            ].astype(BF16)
        if rows < THIRD:
            tile = [
                jnp.concatenate([bias[...].astype(F32)[None], filler], 1)
                for bias in (query_bias, value_bias)
            ]
            tile.append(jnp.zeros((THIRD - rows - 2, width), F32))
            to[local + rows : local + THIRD, :] = jnp.concatenate(tile, 0).astype(BF16)

    for t in range(3):
        store(pack_o.at[t], t)
    store(direct_o, 0)
    direct_o[local + THIRD :, :] = out[...]
    for t in (1, 2):

        @pl.when(side == t - 1)
        def _():
            store(mine_o, t)


def attention_rows(place, qkv_rows, table, query_bias, value_bias, out):
    _, local, width = qkv_rows.shape
    block = (local + THIRD, width)
    return call(
        functools.partial(attention_rows_body, local),
        (sds((3,) + block, BF16), sds(block, BF16), sds((block[0] + local, width), BF16)),
        0,
        0,
        in_specs=[pl.BlockSpec(memory_space=pltpu.SMEM)] + [pl.BlockSpec(memory_space=pltpu.VMEM)] * 5,
        scratch_shapes=[pltpu.VMEM((table.shape[0], PAD, KEYS), F32)],
    )(place, qkv_rows, table, query_bias, value_bias, out)


def hidden_rows_body(place, up, down, bias, feed_o, mine_o, direct_o):
    count = feed_o.shape[0]
    width = up.shape[0]
    side = place[0]
    for at in range(count):
        hidden = slice(at * HID, (at + 1) * HID)
        out = feed_o.at[at]
        out[0:HID, :] = up[:, hidden].T
        out[HID : 2 * HID, :] = down[hidden, :]
        row = jnp.concatenate([bias[...].astype(F32)[None][:, hidden], jnp.zeros((1, width - HID), F32)], 1)
        out[2 * HID :, :] = jnp.concatenate([row, jnp.zeros((15, width), F32)], 0).astype(BF16)
    direct_o[...] = feed_o[0]
    mine_o[...] = feed_o[1 + side]


def hidden_rows(place, up, down, bias):
    width, hidden = up.shape
    block = (2 * HID + 16, width)
    return call(
        hidden_rows_body,
        (sds((hidden // HID,) + block, BF16), sds(block, BF16), sds(block, BF16)),
        0,
        0,
        in_specs=[pl.BlockSpec(memory_space=pltpu.SMEM)] + [pl.BlockSpec(memory_space=pltpu.VMEM)] * 3,
    )(place, up, down, bias)


def attention_forward_body(images, local, near, place, first, *refs):
    packs = refs[: 2 if near else 6]
    qkv_o, prob_o, ctx_o, w_s, bias_s = refs[len(packs) :]
    pair = 2 * local
    heads = local // HEAD_DIM
    big = images * PAD
    score_scale = HEAD_DIM ** (-0.5)
    side = place[0]
    shards = three(packs, near)
    gather_weights(w_s, shards, near, side, local)
    small = local + PAD - 2 * THIRD
    tiles = []
    for at, blocks in enumerate(shards):
        for block, spot in zip(blocks, spots_of(near, side)):
            row = spot * THIRD
            row = row if near else pl.multiple_of(row, 16)
            for h in range(heads):
                bias_s[at * heads + h, pl.ds(row, THIRD), :] = block[
                    local : local + THIRD, h * KEYS : (h + 1) * KEYS
                ].astype(F32)
        last = [block[small : small + 16, 0:local].astype(F32) for block in blocks[1:]]
        tiles.append(last[1] if near else jnp.where(side == 0, last[1], last[0]))
    shift = jnp.concatenate(tiles, 1)
    for t in range(3):
        value = mm(first[...], w_s[t * pair : (t + 1) * pair, :], NT)
        if t == 0:
            value = value + shift[0:1]
        if t == 2:
            value = value + shift[1:2]
        qkv_o[t, 0:big, :] = value.astype(BF16)
        qkv_o[t, big:, :] = jnp.zeros((KEYS - PAD, pair), BF16)
    lane = lax.broadcasted_iota(jnp.int32, (1, 128), 1)
    first_half = (lane < HEAD_DIM).astype(BF16)
    halves = (first_half, 1 - first_half)

    def image(i, carry):
        row = pl.multiple_of(i * PAD, 16)
        for tile in range(pair // 128):
            lanes = slice(128 * tile, 128 * tile + 128)
            q = qkv_o[0, pl.ds(row, PAD), lanes]
            k = qkv_o[1, pl.ds(row, KEYS), lanes]
            v = qkv_o[2, pl.ds(row, KEYS), lanes]
            context = None
            for half in range(2):
                head = 2 * tile + half
                scores = mm(q * halves[half], k, NT) * score_scale + bias_s[head, 0:PAD, :]
                top = jnp.max(scores, -1, keepdims=True)
                powers = jnp.exp(scores - top)
                share = 1.0 / jnp.sum(powers, -1, keepdims=True)
                probabilities = (powers * share).astype(BF16)
                prob_o[head, pl.ds(row, PAD), :] = probabilities
                part = mm(probabilities, v * halves[half])
                context = part if context is None else context + part
            ctx_o[pl.ds(row, PAD), lanes] = context.astype(BF16)
        return carry

    lax.fori_loop(0, images, image, 0)


def attention_forward(place, first, packs, near, images, local):
    big, width = first.shape
    pair = 2 * local
    heads = pair // HEAD_DIM
    flops = 2 * big * (width * 3 * pair + 2 * KEYS * HEAD_DIM * heads)
    return call(
        functools.partial(attention_forward_body, images, local, near),
        (
            sds((3, big + KEYS - PAD, pair), BF16),
            sds((heads, big, KEYS), BF16),
            sds((big, pair), BF16),
        ),
        flops * 2,
        0,
        in_specs=[pl.BlockSpec(memory_space=pltpu.SMEM)]
        + [pl.BlockSpec(memory_space=pltpu.VMEM)] * (1 + len(packs)),
        scratch_shapes=[pltpu.VMEM((3 * pair, width), BF16), pltpu.VMEM((heads, 3 * THIRD, KEYS), F32)],
    )(place, first, *packs)


def middle_body(images, local, ctx_a, ctx_b, p0, p1, p2, p3, started, vec, branch_o, second_o, w_s):
    pair = 2 * local
    for at, part in enumerate((p0, p1, p2, p3)):
        w_s[at * local : (at + 1) * local, :] = part[part.shape[0] - local :, :]

    def image(i, carry):
        row = pl.multiple_of(i * PAD, 16)
        block = pl.ds(row, PAD)
        branch = (
            mm(ctx_a[block, :], w_s[0:pair, :])
            + mm(ctx_b[block, :], w_s[pair : 2 * pair, :])
            + vec[OUTPUT_BIAS : OUTPUT_BIAS + 1]
        )
        branch_o[block, :] = branch
        middle = started[block, :].astype(F32) + vec[ATT_SCALE : ATT_SCALE + 1] * branch
        normed, _ = norm_parts(middle)
        second_o[block, :] = (
            normed * vec[SECOND_GAIN : SECOND_GAIN + 1] + vec[SECOND_BIAS : SECOND_BIAS + 1]
        ).astype(BF16)
        return carry

    lax.fori_loop(0, images, image, 0)


def middle_stage(ctx_a, ctx_b, packs, started, vec, images, local):
    big, width = started.shape
    return call(
        functools.partial(middle_body, images, local),
        (
            sds((big, width), F32),
            sds((big, width), BF16),
        ),
        2 * big * width * width,
        big * width * 16,
        scratch_shapes=[pltpu.VMEM((4 * local, width), BF16)],
    )(ctx_a, ctx_b, *packs, started, vec)


def feed_body(groups, near, cut, place, second, fg, *refs):
    count = sum(groups)
    weights = refs[: 1 if near else count]
    feed_o, sg_o, *refs = refs[len(weights) :]
    parts = 2 * groups[0] if cut else 0
    pieces, refs = refs[:parts], refs[parts:]
    grads, refs = refs[: len(groups) - bool(cut)], refs[len(groups) - bool(cut) :]
    biases, refs = refs[: len(groups)], refs[len(groups) :]
    wu_s, wd_s, act_s, pg_s, *whole_s = refs
    grads = [*whole_s, *grads]
    width = second.shape[1]
    side = place[0]
    blocks = [weights[0].at[at] for at in range(count)] if near else weights
    wholes = [slice(HID * at, HID * at + HID) for at in range(count)]
    for block, rows in zip(blocks, wholes):
        wu_s[rows, :] = block[0:HID, :]
        wd_s[rows, :] = block[HID : 2 * HID, :]
    sums = []
    for block, rows in zip(blocks, wholes):
        shift = block[2 * HID : 2 * HID + 16, 0:HID].astype(F32)[0:1]
        pre = mm(second[...], wu_s[rows, :], NT) + shift
        back = mm(fg[...], wd_s[rows, :], NT)
        cdf = 0.5 * (1.0 + lax.erf(pre * HALF_ROOT))
        act_s[:, rows] = (pre * cdf).astype(BF16)
        slope = cdf + pre * (jnp.exp(-0.5 * pre * pre) * DENSITY_FACTOR)
        pg = (back * slope).astype(BF16)
        pg_s[:, rows] = pg
        sums.append(colsum(pg.astype(F32)))
    for at in range(0, width, HID):
        lanes = slice(at, at + HID)
        feed_o[:, lanes] = mm(act_s[...], wd_s[:, lanes]).astype(BF16)
        sg_o[:, lanes] = mm(pg_s[...], wu_s[:, lanes]).astype(BF16)
    at = 0
    for grad, bias, group in zip(grads, biases, groups):
        for local in range(group):
            target = slice(HID * local, HID * local + HID)
            grad[side, target, :] = mm(pg_s[:, wholes[at]], second[...], TN).astype(BF16)
            grad[1 - side, target, :] = mm(act_s[:, wholes[at]], fg[...], TN).astype(BF16)
            bias[:, target] = jnp.broadcast_to(sums[at], (8, HID))
            at += 1
    for at, piece in enumerate(pieces):
        block = at % groups[0]
        piece[...] = grads[0][at // groups[0], block * HID : (block + 1) * HID, :]


def feed_stage(place, second, fg, weights, groups, near, cut=False):
    big, width = second.shape
    hidden = sum(groups) * HID
    return call(
        functools.partial(feed_body, groups, near, cut),
        (
            sds((big, width), BF16),
            sds((big, width), BF16),
            *[sds((HID, width), BF16)] * (2 * groups[0] if cut else 0),
            *[sds((2, group * HID, width), BF16) for group in groups[cut:]],
            *[sds((8, group * HID), F32) for group in groups],
        ),
        12 * big * width * hidden,
        0,
        in_specs=[pl.BlockSpec(memory_space=pltpu.SMEM)]
        + [pl.BlockSpec(memory_space=pltpu.VMEM)] * (2 + len(weights)),
        scratch_shapes=[
            pltpu.VMEM((hidden, width), BF16),
            pltpu.VMEM((hidden, width), BF16),
            pltpu.VMEM((big, hidden), BF16),
            pltpu.VMEM((big, hidden), BF16),
        ]
        + ([pltpu.VMEM((2, groups[0] * HID, width), BF16)] if cut else []),
    )(place, second, fg, *weights)


def turn_body(images, parts, *refs):
    feeds = refs[0:parts]
    sgs = refs[parts : 2 * parts]
    started, branch, g, vec, out_o, mg_o, ag_o, sums_o, wide_s = refs[2 * parts :]
    width = branch.shape[1]
    sums_o[...] = jnp.zeros(sums_o.shape, F32)

    for i in range(images):
        block = slice(i * PAD, (i + 1) * PAD)
        feed = vec[DOWN_BIAS : DOWN_BIAS + 1]
        sg = jnp.zeros((PAD, width), F32)
        for at in range(parts):
            feed = feed + feeds[at][block, :].astype(F32)
            sg = sg + sgs[at][block, :].astype(F32)
        rows = g[block, :].astype(F32)
        mid = started[block, :].astype(F32) + vec[ATT_SCALE : ATT_SCALE + 1] * branch[block, :]
        out = mid + vec[FEED_SCALE : FEED_SCALE + 1] * feed
        wide_s[i * LEN : (i + 1) * LEN, :] = out[0:LEN]
        normed, inverse = norm_parts(mid)
        grad = rows + norm_back(sg, normed, inverse, vec[SECOND_GAIN : SECOND_GAIN + 1])
        mg_o[block, :] = grad
        att = (vec[ATT_SCALE : ATT_SCALE + 1] * grad).astype(BF16)
        ag_o[block, :] = att
        sums_o[0:1, :] += colsum(rows * feed)
        sums_o[1:2, :] += colsum(sg * normed)
        sums_o[2:3, :] += colsum(sg)
        sums_o[3:4, :] += colsum(grad * branch[block, :])
        sums_o[4:5, :] += colsum(att.astype(F32))
    out_o[...] = wide_s[0 : out_o.shape[0], :].astype(BF16)


def turn_stage(feeds, sgs, started, branch, g, vec, images):
    big, width = branch.shape
    rows = images * LEN
    return call(
        functools.partial(turn_body, images, len(feeds)),
        (sds((rows, width), BF16), sds((big, width), F32), sds((big, width), BF16), sds((8, width), F32)),
        40 * big * width,
        big * width * (18 + 4 * len(feeds)),
        scratch_shapes=[pltpu.VMEM((-(-rows // 8) * 8, width), F32)],
    )(*feeds, *sgs, started, branch, g, vec)


def attention_backward_body(images, local, near, place, first, ag, ctx, qkv, prob, *refs):
    packs = refs[: 2 if near else 6]
    out_a, out_b, *refs = refs[len(packs) :]
    if near:
        (up_a, up_b), refs = [ref[0:1, :] for ref in refs[:2]], refs[2:]
    else:
        ups = []
        for shared, rest in (refs[0:2], refs[2:4]):
            shared, short, other = shared[0:1, :], rest[0:1, 0:HID], rest[0:1, HID:]
            low = jnp.where(place[0] == 0, shared, other)
            ups.append(jnp.concatenate([short, low, jnp.where(place[0] == 0, other, shared)], 1))
        (up_a, up_b), refs = ups, refs[4:]
    grad_a, *refs = refs
    parts, (fg_o, w_s, cg_s, tg_s, bias_s, wo_s, *grad_b) = (refs[:1], refs[1:]) if near else (refs[:2], refs[2:])
    grad_b = parts[0] if near else grad_b[0]
    pair = 2 * local
    heads = local // HEAD_DIM
    big, width = first.shape
    score_scale = HEAD_DIM ** (-0.5)
    side = place[0]
    sides = (side, 1 - side)
    gather_weights(w_s, three(packs, near), near, side, local)
    wo_s[0:local, :] = out_a[out_a.shape[0] - local :, :]
    wo_s[local:pair, :] = out_b[out_b.shape[0] - local :, :]
    cg_s[0:big, :] = mm(ag[...], wo_s[...], NT).astype(BF16)
    d_out = mm(ctx[...], ag[...], TN).astype(BF16)
    grad_a[sides[1], local : 2 * local, :] = d_out[0:local]
    grad_b[sides[1], local : 2 * local, :] = d_out[local:pair]
    bias_s[...] = jnp.zeros(bias_s.shape, F32)
    lane = lax.broadcasted_iota(jnp.int32, (1, 128), 1)
    first_half = (lane < HEAD_DIM).astype(BF16)
    halves = (first_half, 1 - first_half)

    def image(i, carry):
        row = pl.multiple_of(i * PAD, 16)
        for tile in range(pair // 128):
            lanes = slice(128 * tile, 128 * tile + 128)
            q = qkv[0, pl.ds(row, PAD), lanes]
            k = qkv[1, pl.ds(row, KEYS), lanes]
            v = qkv[2, pl.ds(row, KEYS), lanes]
            do = cg_s[pl.ds(row, PAD), lanes]
            dq = dk = dv = None
            for half in range(2):
                head = 2 * tile + half
                p = prob[head, pl.ds(row, PAD), :]
                do_half = do * halves[half]
                dp = mm(do_half, v, NT)
                p32 = p.astype(F32)
                ds = p32 * (dp - jnp.sum(dp * p32, -1, keepdims=True))
                bias_s[head] += ds
                ds = ds.astype(BF16)
                dv_part = mm(p, do_half, TN)
                dk_part = mm(ds, q * halves[half], TN)
                dq_part = mm(ds, k * halves[half])
                dq = dq_part if dq is None else dq + dq_part
                dk = dk_part if dk is None else dk + dk_part
                dv = dv_part if dv is None else dv + dv_part
            block = pl.ds(row, PAD)
            tg_s[block, 128 * tile : 128 * tile + 128] = (dq * score_scale).astype(BF16)
            tg_s[block, pair + 128 * tile : pair + 128 * tile + 128] = (dk[0:PAD] * score_scale).astype(BF16)
            tg_s[block, 2 * pair + 128 * tile : 2 * pair + 128 * tile + 128] = dv[0:PAD].astype(BF16)
        return carry

    lax.fori_loop(0, images, image, 0)
    small = (2 * local + CUT, 2 * local + PAD - CUT)
    filler = jnp.zeros((1, width - local), F32)
    sums = []
    for t, (half, row) in enumerate(((0, 0), (0, local), (1, 0))):
        part = tg_s[:, t * pair : (t + 1) * pair]
        dw = mm(part, first[...], TN).astype(BF16)
        grad_a[sides[half], row : row + local, :] = dw[0:local]
        grad_b[sides[half], row : row + local, :] = dw[local:pair]
        sums.append(colsum(part.astype(F32)))
    for at, (grad, hidden_bias) in enumerate(((grad_a, up_a), (grad_b, up_b))):
        lanes = slice(at * local, (at + 1) * local)
        grad[sides[0], small[0] :, :] = jnp.concatenate(
            [
                jnp.concatenate([sums[0][:, lanes], filler], 1),
                hidden_bias,
                jnp.zeros((14, width), F32),
            ],
            0,
        ).astype(BF16)
        grad[sides[1], small[1] :, :] = jnp.concatenate(
            [jnp.concatenate([sums[2][:, lanes], filler], 1), jnp.zeros((31, width), F32)], 0
        ).astype(BF16)
        for h in range(heads):
            lanes = slice(h * KEYS, (h + 1) * KEYS)
            grad[sides[0], 2 * local : 2 * local + CUT, lanes] = bias_s[at * heads + h, 0:CUT].astype(BF16)
            grad[sides[1], 2 * local : 2 * local + PAD - CUT, lanes] = bias_s[
                at * heads + h, CUT:PAD
            ].astype(BF16)
    fg_o[...] = mm(tg_s[...], w_s[...]).astype(BF16)
    if not near:
        for at, to in enumerate(parts):
            to[...] = grad_b[at]


def attention_backward(place, first, ag, forward, packs, near, outs, ups, images, local):
    qkv, prob, ctx = forward
    big, width = first.shape
    pair = 2 * local
    heads = pair // HEAD_DIM
    flops = 2 * big * (8 * width * pair + 8 * KEYS * HEAD_DIM * heads)
    half = 2 * local + CUT + 16
    pack = sds((2, half, width), BF16)
    piece = sds((half, width), BF16)
    return call(
        functools.partial(attention_backward_body, images, local, near),
        (pack,) + ((pack,) if near else (piece,) * 2) + (sds((big, width), BF16),),
        flops * 2,
        2 * big * (3 * width + 5 * pair + heads * KEYS),
        scratch_shapes=[
            pltpu.VMEM((3 * pair, width), BF16),
            pltpu.VMEM((big, pair), BF16),
            pltpu.VMEM((big, 3 * pair), BF16),
            pltpu.VMEM((heads, PAD, KEYS), F32),
            pltpu.VMEM((pair, width), BF16),
        ]
        + ([] if near else [pltpu.VMEM((2, half, width), BF16)]),
        in_specs=[pl.BlockSpec(memory_space=pltpu.SMEM)] + [pl.BlockSpec(memory_space=pltpu.VMEM)] * (7 + len(packs) + len(ups)),
    )(place, first, ag, ctx, qkv, prob, *packs, *outs, *ups)


def finish_body(images, fg_a, fg_b, mg, started, mask, vec, grad_o, sums_o, wide_s):
    width = mg.shape[1]
    rows = grad_o.shape[0]
    sums_o[...] = jnp.zeros(sums_o.shape, F32)
    for i in range(images):
        block = slice(i * PAD, (i + 1) * PAD)
        fgrad = fg_a[block, :].astype(F32) + fg_b[block, :].astype(F32)
        normed, inverse = norm_parts(started[block, :].astype(F32))
        total = mg[block, :] + norm_back(fgrad, normed, inverse, vec[FIRST_GAIN : FIRST_GAIN + 1])
        sums_o[0:1, :] += colsum(fgrad * normed)
        sums_o[1:2, :] += colsum(fgrad)
        wide_s[i * LEN : (i + 1) * LEN, :] = total[0:LEN]
    picked = mask[...] == 1.0
    for j in range(width // 128):
        lanes = slice(128 * j, 128 * j + 128)
        value = wide_s[0:rows, lanes]
        kept = jnp.where(picked, 0.0, value)
        grad_o[:, lanes] = kept
        sums_o[2:3, lanes] = colsum(value - kept)


def finish_stage(fg_a, fg_b, mg, started, mask_cols, vec, images):
    big, width = mg.shape
    rows = images * LEN
    return call(
        functools.partial(finish_body, images),
        (sds((rows, width), F32), sds((8, width), F32)),
        30 * big * width,
        big * width * 14,
        scratch_shapes=[pltpu.VMEM((-(-rows // 8) * 8, width), F32)],
    )(fg_a, fg_b, mg, started, mask_cols, vec)


def feed_final_body(place, piece, beyond, up_o, down_o):
    near = place[0] == 0
    up_o[...] = jnp.where(near, piece[...], beyond[...]).T.astype(F32)
    down_o[...] = jnp.where(near, beyond[...], piece[...]).astype(F32)


def feed_final(place, piece, beyond):
    hidden, width = piece.shape
    return call(
        feed_final_body,
        (sds((width, hidden), F32), sds((hidden, width), F32)),
        0,
        0,
        in_specs=[pl.BlockSpec(memory_space=pltpu.SMEM)] + [pl.BlockSpec(memory_space=pltpu.VMEM)] * 2,
    )(place, piece, beyond)


def attention_final_body(local, place, piece, beyond, qkv_o, out_o, table_o, query_o, value_o, hidden_o):
    near = place[0] == 0
    heads, length, _ = table_o.shape
    first = lambda rows: jnp.where(near, piece[rows, :], beyond[rows, :]).astype(F32)
    second = lambda rows: jnp.where(near, beyond[rows, :], piece[rows, :]).astype(F32)
    qkv_o[0] = first(slice(0, local))
    qkv_o[1] = first(slice(local, 2 * local))
    qkv_o[2] = second(slice(0, local))
    out_o[...] = second(slice(local, 2 * local))
    at = 2 * local
    top, low = first(slice(at, at + CUT)), second(slice(at, at + PAD - CUT))
    for h in range(heads):
        table_o[h, 0:CUT, :] = top[:, h * KEYS : h * KEYS + length]
        table_o[h, CUT:length, :] = low[0 : length - CUT, h * KEYS : h * KEYS + length]
    tile = first(slice(at + CUT, at + CUT + 16))
    query_o[...] = tile[0, 0:local]
    hidden_o[...] = tile[1, :]
    tile = second(slice(at + PAD - CUT, at + PAD - CUT + 16))
    value_o[...] = tile[0, 0:local]


def attention_final(place, piece, beyond, local, heads):
    width = piece.shape[1]
    return call(
        functools.partial(attention_final_body, local),
        (
            sds((3, local, width), F32),
            sds((local, width), F32),
            sds((heads, LEN, LEN), F32),
            sds((local,), F32),
            sds((local,), F32),
            sds((width,), F32),
        ),
        0,
        0,
        in_specs=[pl.BlockSpec(memory_space=pltpu.SMEM)] + [pl.BlockSpec(memory_space=pltpu.VMEM)] * 2,
    )(place, piece, beyond)


def flip(value, axis, size, bit):
    return lax.ppermute(value, axis, [(i, i ^ bit) for i in range(size)])


def gathered_body(count, place, *refs):
    *values, out = refs
    rows = out.shape[1]
    for at in range(count):
        block = pl.ds(pl.multiple_of(jnp.bitwise_xor(place[1], at) * rows, 16 if rows % 16 == 0 else 8), rows)
        total = None
        for value in values:
            part = (value[block, :] if len(value.shape) == 2 else value[0, block, :]).astype(F32)
            total = part if total is None else total + part
        out[at] = total.astype(BF16)


def summed_pieces(place, values, count):
    rows, width = values[-1].shape
    specs = [
        pl.BlockSpec((1, rows, width), lambda i: (0, 0, 0))
        if len(v.shape) == 3
        else pl.BlockSpec((rows, width), lambda i: (0, 0))
        for v in values
    ]
    return call(
        functools.partial(gathered_body, count),
        sds((count, rows // count, width), BF16),
        0,
        0,
        grid=(1,),
        in_specs=[pl.BlockSpec(memory_space=pltpu.SMEM)] + specs,
        out_specs=pl.BlockSpec((count, rows // count, width), lambda i: (0, 0, 0)),
    )(place, *values)


def feed_merged_body(count, place, near_a, near_b, got_x, y_shared, d_shared, y_rest, d_rest, out, sum_s):
    side = place[0]
    sum_s[...] = near_a[0].astype(F32) + near_b[0].astype(F32) + got_x[...].astype(F32)
    ours = pl.ds(pl.multiple_of((1 + side) * HID, HID), HID)
    theirs = pl.ds(pl.multiple_of((2 - side) * HID, HID), HID)
    sum_s[0:HID, :] += y_rest[0:HID, :].astype(F32) + d_rest[0:HID, :].astype(F32)
    sum_s[ours, :] += y_shared[...].astype(F32) + d_rest[HID:, :].astype(F32)
    sum_s[theirs, :] += d_shared[...].astype(F32) + y_rest[HID:, :].astype(F32)
    rows = out.shape[1]
    for at in range(count):
        block = pl.ds(pl.multiple_of(jnp.bitwise_xor(place[1], at) * rows, 8), rows)
        out[at] = sum_s[block, :].astype(BF16)


def feed_merged(place, values, count):
    rows, width = values[2].shape
    near = pl.BlockSpec((1, rows, width), lambda i: (0, 0, 0))
    flat = [pl.BlockSpec(v.shape, lambda i: (0, 0)) for v in values[2:]]
    return call(
        functools.partial(feed_merged_body, count),
        sds((count, rows // count, width), BF16),
        0,
        0,
        grid=(1,),
        in_specs=[pl.BlockSpec(memory_space=pltpu.SMEM), near, near] + flat,
        out_specs=pl.BlockSpec((count, rows // count, width), lambda i: (0, 0, 0)),
        scratch_shapes=[pltpu.VMEM((rows, width), F32)],
    )(place, *values)


def placed_body(place, *refs):
    *values, out = refs
    rows = values[0].shape[0]
    for at, value in enumerate(values):
        out[pl.ds(pl.multiple_of(jnp.bitwise_xor(place[1], at) * rows, 16 if rows % 16 == 0 else 8), rows), :] = value[...]


def placed(place, values):
    rows, width = values[0].shape
    return call(
        placed_body,
        sds((rows * len(values), width), BF16),
        rows * width,
        4 * len(values) * rows * width,
        in_specs=[pl.BlockSpec(memory_space=pltpu.SMEM)]
        + [pl.BlockSpec(memory_space=pltpu.VMEM)] * len(values),
    )(place, *values)


def added(left, right):
    return (left.astype(F32) + right.astype(F32)).astype(BF16)


def total(values):
    return sum(v.astype(F32) for v in values).astype(BF16)


def joined(parts, half):
    return jnp.concatenate(parts[2 * half : 2 * half + 2], 0)


def after(values, *earlier):
    return lax.optimization_barrier((values, earlier))[0]


def sync(*values):
    return lax.optimization_barrier(values)


def wide_groups(wide, most):
    groups = []
    bit = 2
    while bit < wide:
        size = min(most, wide // bit)
        groups.append((bit, size))
        bit *= size
    return groups


def per_device(
    wide,
    narrow,
    tokens,
    patch_mask,
    cotangent,
    mask_token,
    first_gain,
    first_bias,
    qkv_weight,
    query_bias,
    value_bias,
    position_bias,
    output_weight,
    output_bias,
    attention_scale,
    second_gain,
    second_bias,
    up_weight,
    up_bias,
    down_weight,
    down_bias,
    feedforward_scale,
):
    rows, width = tokens.shape
    images = rows // LEN
    local = qkv_weight.shape[2]
    heads = local // HEAD_DIM
    core = functools.partial(flip, axis="narrow", size=narrow, bit=1)
    across = functools.partial(flip, axis="narrow", size=narrow, bit=2)
    beside = functools.partial(flip, axis="wide", size=wide, bit=1)

    def corner(value):
        pairs = [
            (w * narrow + n, (w ^ 1) * narrow + (n ^ 2)) for w in range(wide) for n in range(narrow)
        ]
        return lax.ppermute(value, ("wide", "narrow"), pairs)

    me = lax.axis_index("wide")
    side = me & 1
    feed_groups, att_groups = [
        [
            (bit, size, jnp.stack([side, (me // bit) & (size - 1)]).astype(jnp.int32))
            for bit, size in wide_groups(wide, most)
        ]
        for most in (2, 2)
    ]
    place = feed_groups[0][2]

    count = up_weight.shape[1] // HID
    pack0, mine, direct = attention_rows(
        place, qkv_weight.transpose(1, 2, 0), position_bias, query_bias, value_bias, output_weight
    )
    pack_got2 = across(mine)
    pack_direct2 = across(direct)
    pack1 = core(pack0)
    out1 = core(output_weight)
    feed0, mine, direct = hidden_rows(place, up_weight, down_weight, up_bias)

    vectors = (
        mask_token,
        first_gain,
        first_bias,
        output_bias,
        attention_scale,
        second_gain,
        second_bias,
        down_bias,
        feedforward_scale,
    )
    mask_cols = jnp.broadcast_to(patch_mask.astype(F32)[:, None], (rows, 128))

    started, first, g, fg, sums_a, vec = prep(tokens, mask_cols, cotangent, vectors)
    first, pack_got2, pack1, mine, direct, feed0 = sync(first, pack_got2, pack1, mine, direct, feed0)
    pack_other2 = beside(pack_got2)
    pack_got3 = core(pack_got2)
    feed1 = core(feed0)
    att_a = attention_forward(place, first, (pack0, pack1), True, images, local)
    got2 = across(mine)
    att_a, pack_direct2, pack_other2, out1 = sync(att_a, pack_direct2, pack_other2, out1)
    pack_direct3 = core(pack_direct2)
    pack_other3 = core(pack_other2)
    far_packs = (pack_direct2, pack_got2, pack_other2, pack_direct3, pack_got3, pack_other3)
    att_b = attention_forward(place, first, far_packs, False, images, local)
    outs = (output_weight, out1, pack_direct2, pack_direct3)
    branch, second = middle_stage(att_a[2], att_b[2], outs, started, vec, images, local)
    second, feed1, got2 = sync(second, feed1, got2)
    direct2 = across(after(direct, got2))
    other2 = beside(got2)
    got3 = core(got2)
    second, got3 = sync(second, got3)
    feed_s, sg_s, *g3, g2, bias3s, bias2s = feed_stage(
        place, second, fg, (got3, got2), (1, 1), False, True
    )
    fg, g3 = sync(after(fg, feed_s), g3)
    from3s = [core(part) for part in g3]
    feed_1, sg_1, d1, bias1 = feed_stage(place, second, fg, (feed1,), (count,), True)
    fg, from3s = sync(after(fg, feed_1), from3s)
    far = [added(g2[at], from3s[at]) for at in range(2)]
    fg, far = sync(fg, far)
    y_shared = across(far[0])
    d_shared = corner(far[1])
    feed_0, sg_0, d0, bias0 = feed_stage(place, second, fg, (feed0,), (count,), True)
    fg, d0, d1, direct2, other2 = sync(after(fg, feed_0), d0, d1, direct2, other2)
    direct3 = core(direct2)
    other3 = core(other2)
    fg, direct3, other3 = sync(fg, direct3, other3)
    from1 = core(after(d1, direct3))
    feed_3, sg_3, *d3, bias3 = feed_stage(
        place, second, fg, (direct3, other3), (count - 1,), False, True
    )
    fg, d3 = sync(after(fg, feed_3), d3)
    from3 = [core(part) for part in d3]
    near1 = added(d0[1], after(from1, d3)[1])
    fg, near1 = sync(fg, near1)
    got_x = beside(near1)
    feed_2, sg_2, d2, bias2 = feed_stage(place, second, fg, (direct2, other2), (count - 1,), False)
    d2, y_shared, d_shared = sync(d2, y_shared, d_shared)
    d2, from3 = sync(d2, from3)
    far = [added(d2[at], joined(from3, at)) for at in range(2)]
    g, far = sync(g, far)
    y_rest = across(far[0])
    d_rest = corner(far[1])
    layer_out, mg, ag, sums_b = turn_stage(
        (feed_0, feed_1, feed_2, feed_3, feed_s),
        (sg_0, sg_1, sg_2, sg_3, sg_s),
        started,
        branch,
        g,
        vec,
        images,
    )
    back_b = attention_backward(
        place, first, ag, att_b, far_packs, False, outs[2:], (bias2s, bias2, bias3s, bias3), images, local
    )
    ag, back_b, got_x = sync(ag, back_b, got_x)
    att_from3 = [core(part) for part in back_b[1:3]]
    back_a = attention_backward(
        place, first, ag, att_a, (pack0, pack1), True, outs[:2], (bias0, bias1), images, local
    )
    grad0, fg_a = back_a[0], back_a[2]
    grad2, fg_b = back_b[0], back_b[3]

    def gradient_chain(groups, kept, coming, final, merged=summed_pieces):
        values = yield kept, coming
        for bit, size, spot in groups:
            pieces = merged(spot, values, size)
            merged = summed_pieces
            values = yield pieces[0], [flip(pieces[at], "wide", wide, bit * at) for at in range(1, size)]
        piece = total(values)
        for bit, size, spot in groups[::-1]:
            values = yield piece, [flip(piece, "wide", wide, bit * at) for at in range(1, size)]
            piece = placed(spot, values)
        piece, beyond = yield piece, [beside(piece)]
        yield final(place, piece, beyond), []

    def vector_chain(vectors):
        for axis, size in (("narrow", narrow), ("wide", wide)):
            bit = 1
            while bit < size:
                vectors, partner = yield vectors, [flip(vectors, axis, size, bit)]
                vectors = vectors + partner
                bit *= 2
        yield vectors, []

    chains = {
        "feed": gradient_chain(
            feed_groups,
            [d0, from1, got_x, y_shared, d_shared],
            [y_rest, d_rest],
            feed_final,
            feed_merged,
        ),
    }
    live = {name: next(chain) for name, chain in chains.items()}

    def advance(name):
        kept, coming = live[name]
        if not coming:
            return
        others = {other: live[other][0] for other in live if other != name}
        kept, coming, others = sync(kept, coming, others)
        for other, value in others.items():
            live[other] = (value, live[other][1])
        live[name] = chains[name].send((list(kept) if isinstance(kept, (list, tuple)) else [kept]) + list(coming))

    stages = 2 * len(feed_groups), 2 * len(att_groups)
    kept, coming = live["feed"]
    coming, fg_a = sync(coming, fg_a)
    live["feed"] = (kept, coming)
    advance("feed")
    kept, att_from3, grad1, fg_a = sync(live["feed"][0], att_from3, back_a[1], fg_a)
    att_from1 = core(grad1)
    att_far = [added(grad2[at], att_from3[at]) for at in range(2)]
    kept, att_far = sync(kept, att_far)
    live["feed"] = (kept, live["feed"][1])
    att_coming = [across(att_far[0]), corner(att_far[1])]
    att_coming.append(beside(added(grad0[1], att_from1[1])))
    chains["att"] = gradient_chain(
        att_groups,
        [grad0, att_from1],
        att_coming,
        functools.partial(attention_final, local=local, heads=heads),
    )
    live["att"] = next(chains["att"])
    advance("feed")
    kept, fg_a = sync(live["feed"][0], fg_a)
    live["feed"] = (kept, live["feed"][1])
    input_grad, sums_c = finish_stage(fg_a, fg_b, mg, started, mask_cols, vec, images)
    vectors = jnp.concatenate([sums_a[0:1], sums_b[0:5], sums_c[0:3], jnp.zeros((7, width), F32)], 0)
    chains["vectors"] = vector_chain(vectors)
    live["vectors"] = next(chains["vectors"])
    order = ["feed", "vectors", "att", "vectors", "feed", "vectors", "att", "feed", "vectors", "att"]
    order += ["vectors", "att", "feed"] * (stages[0] - 4) + ["vectors", "att"] * (stages[1] - 4)
    order += ["vectors", "att", "att"] + ["vectors"] * 8 + ["feed", "att"] * 8
    for name in order:
        advance(name)

    dup, ddown = live["feed"][0]
    dqkv, dout, dpos, dquery, dvalue, dhidden = live["att"][0]
    vectors = live["vectors"][0]
    return (
        layer_out,
        input_grad,
        vectors[8],
        vectors[6],
        vectors[7],
        dqkv.transpose(2, 0, 1),
        dquery,
        dvalue,
        dpos,
        dout,
        vectors[5],
        vectors[4],
        vectors[2],
        vectors[3],
        dup,
        dhidden,
        ddown,
        vectors[0],
        vectors[1],
    )


def solution(mesh):
    rows = P(("wide", "narrow"), None)
    in_specs = (
        rows,
        P(("wide", "narrow")),
        rows,
        P(),
        P(),
        P(),
        P(None, None, "narrow"),
        P("narrow"),
        P("narrow"),
        P("narrow", None, None),
        P("narrow", None),
        P(),
        P(),
        P(),
        P(),
        P(None, "narrow"),
        P("narrow"),
        P("narrow", None),
        P(),
        P(),
    )
    out_specs = (
        rows,
        rows,
        P(),
        P(),
        P(),
        P(None, None, "narrow"),
        P("narrow"),
        P("narrow"),
        P("narrow", None, None),
        P("narrow", None),
        P(),
        P(),
        P(),
        P(),
        P(None, "narrow"),
        P("narrow"),
        P("narrow", None),
        P(),
        P(),
    )
    body = functools.partial(per_device, mesh.shape["wide"], mesh.shape["narrow"])
    return jax.shard_map(body, mesh=mesh, in_specs=in_specs, out_specs=out_specs, check_vma=False)
```

```python
import functools

import jax
import jax.numpy as jnp
from jax import lax
from jax.experimental import pallas as pl
from jax.experimental.pallas import tpu as pltpu
from jax.sharding import PartitionSpec as P

HEAD_DIM = 64
LEN = 197
PAD = 208
KEYS = 256
EPSILON = 1e-06
HALF_ROOT = 0.7071067811865476
DENSITY_FACTOR = 0.3989422804014327
FAR = -1e30
F32 = jnp.float32
BF16 = jnp.bfloat16
MIB = 1024 * 1024

(MASK_TOKEN, FIRST_GAIN, FIRST_BIAS, OUTPUT_BIAS, ATT_SCALE, SECOND_GAIN, SECOND_BIAS, DOWN_BIAS, FEED_SCALE) = range(9)

NT = (((1,), (1,)), ((), ()))
TN = (((0,), (0,)), ((), ()))
NN = (((1,), (0,)), ((), ()))


def mm(left, right, dims=NN):
    return lax.dot_general(left, right, dims, preferred_element_type=F32)


def call(body, out_shape, flops, bytes_accessed, trans=0, vmem=12, **kw):
    return pl.pallas_call(
        body,
        out_shape=out_shape,
        compiler_params=pltpu.CompilerParams(vmem_limit_bytes=vmem * MIB),
        cost_estimate=pl.CostEstimate(
            flops=int(flops) // 64, bytes_accessed=1024, transcendentals=0
        ),
        **kw,
    )


def sds(shape, dtype):
    return jax.ShapeDtypeStruct(shape, dtype)


def norm_parts(values):
    average = jnp.mean(values, -1, keepdims=True)
    centered = values - average
    inverse_dev = lax.rsqrt(jnp.mean(centered * centered, -1, keepdims=True) + EPSILON)
    return centered * inverse_dev, inverse_dev


def norm_back(grad_rows, normed, inverse_dev, gain):
    scaled = grad_rows * gain
    return inverse_dev * (
        scaled
        - jnp.mean(scaled, -1, keepdims=True)
        - normed * jnp.mean(scaled * normed, -1, keepdims=True)
    )


def colsum(values):
    return jnp.sum(values, 0, keepdims=True)


def prep_body(images, tok, mask, cot, *refs):
    *vectors, started_o, first_o, g_o, fg_o, sums_o, vec, wide_s, pad_s = refs
    vec[...] = jnp.zeros(vec.shape, F32)
    for at, vector in enumerate(vectors):
        vec[at : at + 1, :] = vector[...].astype(F32)[None]
    width = tok.shape[1]
    rows = tok.shape[0]
    picked = mask[...] == 1.0
    for j in range(width // 128):
        lanes = slice(128 * j, 128 * j + 128)
        wide_s[0:rows, lanes] = jnp.where(
            picked, vec[MASK_TOKEN : MASK_TOKEN + 1, lanes], tok[:, lanes].astype(F32)
        )
    for i in range(images):
        pad_s[0:LEN, :] = wide_s[i * LEN : (i + 1) * LEN, :]
        pad_s[LEN:PAD, :] = jnp.zeros((PAD - LEN, width), F32)
        values = pad_s[...]
        normed, _ = norm_parts(values)
        block = slice(i * PAD, (i + 1) * PAD)
        started_o[block, :] = values.astype(BF16)
        first_o[block, :] = (
            normed * vec[FIRST_GAIN : FIRST_GAIN + 1] + vec[FIRST_BIAS : FIRST_BIAS + 1]
        ).astype(BF16)
    wide_s[0:rows, :] = cot[...].astype(F32)
    total = jnp.zeros((1, width), F32)
    for i in range(images):
        pad_s[0:LEN, :] = wide_s[i * LEN : (i + 1) * LEN, :]
        values = pad_s[...]
        block = slice(i * PAD, (i + 1) * PAD)
        g_o[block, :] = values.astype(BF16)
        feed_grad = (values * vec[FEED_SCALE : FEED_SCALE + 1]).astype(BF16)
        fg_o[block, :] = feed_grad
        total += colsum(feed_grad.astype(F32))
    sums_o[0:1, :] = total
    sums_o[1:8, :] = jnp.zeros((7, width), F32)


def prep(tokens, mask_cols, cotangent, vectors):
    rows, width = tokens.shape
    images = rows // LEN
    big = images * PAD
    b = sds((big, width), BF16)
    return call(
        functools.partial(prep_body, images),
        (b, b, b, b, sds((8, width), F32), sds((16, width), F32)),
        10 * rows * width,
        6 * 2 * rows * width,
        scratch_shapes=[pltpu.VMEM((-(-rows // 8) * 8, width), F32), pltpu.VMEM((PAD, width), F32)],
    )(tokens, mask_cols, cotangent, *vectors)


THIRD = 80
CUT = 112
HID = 256


def three(refs, near):
    if near:
        return [[ref.at[at] for at in range(3)] for ref in refs]
    return [refs[0:3], refs[3:6]]


def spots_of(near, side):
    return (0, 1, 2) if near else (0, 1 + side, 2 - side)


def gather_weights(w_s, shards, near, side, local):
    for at, blocks in enumerate(shards):
        for block, spot in zip(blocks, spots_of(near, side)):
            row = spot * 2 * local + at * local
            row = row if near else pl.multiple_of(row, 64)
            w_s[pl.ds(row, local), :] = block[0:local, :]


def attention_rows_body(local, place, qkv, table, query_bias, value_bias, out, pack_o, mine_o, direct_o, table_s):
    heads, length, _ = table.shape
    width = qkv.shape[2]
    side = place[0]
    filler = jnp.zeros((1, width - local), F32)
    for h in range(heads):
        table_s[h] = jnp.full(table_s.shape[1:], FAR, F32)
        table_s[h, 0:length, 0:length] = table[h].astype(F32)

    def store(to, t):
        to[0:local, :] = qkv[t]
        rows = min(THIRD, PAD - t * THIRD)
        for h in range(heads):
            to[local : local + rows, h * KEYS : (h + 1) * KEYS] = table_s[
                h, t * THIRD : t * THIRD + rows, :
            ].astype(BF16)
        if rows < THIRD:
            tile = [
                jnp.concatenate([bias[...].astype(F32)[None], filler], 1)
                for bias in (query_bias, value_bias)
            ]
            tile.append(jnp.zeros((THIRD - rows - 2, width), F32))
            to[local + rows : local + THIRD, :] = jnp.concatenate(tile, 0).astype(BF16)

    for t in range(3):
        store(pack_o.at[t], t)
    store(direct_o, 0)
    direct_o[local + THIRD :, :] = out[...]
    for t in (1, 2):

        @pl.when(side == t - 1)
        def _():
            store(mine_o, t)


def attention_rows(place, qkv_rows, table, query_bias, value_bias, out):
    _, local, width = qkv_rows.shape
    block = (local + THIRD, width)
    return call(
        functools.partial(attention_rows_body, local),
        (sds((3,) + block, BF16), sds(block, BF16), sds((block[0] + local, width), BF16)),
        0,
        0,
        in_specs=[pl.BlockSpec(memory_space=pltpu.SMEM)] + [pl.BlockSpec(memory_space=pltpu.VMEM)] * 5,
        scratch_shapes=[pltpu.VMEM((table.shape[0], PAD, KEYS), F32)],
    )(place, qkv_rows, table, query_bias, value_bias, out)


def hidden_rows_body(place, up, down, bias, feed_o, mine_o, direct_o):
    count = feed_o.shape[0]
    width = up.shape[0]
    side = place[0]
    for at in range(count):
        hidden = slice(at * HID, (at + 1) * HID)
        out = feed_o.at[at]
        out[0:HID, :] = up[:, hidden].T
        out[HID : 2 * HID, :] = down[hidden, :]
        row = jnp.concatenate([bias[...].astype(F32)[None][:, hidden], jnp.zeros((1, width - HID), F32)], 1)
        out[2 * HID :, :] = jnp.concatenate([row, jnp.zeros((15, width), F32)], 0).astype(BF16)
    direct_o[...] = feed_o[0]
    mine_o[...] = feed_o[1 + side]


def hidden_rows(place, up, down, bias):
    width, hidden = up.shape
    block = (2 * HID + 16, width)
    return call(
        hidden_rows_body,
        (sds((hidden // HID,) + block, BF16), sds(block, BF16), sds(block, BF16)),
        0,
        0,
        in_specs=[pl.BlockSpec(memory_space=pltpu.SMEM)] + [pl.BlockSpec(memory_space=pltpu.VMEM)] * 3,
    )(place, up, down, bias)


def attention_forward_body(images, local, near, place, first, *refs):
    packs = refs[: 2 if near else 6]
    qkv_o, prob_o, ctx_o, w_s, bias_s = refs[len(packs) :]
    pair = 2 * local
    heads = local // HEAD_DIM
    big = images * PAD
    score_scale = HEAD_DIM ** (-0.5)
    side = place[0]
    shards = three(packs, near)
    gather_weights(w_s, shards, near, side, local)
    small = local + PAD - 2 * THIRD
    tiles = []
    for at, blocks in enumerate(shards):
        for block, spot in zip(blocks, spots_of(near, side)):
            row = spot * THIRD
            row = row if near else pl.multiple_of(row, 16)
            for h in range(heads):
                bias_s[at * heads + h, pl.ds(row, THIRD), :] = block[
                    local : local + THIRD, h * KEYS : (h + 1) * KEYS
                ].astype(F32)
        last = [block[small : small + 16, 0:local].astype(F32) for block in blocks[1:]]
        tiles.append(last[1] if near else jnp.where(side == 0, last[1], last[0]))
    shift = jnp.concatenate(tiles, 1)
    for t in range(3):
        value = mm(first[...], w_s[t * pair : (t + 1) * pair, :], NT)
        if t == 0:
            value = value + shift[0:1]
        if t == 2:
            value = value + shift[1:2]
        qkv_o[t, 0:big, :] = value.astype(BF16)
        qkv_o[t, big:, :] = jnp.zeros((KEYS - PAD, pair), BF16)
    lane = lax.broadcasted_iota(jnp.int32, (1, 128), 1)
    first_half = (lane < HEAD_DIM).astype(BF16)
    halves = (first_half, 1 - first_half)

    def image(i, carry):
        row = pl.multiple_of(i * PAD, 16)
        for tile in range(pair // 128):
            lanes = slice(128 * tile, 128 * tile + 128)
            q = qkv_o[0, pl.ds(row, PAD), lanes]
            k = qkv_o[1, pl.ds(row, KEYS), lanes]
            v = qkv_o[2, pl.ds(row, KEYS), lanes]
            context = None
            for half in range(2):
                head = 2 * tile + half
                scores = mm(q * halves[half], k, NT) * score_scale + bias_s[head, 0:PAD, :]
                top = jnp.max(scores, -1, keepdims=True)
                powers = jnp.exp(scores - top)
                share = 1.0 / jnp.sum(powers, -1, keepdims=True)
                probabilities = (powers * share).astype(BF16)
                prob_o[head, pl.ds(row, PAD), :] = probabilities
                part = mm(probabilities, v * halves[half])
                context = part if context is None else context + part
            ctx_o[pl.ds(row, PAD), lanes] = context.astype(BF16)
        return carry

    lax.fori_loop(0, images, image, 0)


def attention_forward(place, first, packs, near, images, local):
    big, width = first.shape
    pair = 2 * local
    heads = pair // HEAD_DIM
    flops = 2 * big * (width * 3 * pair + 2 * KEYS * HEAD_DIM * heads)
    return call(
        functools.partial(attention_forward_body, images, local, near),
        (
            sds((3, big + KEYS - PAD, pair), BF16),
            sds((heads, big, KEYS), BF16),
            sds((big, pair), BF16),
        ),
        flops * 2,
        0,
        in_specs=[pl.BlockSpec(memory_space=pltpu.SMEM)]
        + [pl.BlockSpec(memory_space=pltpu.VMEM)] * (1 + len(packs)),
        scratch_shapes=[pltpu.VMEM((3 * pair, width), BF16), pltpu.VMEM((heads, 3 * THIRD, KEYS), F32)],
    )(place, first, *packs)


def middle_body(images, local, ctx_a, ctx_b, p0, p1, p2, p3, started, vec, branch_o, second_o, w_s):
    pair = 2 * local
    for at, part in enumerate((p0, p1, p2, p3)):
        w_s[at * local : (at + 1) * local, :] = part[part.shape[0] - local :, :]

    def image(i, carry):
        row = pl.multiple_of(i * PAD, 16)
        block = pl.ds(row, PAD)
        branch = (
            mm(ctx_a[block, :], w_s[0:pair, :])
            + mm(ctx_b[block, :], w_s[pair : 2 * pair, :])
            + vec[OUTPUT_BIAS : OUTPUT_BIAS + 1]
        )
        branch_o[block, :] = branch
        middle = started[block, :].astype(F32) + vec[ATT_SCALE : ATT_SCALE + 1] * branch
        normed, _ = norm_parts(middle)
        second_o[block, :] = (
            normed * vec[SECOND_GAIN : SECOND_GAIN + 1] + vec[SECOND_BIAS : SECOND_BIAS + 1]
        ).astype(BF16)
        return carry

    lax.fori_loop(0, images, image, 0)


def middle_stage(ctx_a, ctx_b, packs, started, vec, images, local):
    big, width = started.shape
    return call(
        functools.partial(middle_body, images, local),
        (
            sds((big, width), F32),
            sds((big, width), BF16),
        ),
        2 * big * width * width,
        big * width * 16,
        scratch_shapes=[pltpu.VMEM((4 * local, width), BF16)],
    )(ctx_a, ctx_b, *packs, started, vec)


def feed_body(groups, near, cut, place, second, fg, *refs):
    count = sum(groups)
    weights = refs[: 1 if near else count]
    feed_o, sg_o, *refs = refs[len(weights) :]
    parts = 2 * groups[0] if cut else 0
    pieces, refs = refs[:parts], refs[parts:]
    grads, refs = refs[: len(groups) - bool(cut)], refs[len(groups) - bool(cut) :]
    biases, refs = refs[: len(groups)], refs[len(groups) :]
    wu_s, wd_s, act_s, pg_s, *whole_s = refs
    grads = [*whole_s, *grads]
    width = second.shape[1]
    side = place[0]
    blocks = [weights[0].at[at] for at in range(count)] if near else weights
    wholes = [slice(HID * at, HID * at + HID) for at in range(count)]
    for block, rows in zip(blocks, wholes):
        wu_s[rows, :] = block[0:HID, :]
        wd_s[rows, :] = block[HID : 2 * HID, :]
    sums = []
    for block, rows in zip(blocks, wholes):
        shift = block[2 * HID : 2 * HID + 16, 0:HID].astype(F32)[0:1]
        pre = mm(second[...], wu_s[rows, :], NT) + shift
        back = mm(fg[...], wd_s[rows, :], NT)
        cdf = 0.5 * (1.0 + lax.erf(pre * HALF_ROOT))
        act_s[:, rows] = (pre * cdf).astype(BF16)
        slope = cdf + pre * (jnp.exp(-0.5 * pre * pre) * DENSITY_FACTOR)
        pg = (back * slope).astype(BF16)
        pg_s[:, rows] = pg
        sums.append(colsum(pg.astype(F32)))
    for at in range(0, width, HID):
        lanes = slice(at, at + HID)
        feed_o[:, lanes] = mm(act_s[...], wd_s[:, lanes]).astype(BF16)
        sg_o[:, lanes] = mm(pg_s[...], wu_s[:, lanes]).astype(BF16)
    at = 0
    for grad, bias, group in zip(grads, biases, groups):
        for local in range(group):
            target = slice(HID * local, HID * local + HID)
            grad[side, target, :] = mm(pg_s[:, wholes[at]], second[...], TN).astype(BF16)
            grad[1 - side, target, :] = mm(act_s[:, wholes[at]], fg[...], TN).astype(BF16)
            bias[:, target] = jnp.broadcast_to(sums[at], (8, HID))
            at += 1
    for at, piece in enumerate(pieces):
        block = at % groups[0]
        piece[...] = grads[0][at // groups[0], block * HID : (block + 1) * HID, :]


def feed_stage(place, second, fg, weights, groups, near, cut=False):
    big, width = second.shape
    hidden = sum(groups) * HID
    return call(
        functools.partial(feed_body, groups, near, cut),
        (
            sds((big, width), BF16),
            sds((big, width), BF16),
            *[sds((HID, width), BF16)] * (2 * groups[0] if cut else 0),
            *[sds((2, group * HID, width), BF16) for group in groups[cut:]],
            *[sds((8, group * HID), F32) for group in groups],
        ),
        12 * big * width * hidden,
        0,
        in_specs=[pl.BlockSpec(memory_space=pltpu.SMEM)]
        + [pl.BlockSpec(memory_space=pltpu.VMEM)] * (2 + len(weights)),
        scratch_shapes=[
            pltpu.VMEM((hidden, width), BF16),
            pltpu.VMEM((hidden, width), BF16),
            pltpu.VMEM((big, hidden), BF16),
            pltpu.VMEM((big, hidden), BF16),
        ]
        + ([pltpu.VMEM((2, groups[0] * HID, width), BF16)] if cut else []),
    )(place, second, fg, *weights)


def turn_body(images, parts, *refs):
    feeds = refs[0:parts]
    sgs = refs[parts : 2 * parts]
    started, branch, g, vec, out_o, mg_o, ag_o, sums_o, wide_s = refs[2 * parts :]
    width = branch.shape[1]
    sums_o[...] = jnp.zeros(sums_o.shape, F32)

    for i in range(images):
        block = slice(i * PAD, (i + 1) * PAD)
        feed = vec[DOWN_BIAS : DOWN_BIAS + 1]
        sg = jnp.zeros((PAD, width), F32)
        for at in range(parts):
            feed = feed + feeds[at][block, :].astype(F32)
            sg = sg + sgs[at][block, :].astype(F32)
        rows = g[block, :].astype(F32)
        mid = started[block, :].astype(F32) + vec[ATT_SCALE : ATT_SCALE + 1] * branch[block, :]
        out = mid + vec[FEED_SCALE : FEED_SCALE + 1] * feed
        wide_s[i * LEN : (i + 1) * LEN, :] = out[0:LEN]
        normed, inverse = norm_parts(mid)
        grad = rows + norm_back(sg, normed, inverse, vec[SECOND_GAIN : SECOND_GAIN + 1])
        mg_o[block, :] = grad
        att = (vec[ATT_SCALE : ATT_SCALE + 1] * grad).astype(BF16)
        ag_o[block, :] = att
        sums_o[0:1, :] += colsum(rows * feed)
        sums_o[1:2, :] += colsum(sg * normed)
        sums_o[2:3, :] += colsum(sg)
        sums_o[3:4, :] += colsum(grad * branch[block, :])
        sums_o[4:5, :] += colsum(att.astype(F32))
    out_o[...] = wide_s[0 : out_o.shape[0], :].astype(BF16)


def turn_stage(feeds, sgs, started, branch, g, vec, images):
    big, width = branch.shape
    rows = images * LEN
    return call(
        functools.partial(turn_body, images, len(feeds)),
        (sds((rows, width), BF16), sds((big, width), F32), sds((big, width), BF16), sds((8, width), F32)),
        40 * big * width,
        big * width * (18 + 4 * len(feeds)),
        scratch_shapes=[pltpu.VMEM((-(-rows // 8) * 8, width), F32)],
    )(*feeds, *sgs, started, branch, g, vec)


def attention_backward_body(images, local, near, place, first, ag, ctx, qkv, prob, *refs):
    packs = refs[: 2 if near else 6]
    out_a, out_b, *refs = refs[len(packs) :]
    if near:
        (up_a, up_b), refs = [ref[0:1, :] for ref in refs[:2]], refs[2:]
    else:
        ups = []
        for shared, rest in (refs[0:2], refs[2:4]):
            shared, short, other = shared[0:1, :], rest[0:1, 0:HID], rest[0:1, HID:]
            low = jnp.where(place[0] == 0, shared, other)
            ups.append(jnp.concatenate([short, low, jnp.where(place[0] == 0, other, shared)], 1))
        (up_a, up_b), refs = ups, refs[4:]
    grad_a, *refs = refs
    parts, (fg_o, w_s, cg_s, tg_s, bias_s, wo_s, *grad_b) = (refs[:1], refs[1:]) if near else (refs[:2], refs[2:])
    grad_b = parts[0] if near else grad_b[0]
    pair = 2 * local
    heads = local // HEAD_DIM
    big, width = first.shape
    score_scale = HEAD_DIM ** (-0.5)
    side = place[0]
    sides = (side, 1 - side)
    gather_weights(w_s, three(packs, near), near, side, local)
    wo_s[0:local, :] = out_a[out_a.shape[0] - local :, :]
    wo_s[local:pair, :] = out_b[out_b.shape[0] - local :, :]
    cg_s[0:big, :] = mm(ag[...], wo_s[...], NT).astype(BF16)
    d_out = mm(ctx[...], ag[...], TN).astype(BF16)
    grad_a[sides[1], local : 2 * local, :] = d_out[0:local]
    grad_b[sides[1], local : 2 * local, :] = d_out[local:pair]
    bias_s[...] = jnp.zeros(bias_s.shape, F32)
    lane = lax.broadcasted_iota(jnp.int32, (1, 128), 1)
    first_half = (lane < HEAD_DIM).astype(BF16)
    halves = (first_half, 1 - first_half)

    def image(i, carry):
        row = pl.multiple_of(i * PAD, 16)
        for tile in range(pair // 128):
            lanes = slice(128 * tile, 128 * tile + 128)
            q = qkv[0, pl.ds(row, PAD), lanes]
            k = qkv[1, pl.ds(row, KEYS), lanes]
            v = qkv[2, pl.ds(row, KEYS), lanes]
            do = cg_s[pl.ds(row, PAD), lanes]
            dq = dk = dv = None
            for half in range(2):
                head = 2 * tile + half
                p = prob[head, pl.ds(row, PAD), :]
                do_half = do * halves[half]
                dp = mm(do_half, v, NT)
                p32 = p.astype(F32)
                ds = p32 * (dp - jnp.sum(dp * p32, -1, keepdims=True))
                bias_s[head] += ds
                ds = ds.astype(BF16)
                dv_part = mm(p, do_half, TN)
                dk_part = mm(ds, q * halves[half], TN)
                dq_part = mm(ds, k * halves[half])
                dq = dq_part if dq is None else dq + dq_part
                dk = dk_part if dk is None else dk + dk_part
                dv = dv_part if dv is None else dv + dv_part
            block = pl.ds(row, PAD)
            tg_s[block, 128 * tile : 128 * tile + 128] = (dq * score_scale).astype(BF16)
            tg_s[block, pair + 128 * tile : pair + 128 * tile + 128] = (dk[0:PAD] * score_scale).astype(BF16)
            tg_s[block, 2 * pair + 128 * tile : 2 * pair + 128 * tile + 128] = dv[0:PAD].astype(BF16)
        return carry

    lax.fori_loop(0, images, image, 0)
    small = (2 * local + CUT, 2 * local + PAD - CUT)
    filler = jnp.zeros((1, width - local), F32)
    sums = []
    for t, (half, row) in enumerate(((0, 0), (0, local), (1, 0))):
        part = tg_s[:, t * pair : (t + 1) * pair]
        dw = mm(part, first[...], TN).astype(BF16)
        grad_a[sides[half], row : row + local, :] = dw[0:local]
        grad_b[sides[half], row : row + local, :] = dw[local:pair]
        sums.append(colsum(part.astype(F32)))
    for at, (grad, hidden_bias) in enumerate(((grad_a, up_a), (grad_b, up_b))):
        lanes = slice(at * local, (at + 1) * local)
        grad[sides[0], small[0] :, :] = jnp.concatenate(
            [
                jnp.concatenate([sums[0][:, lanes], filler], 1),
                hidden_bias,
                jnp.zeros((14, width), F32),
            ],
            0,
        ).astype(BF16)
        grad[sides[1], small[1] :, :] = jnp.concatenate(
            [jnp.concatenate([sums[2][:, lanes], filler], 1), jnp.zeros((31, width), F32)], 0
        ).astype(BF16)
        for h in range(heads):
            lanes = slice(h * KEYS, (h + 1) * KEYS)
            grad[sides[0], 2 * local : 2 * local + CUT, lanes] = bias_s[at * heads + h, 0:CUT].astype(BF16)
            grad[sides[1], 2 * local : 2 * local + PAD - CUT, lanes] = bias_s[
                at * heads + h, CUT:PAD
            ].astype(BF16)
    fg_o[...] = mm(tg_s[...], w_s[...]).astype(BF16)
    if not near:
        for at, to in enumerate(parts):
            to[...] = grad_b[at]


def attention_backward(place, first, ag, forward, packs, near, outs, ups, images, local):
    qkv, prob, ctx = forward
    big, width = first.shape
    pair = 2 * local
    heads = pair // HEAD_DIM
    flops = 2 * big * (8 * width * pair + 8 * KEYS * HEAD_DIM * heads)
    half = 2 * local + CUT + 16
    pack = sds((2, half, width), BF16)
    piece = sds((half, width), BF16)
    return call(
        functools.partial(attention_backward_body, images, local, near),
        (pack,) + ((pack,) if near else (piece,) * 2) + (sds((big, width), BF16),),
        flops * 2,
        2 * big * (3 * width + 5 * pair + heads * KEYS),
        scratch_shapes=[
            pltpu.VMEM((3 * pair, width), BF16),
            pltpu.VMEM((big, pair), BF16),
            pltpu.VMEM((big, 3 * pair), BF16),
            pltpu.VMEM((heads, PAD, KEYS), F32),
            pltpu.VMEM((pair, width), BF16),
        ]
        + ([] if near else [pltpu.VMEM((2, half, width), BF16)]),
        in_specs=[pl.BlockSpec(memory_space=pltpu.SMEM)] + [pl.BlockSpec(memory_space=pltpu.VMEM)] * (7 + len(packs) + len(ups)),
    )(place, first, ag, ctx, qkv, prob, *packs, *outs, *ups)


def finish_body(images, fg_a, fg_b, mg, started, mask, vec, grad_o, sums_o, wide_s):
    width = mg.shape[1]
    rows = grad_o.shape[0]
    sums_o[...] = jnp.zeros(sums_o.shape, F32)
    for i in range(images):
        block = slice(i * PAD, (i + 1) * PAD)
        fgrad = fg_a[block, :].astype(F32) + fg_b[block, :].astype(F32)
        normed, inverse = norm_parts(started[block, :].astype(F32))
        total = mg[block, :] + norm_back(fgrad, normed, inverse, vec[FIRST_GAIN : FIRST_GAIN + 1])
        sums_o[0:1, :] += colsum(fgrad * normed)
        sums_o[1:2, :] += colsum(fgrad)
        wide_s[i * LEN : (i + 1) * LEN, :] = total[0:LEN]
    picked = mask[...] == 1.0
    for j in range(width // 128):
        lanes = slice(128 * j, 128 * j + 128)
        value = wide_s[0:rows, lanes]
        kept = jnp.where(picked, 0.0, value)
        grad_o[:, lanes] = kept
        sums_o[2:3, lanes] = colsum(value - kept)


def finish_stage(fg_a, fg_b, mg, started, mask_cols, vec, images):
    big, width = mg.shape
    rows = images * LEN
    return call(
        functools.partial(finish_body, images),
        (sds((rows, width), F32), sds((8, width), F32)),
        30 * big * width,
        big * width * 14,
        scratch_shapes=[pltpu.VMEM((-(-rows // 8) * 8, width), F32)],
    )(fg_a, fg_b, mg, started, mask_cols, vec)


def feed_final_body(place, piece, beyond, up_o, down_o):
    near = place[0] == 0
    up_o[...] = jnp.where(near, piece[...], beyond[...]).T.astype(F32)
    down_o[...] = jnp.where(near, beyond[...], piece[...]).astype(F32)


def feed_final(place, piece, beyond):
    hidden, width = piece.shape
    return call(
        feed_final_body,
        (sds((width, hidden), F32), sds((hidden, width), F32)),
        0,
        0,
        in_specs=[pl.BlockSpec(memory_space=pltpu.SMEM)] + [pl.BlockSpec(memory_space=pltpu.VMEM)] * 2,
    )(place, piece, beyond)


def attention_final_body(local, place, piece, beyond, qkv_o, out_o, table_o, query_o, value_o, hidden_o):
    near = place[0] == 0
    heads, length, _ = table_o.shape
    first = lambda rows: jnp.where(near, piece[rows, :], beyond[rows, :]).astype(F32)
    second = lambda rows: jnp.where(near, beyond[rows, :], piece[rows, :]).astype(F32)
    qkv_o[0] = first(slice(0, local))
    qkv_o[1] = first(slice(local, 2 * local))
    qkv_o[2] = second(slice(0, local))
    out_o[...] = second(slice(local, 2 * local))
    at = 2 * local
    top, low = first(slice(at, at + CUT)), second(slice(at, at + PAD - CUT))
    for h in range(heads):
        table_o[h, 0:CUT, :] = top[:, h * KEYS : h * KEYS + length]
        table_o[h, CUT:length, :] = low[0 : length - CUT, h * KEYS : h * KEYS + length]
    tile = first(slice(at + CUT, at + CUT + 16))
    query_o[...] = tile[0, 0:local]
    hidden_o[...] = tile[1, :]
    tile = second(slice(at + PAD - CUT, at + PAD - CUT + 16))
    value_o[...] = tile[0, 0:local]


def attention_final(place, piece, beyond, local, heads):
    width = piece.shape[1]
    return call(
        functools.partial(attention_final_body, local),
        (
            sds((3, local, width), F32),
            sds((local, width), F32),
            sds((heads, LEN, LEN), F32),
            sds((local,), F32),
            sds((local,), F32),
            sds((width,), F32),
        ),
        0,
        0,
        in_specs=[pl.BlockSpec(memory_space=pltpu.SMEM)] + [pl.BlockSpec(memory_space=pltpu.VMEM)] * 2,
    )(place, piece, beyond)


def flip(value, axis, size, bit):
    return lax.ppermute(value, axis, [(i, i ^ bit) for i in range(size)])


def gathered_body(count, place, *refs):
    *values, out = refs
    rows = out.shape[1]
    for at in range(count):
        block = pl.ds(pl.multiple_of(jnp.bitwise_xor(place[1], at) * rows, 16 if rows % 16 == 0 else 8), rows)
        total = None
        for value in values:
            part = (value[block, :] if len(value.shape) == 2 else value[0, block, :]).astype(F32)
            total = part if total is None else total + part
        out[at] = total.astype(BF16)


def summed_pieces(place, values, count):
    rows, width = values[-1].shape
    specs = [
        pl.BlockSpec((1, rows, width), lambda i: (0, 0, 0))
        if len(v.shape) == 3
        else pl.BlockSpec((rows, width), lambda i: (0, 0))
        for v in values
    ]
    return call(
        functools.partial(gathered_body, count),
        sds((count, rows // count, width), BF16),
        0,
        0,
        grid=(1,),
        in_specs=[pl.BlockSpec(memory_space=pltpu.SMEM)] + specs,
        out_specs=pl.BlockSpec((count, rows // count, width), lambda i: (0, 0, 0)),
    )(place, *values)


def feed_merged_body(count, place, near_a, near_b, got_x, y_shared, d_shared, y_rest, d_rest, out, sum_s):
    side = place[0]
    sum_s[...] = near_a[0].astype(F32) + near_b[0].astype(F32) + got_x[...].astype(F32)
    ours = pl.ds(pl.multiple_of((1 + side) * HID, HID), HID)
    theirs = pl.ds(pl.multiple_of((2 - side) * HID, HID), HID)
    sum_s[0:HID, :] += y_rest[0:HID, :].astype(F32) + d_rest[0:HID, :].astype(F32)
    sum_s[ours, :] += y_shared[...].astype(F32) + d_rest[HID:, :].astype(F32)
    sum_s[theirs, :] += d_shared[...].astype(F32) + y_rest[HID:, :].astype(F32)
    rows = out.shape[1]
    for at in range(count):
        block = pl.ds(pl.multiple_of(jnp.bitwise_xor(place[1], at) * rows, 8), rows)
        out[at] = sum_s[block, :].astype(BF16)


def feed_merged(place, values, count):
    rows, width = values[2].shape
    near = pl.BlockSpec((1, rows, width), lambda i: (0, 0, 0))
    flat = [pl.BlockSpec(v.shape, lambda i: (0, 0)) for v in values[2:]]
    return call(
        functools.partial(feed_merged_body, count),
        sds((count, rows // count, width), BF16),
        0,
        0,
        grid=(1,),
        in_specs=[pl.BlockSpec(memory_space=pltpu.SMEM), near, near] + flat,
        out_specs=pl.BlockSpec((count, rows // count, width), lambda i: (0, 0, 0)),
        scratch_shapes=[pltpu.VMEM((rows, width), F32)],
    )(place, *values)


def placed_body(place, *refs):
    *values, out = refs
    rows = values[0].shape[0]
    for at, value in enumerate(values):
        out[pl.ds(pl.multiple_of(jnp.bitwise_xor(place[1], at) * rows, 16 if rows % 16 == 0 else 8), rows), :] = value[...]


def placed(place, values):
    rows, width = values[0].shape
    return call(
        placed_body,
        sds((rows * len(values), width), BF16),
        rows * width,
        4 * len(values) * rows * width,
        in_specs=[pl.BlockSpec(memory_space=pltpu.SMEM)]
        + [pl.BlockSpec(memory_space=pltpu.VMEM)] * len(values),
    )(place, *values)


def added(left, right):
    return (left.astype(F32) + right.astype(F32)).astype(BF16)


def total(values):
    return sum(v.astype(F32) for v in values).astype(BF16)


def joined(parts, half):
    return jnp.concatenate(parts[2 * half : 2 * half + 2], 0)


def after(values, *earlier):
    return lax.optimization_barrier((values, earlier))[0]


def sync(*values):
    return lax.optimization_barrier(values)


def wide_groups(wide, most):
    groups = []
    bit = 2
    while bit < wide:
        size = min(most, wide // bit)
        groups.append((bit, size))
        bit *= size
    return groups


def per_device(
    wide,
    narrow,
    tokens,
    patch_mask,
    cotangent,
    mask_token,
    first_gain,
    first_bias,
    qkv_weight,
    query_bias,
    value_bias,
    position_bias,
    output_weight,
    output_bias,
    attention_scale,
    second_gain,
    second_bias,
    up_weight,
    up_bias,
    down_weight,
    down_bias,
    feedforward_scale,
):
    rows, width = tokens.shape
    images = rows // LEN
    local = qkv_weight.shape[2]
    heads = local // HEAD_DIM
    core = functools.partial(flip, axis="narrow", size=narrow, bit=1)
    across = functools.partial(flip, axis="narrow", size=narrow, bit=2)
    beside = functools.partial(flip, axis="wide", size=wide, bit=1)

    def corner(value):
        pairs = [
            (w * narrow + n, (w ^ 1) * narrow + (n ^ 2)) for w in range(wide) for n in range(narrow)
        ]
        return lax.ppermute(value, ("wide", "narrow"), pairs)

    me = lax.axis_index("wide")
    side = me & 1
    feed_groups, att_groups = [
        [
            (bit, size, jnp.stack([side, (me // bit) & (size - 1)]).astype(jnp.int32))
            for bit, size in wide_groups(wide, most)
        ]
        for most in (2, 2)
    ]
    place = feed_groups[0][2]

    count = up_weight.shape[1] // HID
    pack0, mine, direct = attention_rows(
        place, qkv_weight.transpose(1, 2, 0), position_bias, query_bias, value_bias, output_weight
    )
    pack_got2 = across(mine)
    pack_direct2 = across(direct)
    pack1 = core(pack0)
    out1 = core(output_weight)
    feed0, mine, direct = hidden_rows(place, up_weight, down_weight, up_bias)

    vectors = (
        mask_token,
        first_gain,
        first_bias,
        output_bias,
        attention_scale,
        second_gain,
        second_bias,
        down_bias,
        feedforward_scale,
    )
    mask_cols = jnp.broadcast_to(patch_mask.astype(F32)[:, None], (rows, 128))

    started, first, g, fg, sums_a, vec = prep(tokens, mask_cols, cotangent, vectors)
    first, pack_got2, pack1, mine, direct, feed0 = sync(first, pack_got2, pack1, mine, direct, feed0)
    pack_other2 = beside(pack_got2)
    pack_got3 = core(pack_got2)
    feed1 = core(feed0)
    att_a = attention_forward(place, first, (pack0, pack1), True, images, local)
    got2 = across(mine)
    att_a, pack_direct2, pack_other2, out1 = sync(att_a, pack_direct2, pack_other2, out1)
    pack_direct3 = core(pack_direct2)
    pack_other3 = core(pack_other2)
    far_packs = (pack_direct2, pack_got2, pack_other2, pack_direct3, pack_got3, pack_other3)
    att_b = attention_forward(place, first, far_packs, False, images, local)
    outs = (output_weight, out1, pack_direct2, pack_direct3)
    branch, second = middle_stage(att_a[2], att_b[2], outs, started, vec, images, local)
    second, feed1, got2 = sync(second, feed1, got2)
    direct2 = across(after(direct, got2))
    other2 = beside(got2)
    got3 = core(got2)
    second, got3 = sync(second, got3)
    feed_s, sg_s, *g3, g2, bias3s, bias2s = feed_stage(
        place, second, fg, (got3, got2), (1, 1), False, True
    )
    fg, g3 = sync(after(fg, feed_s), g3)
    from3s = [core(part) for part in g3]
    feed_1, sg_1, d1, bias1 = feed_stage(place, second, fg, (feed1,), (count,), True)
    fg, from3s = sync(after(fg, feed_1), from3s)
    far = [added(g2[at], from3s[at]) for at in range(2)]
    fg, far = sync(fg, far)
    y_shared = across(far[0])
    d_shared = corner(far[1])
    feed_0, sg_0, d0, bias0 = feed_stage(place, second, fg, (feed0,), (count,), True)
    fg, d0, d1, direct2, other2 = sync(after(fg, feed_0), d0, d1, direct2, other2)
    direct3 = core(direct2)
    other3 = core(other2)
    fg, direct3, other3 = sync(fg, direct3, other3)
    from1 = core(after(d1, direct3))
    feed_3, sg_3, *d3, bias3 = feed_stage(
        place, second, fg, (direct3, other3), (count - 1,), False, True
    )
    fg, d3 = sync(after(fg, feed_3), d3)
    from3 = [core(part) for part in d3]
    near1 = added(d0[1], after(from1, d3)[1])
    fg, near1 = sync(fg, near1)
    got_x = beside(near1)
    feed_2, sg_2, d2, bias2 = feed_stage(place, second, fg, (direct2, other2), (count - 1,), False)
    d2, y_shared, d_shared = sync(d2, y_shared, d_shared)
    d2, from3 = sync(d2, from3)
    far = [added(d2[at], joined(from3, at)) for at in range(2)]
    g, far = sync(g, far)
    y_rest = across(far[0])
    d_rest = corner(far[1])
    layer_out, mg, ag, sums_b = turn_stage(
        (feed_0, feed_1, feed_2, feed_3, feed_s),
        (sg_0, sg_1, sg_2, sg_3, sg_s),
        started,
        branch,
        g,
        vec,
        images,
    )
    back_b = attention_backward(
        place, first, ag, att_b, far_packs, False, outs[2:], (bias2s, bias2, bias3s, bias3), images, local
    )
    ag, back_b, got_x = sync(ag, back_b, got_x)
    att_from3 = [core(part) for part in back_b[1:3]]
    back_a = attention_backward(
        place, first, ag, att_a, (pack0, pack1), True, outs[:2], (bias0, bias1), images, local
    )
    grad0, fg_a = back_a[0], back_a[2]
    grad2, fg_b = back_b[0], back_b[3]

    def gradient_chain(groups, kept, coming, final, merged=summed_pieces):
        values = yield kept, coming
        for bit, size, spot in groups:
            pieces = merged(spot, values, size)
            merged = summed_pieces
            values = yield pieces[0], [flip(pieces[at], "wide", wide, bit * at) for at in range(1, size)]
        piece = total(values)
        for bit, size, spot in groups[::-1]:
            values = yield piece, [flip(piece, "wide", wide, bit * at) for at in range(1, size)]
            piece = placed(spot, values)
        piece, beyond = yield piece, [beside(piece)]
        yield final(place, piece, beyond), []

    def vector_chain(vectors):
        for axis, size in (("narrow", narrow), ("wide", wide)):
            bit = 1
            while bit < size:
                vectors, partner = yield vectors, [flip(vectors, axis, size, bit)]
                vectors = vectors + partner
                bit *= 2
        yield vectors, []

    chains = {
        "feed": gradient_chain(
            feed_groups,
            [d0, from1, got_x, y_shared, d_shared],
            [y_rest, d_rest],
            feed_final,
            feed_merged,
        ),
    }
    live = {name: next(chain) for name, chain in chains.items()}

    def advance(name):
        kept, coming = live[name]
        if not coming:
            return
        others = {other: live[other][0] for other in live if other != name}
        kept, coming, others = sync(kept, coming, others)
        for other, value in others.items():
            live[other] = (value, live[other][1])
        live[name] = chains[name].send((list(kept) if isinstance(kept, (list, tuple)) else [kept]) + list(coming))

    stages = 2 * len(feed_groups), 2 * len(att_groups)
    kept, coming = live["feed"]
    coming, fg_a = sync(coming, fg_a)
    live["feed"] = (kept, coming)
    advance("feed")
    kept, att_from3, grad1, fg_a = sync(live["feed"][0], att_from3, back_a[1], fg_a)
    att_from1 = core(grad1)
    att_far = [added(grad2[at], att_from3[at]) for at in range(2)]
    kept, att_far = sync(kept, att_far)
    live["feed"] = (kept, live["feed"][1])
    att_coming = [across(att_far[0]), corner(att_far[1])]
    att_coming.append(beside(added(grad0[1], att_from1[1])))
    chains["att"] = gradient_chain(
        att_groups,
        [grad0, att_from1],
        att_coming,
        functools.partial(attention_final, local=local, heads=heads),
    )
    live["att"] = next(chains["att"])
    advance("feed")
    kept, fg_a = sync(live["feed"][0], fg_a)
    live["feed"] = (kept, live["feed"][1])
    input_grad, sums_c = finish_stage(fg_a, fg_b, mg, started, mask_cols, vec, images)
    vectors = jnp.concatenate([sums_a[0:1], sums_b[0:5], sums_c[0:3], jnp.zeros((7, width), F32)], 0)
    chains["vectors"] = vector_chain(vectors)
    live["vectors"] = next(chains["vectors"])
    order = ["feed", "vectors", "att", "vectors", "feed", "vectors", "att", "feed", "vectors", "att"]
    order += ["vectors", "att", "feed"] * (stages[0] - 4) + ["vectors", "att"] * (stages[1] - 4)
    order += ["att", "vectors", "att"] + ["vectors"] * 8 + ["feed", "att"] * 8
    for name in order:
        advance(name)

    dup, ddown = live["feed"][0]
    dqkv, dout, dpos, dquery, dvalue, dhidden = live["att"][0]
    vectors = live["vectors"][0]
    return (
        layer_out,
        input_grad,
        vectors[8],
        vectors[6],
        vectors[7],
        dqkv.transpose(2, 0, 1),
        dquery,
        dvalue,
        dpos,
        dout,
        vectors[5],
        vectors[4],
        vectors[2],
        vectors[3],
        dup,
        dhidden,
        ddown,
        vectors[0],
        vectors[1],
    )


def solution(mesh):
    rows = P(("wide", "narrow"), None)
    in_specs = (
        rows,
        P(("wide", "narrow")),
        rows,
        P(),
        P(),
        P(),
        P(None, None, "narrow"),
        P("narrow"),
        P("narrow"),
        P("narrow", None, None),
        P("narrow", None),
        P(),
        P(),
        P(),
        P(),
        P(None, "narrow"),
        P("narrow"),
        P("narrow", None),
        P(),
        P(),
    )
    out_specs = (
        rows,
        rows,
        P(),
        P(),
        P(),
        P(None, None, "narrow"),
        P("narrow"),
        P("narrow"),
        P("narrow", None, None),
        P("narrow", None),
        P(),
        P(),
        P(),
        P(),
        P(None, "narrow"),
        P("narrow"),
        P("narrow", None),
        P(),
        P(),
    )
    body = functools.partial(per_device, mesh.shape["wide"], mesh.shape["narrow"])
    return jax.shard_map(body, mesh=mesh, in_specs=in_specs, out_specs=out_specs, check_vma=False)
```
